32 devices in a mesh: expert: 8 (over y, x, core), tensor: 4 (over z).
Axes of the slice: x: 2, y: 2, z: 4, core: 2. Of those that a mesh axis runs over, the one named last changes fastest.
Arguments:
- tokens: bfloat16 [2048, 7168], P(('expert', 'tensor')), may hold values from -6 to 6
- expert_ids: int32 [2048, 2], P('expert'), may hold values from 0 to 2, all different within a row
- gate_scores: int32 [2048, 2], P('expert'), may hold values from 1 to 64
- gate_weight: bfloat16 [3, 7168, 2048], P(None, ('expert', 'tensor')), may hold values from -0.0625 to 0.0625
- up_weight: bfloat16 [3, 7168, 2048], P(None, ('expert', 'tensor')), may hold values from -0.0625 to 0.0625
- down_weight: bfloat16 [3, 7168, 2048], P(None, ('expert', 'tensor')), may hold values from -0.1875 to 0.1875
Outputs:
- mixed: bfloat16 [2048, 7168], P(('expert', 'tensor'))
The draws below stay inside these ranges and needn't reach their ends.
Inputs may be any that keep to these rules, and one draw needn't show every extreme that they name: `expert_ids`: each row names 2 different experts.
All inputs are finite; a program needn't handle non-finite values.
Results may differ from the reference program's by a relative error of at most 0.015.
Values may be sent and summed in bfloat16 or wider, within the bound.
No kernel may reach another device: no remote copies, remote signals or barrier semaphores. Data moves between devices by JAX's collectives and lax.ppermute only.
A program may use at most 128 MiB of HBM per device.

```python
import jax
import jax.numpy as jnp
from jax import lax

D = 7168
FF = 2048
EXPERTS = 3
TOP = 2
TOKENS = 2048
N_TENSOR = 4


def plant(entries, stream_key, least, high):
    dims = entries.shape
    place = [jax.random.randint(jax.random.fold_in(stream_key, axis), (), 0, dims[axis]) for axis in range(len(dims))]
    entries = entries.at[tuple(place)].set(least)
    longest = dims.index(max(dims))
    place[longest] = (place[longest] + 1) % dims[longest]
    return entries.at[tuple(place)].set(high)


def block_scale(own_key, extent, split, smallest, largest):
    gain = 1.0
    for dim, parts in split:
        heights = jax.random.uniform(jax.random.fold_in(jax.random.fold_in(own_key, 6), dim), (parts,), jnp.float32, smallest / len(split), largest / len(split))
        gain = gain * jnp.repeat(jnp.exp(heights), extent[dim] // parts).reshape((-1,) + (1,) * (len(extent) - 1 - dim))
    return gain


def different_ones(stream_key, rows, amount, top, lift):
    ranking = jax.random.permutation(jax.random.fold_in(stream_key, 1), amount)
    favour = ranking
    for power in range(3):
        favour = favour * favour // amount
    favour = favour * lift // amount
    chance = jax.random.randint(jax.random.fold_in(stream_key, 2), (rows, amount), 0, 4096) + favour
    holders = jax.random.permutation(jax.random.fold_in(stream_key, 3), rows)[jnp.arange(amount) % rows]
    chance = jnp.where(jnp.arange(rows)[:, None] == holders[None, :], 1 << 14, chance)
    score = chance * amount + jnp.arange(amount)
    return lax.top_k(score.astype(jnp.int32), top)[1].astype(jnp.int32)


def scatter_about(stream_key, shape, deviation, most, cuts=(), kind=jnp.bfloat16):
    gain = block_scale(stream_key, shape, cuts, -0.22, 0.18) if cuts else 1.0
    values = jax.random.normal(stream_key, shape, jnp.float32) * deviation * gain
    return jnp.minimum(jnp.maximum(values, -most), most).astype(kind)


def setup_inputs(seed: int = 0) -> dict:
    keys = jax.random.split(jax.random.key(seed), 7)
    tokens = scatter_about(keys[0], (TOKENS, D), 1.0, 6.0, ((0, 32),))
    expert_ids = different_ones(keys[1], TOKENS, EXPERTS, TOP, 0)
    gate_scores = plant(jax.random.randint(keys[2], (TOKENS, TOP), 1, 65), jax.random.fold_in(keys[2], 1), 1, 64).astype(jnp.int32)
    gate_weight = scatter_about(keys[3], (EXPERTS, D, FF), D ** -0.5, 0.0625, ((1, 32),))
    up_weight = scatter_about(keys[4], (EXPERTS, D, FF), D ** -0.5, 0.0625, ((1, 32),))
    down_weight = scatter_about(keys[5], (EXPERTS, D, FF), (FF // 2) ** -0.5, 0.1875, ((1, 32),))
    return {"tokens": tokens, "expert_ids": expert_ids, "gate_scores": gate_scores, "gate_weight": gate_weight, "up_weight": up_weight, "down_weight": down_weight}


def activate(gate_sum, up_sum, weight_col):
    return (jax.nn.silu(gate_sum) * up_sum * weight_col).astype(jnp.bfloat16)


def reference(tokens, expert_ids, gate_scores, gate_weight, up_weight, down_weight):
    scores = gate_scores.astype(jnp.float32)
    score_sum = jnp.sum(scores, axis=1, keepdims=True)
    labels = jnp.arange(EXPERTS, dtype=jnp.int32)
    picked = (expert_ids[:, :, None] == labels[None, None, :]).astype(jnp.float32)
    combine = jnp.sum(scores[:, :, None] * picked, axis=1) / score_sum
    hiddens = []
    for which in range(EXPERTS):
        gate_sum = jnp.dot(tokens, gate_weight[which], preferred_element_type=jnp.float32)
        up_sum = jnp.dot(tokens, up_weight[which], preferred_element_type=jnp.float32)
        hiddens.append(activate(gate_sum, up_sum, combine[:, which:which + 1]))
    width = FF // N_TENSOR
    result = jnp.zeros((TOKENS, D), jnp.float32)
    for shard in range(N_TENSOR):
        partial_sum = jnp.zeros((TOKENS, D), jnp.float32)
        for which in range(EXPERTS):
            hid_block = hiddens[which][:, shard * width:(shard + 1) * width]
            down_block = down_weight[which][:, shard * width:(shard + 1) * width]
            partial_sum = partial_sum + lax.dot_general(hid_block, down_block, (((1,), (1,)), ((), ())), preferred_element_type=jnp.float32)
        rounded = lax.optimization_barrier(partial_sum.astype(jnp.bfloat16))
        result = result + rounded.astype(jnp.float32)
    return result.astype(jnp.bfloat16)
```

```python
import jax
import jax.numpy as jnp
from jax import lax
from jax.experimental import pallas as pl
from jax.experimental.pallas import tpu as pltpu
from jax.sharding import PartitionSpec as P

VMEM_BYTES = 48 * 1024 * 1024


def pick_kernel(ids_ref, tok_ref, w_ref, out_ref):
    experts, _, width = w_ref.shape
    tok = tok_ref[...]
    sums = [
        jnp.dot(tok, w_ref[which], preferred_element_type=jnp.float32)
        for which in range(experts)
    ]
    for slot in range(ids_ref.shape[1]):
        chosen = ids_ref[:, slot : slot + 1]
        picked = sums[0]
        for which in range(1, experts):
            picked = jnp.where(chosen == which, sums[which], picked)
        out_ref[:, slot * width : (slot + 1) * width] = picked.astype(out_ref.dtype)


def picked_sums(ids, tok, weight):
    count, depth = tok.shape
    experts, _, width = weight.shape
    slots = ids.shape[1]
    tile = 256
    return pl.pallas_call(
        pick_kernel,
        grid=(count // tile,),
        in_specs=[
            pl.BlockSpec((tile, slots), lambda i: (i, 0)),
            pl.BlockSpec((tile, depth), lambda i: (i, 0)),
            pl.BlockSpec((experts, depth, width), lambda i: (0, 0, 0)),
        ],
        out_specs=pl.BlockSpec((tile, slots * width), lambda i: (i, 0)),
        out_shape=jax.ShapeDtypeStruct((count, slots * width), jnp.bfloat16),
        cost_estimate=pl.CostEstimate(
            flops=2 * count * depth * width * experts,
            bytes_accessed=2 * (count * depth + experts * depth * width + count * slots * width),
            transcendentals=0,
        ),
        compiler_params=pltpu.CompilerParams(vmem_limit_bytes=VMEM_BYTES),
    )(ids, tok, weight)


def down_kernel(ids_ref, hid_ref, w_ref, out_ref):
    experts, _, width = w_ref.shape
    total = None
    for which in range(experts):
        mine = jnp.zeros((hid_ref.shape[0], width), hid_ref.dtype)
        for slot in range(ids_ref.shape[1]):
            part = hid_ref[:, slot * width : (slot + 1) * width]
            mine = jnp.where(ids_ref[:, slot : slot + 1] == which, part, mine)
        term = lax.dot_general(
            mine, w_ref[which], (((1,), (1,)), ((), ())), preferred_element_type=jnp.float32
        )
        total = term if total is None else total + term
    out_ref[...] = total.astype(out_ref.dtype)


def down_sums(ids, hidden, weight):
    count = hidden.shape[0]
    experts, depth, width = weight.shape
    slots = ids.shape[1]
    tile = 256
    return pl.pallas_call(
        down_kernel,
        grid=(count // tile,),
        in_specs=[
            pl.BlockSpec((tile, slots), lambda i: (i, 0)),
            pl.BlockSpec((tile, slots * width), lambda i: (i, 0)),
            pl.BlockSpec((experts, depth, width), lambda i: (0, 0, 0)),
        ],
        out_specs=pl.BlockSpec((tile, depth), lambda i: (i, 0)),
        out_shape=jax.ShapeDtypeStruct((count, depth), jnp.bfloat16),
        cost_estimate=pl.CostEstimate(
            flops=2 * count * depth * width * experts,
            bytes_accessed=2 * (count * depth + experts * depth * width + count * slots * width),
            transcendentals=0,
        ),
        compiler_params=pltpu.CompilerParams(vmem_limit_bytes=VMEM_BYTES),
    )(ids, hidden, weight)


def local(tokens, expert_ids, gate_scores, gate_weight, up_weight, down_weight):
    n_expert, n_tensor = lax.axis_size("expert"), lax.axis_size("tensor")
    rows, model = tokens.shape
    depth = gate_weight.shape[1]
    cut = tokens.reshape(rows, n_expert, n_tensor, depth)
    cut = lax.all_to_all(cut, "tensor", split_axis=2, concat_axis=0, tiled=True)
    tok = lax.all_gather(
        cut.reshape(rows * n_tensor, n_expert * depth), "expert", axis=0, tiled=True
    )
    routing = lax.all_gather(
        jnp.concatenate([expert_ids, gate_scores], axis=1), "expert", axis=0, tiled=True
    )
    slots = expert_ids.shape[1]
    ids, scores = routing[:, :slots], routing[:, slots:].astype(jnp.float32)

    def serve(weight):
        return lax.all_to_all(weight, "expert", split_axis=2, concat_axis=1, tiled=True)

    gate_part = picked_sums(ids, tok, serve(gate_weight))
    gate_sum = lax.psum_scatter(gate_part, "tensor", scatter_dimension=0, tiled=True)
    up_part = picked_sums(ids, tok, serve(up_weight))
    up_sum = lax.psum_scatter(up_part, "tensor", scatter_dimension=0, tiled=True)

    count = gate_sum.shape[0]
    mine = lax.dynamic_slice_in_dim(scores, lax.axis_index("tensor") * count, count, 0)
    combine = mine / jnp.sum(mine, axis=1, keepdims=True)
    width = gate_sum.shape[1] // slots
    combine = jnp.repeat(combine, width, axis=1)
    hidden = (
        jax.nn.silu(gate_sum.astype(jnp.float32)) * up_sum.astype(jnp.float32) * combine
    ).astype(jnp.bfloat16)
    hidden = lax.all_gather(hidden, "tensor", axis=0, tiled=True)

    partial_sum = down_sums(ids, hidden, serve(down_weight))
    mixed = lax.psum_scatter(partial_sum, "expert", scatter_dimension=0, tiled=True)
    mixed = mixed.reshape(rows * n_tensor, n_expert, 1, depth)
    mixed = lax.all_to_all(mixed, "tensor", split_axis=0, concat_axis=2, tiled=True)
    return mixed.reshape(rows, model)


def solution(mesh):
    return jax.shard_map(
        local,
        mesh=mesh,
        in_specs=(
            P(("expert", "tensor"), None),
            P("expert", None),
            P("expert", None),
            P(None, ("expert", "tensor"), None),
            P(None, ("expert", "tensor"), None),
            P(None, ("expert", "tensor"), None),
        ),
        out_specs=P(("expert", "tensor"), None),
        check_vma=False,
    )
```

```python
import functools

import jax
import jax.numpy as jnp
from jax import lax
from jax.experimental import pallas as pl
from jax.experimental.pallas import tpu as pltpu
from jax.sharding import PartitionSpec as P

VMEM_BYTES = 48 * 1024 * 1024
CORES = 2


def fill(place_ref, own_ref, pieces, held, sems):
    experts, depth, _ = own_ref.shape
    width = held.shape[2]
    q, c = place_ref[0], place_ref[1]
    chips = len(pieces) // CORES
    copies = []
    for index in range(CORES * chips):
        side, step = index // chips, index % chips
        source = own_ref.at[:, :, pl.ds(pl.multiple_of(q * width, width), width)]
        if index > 0:
            source = pieces[index]
        block = jnp.bitwise_xor(q, step) * CORES + jnp.bitwise_xor(c, side)
        target = held.at[:, pl.ds(pl.multiple_of(block * depth, 16), depth), :]
        copies.append(pltpu.make_async_copy(source, target, sems.at[index]))
    for copy in copies:
        copy.start()
    for copy in copies:
        copy.wait()


def pick_kernel(count, place_ref, ids_ref, tok_ref, own_ref, *refs):
    pieces, (out_ref, held, sems) = (None,) + refs[: count - 1], refs[count - 1 :]

    @pl.when(pl.program_id(0) == 0)
    def _():
        fill(place_ref, own_ref, pieces, held, sems)

    experts, _, width = held.shape
    tok = tok_ref[...]
    sums = [
        jnp.dot(tok, held[which], preferred_element_type=jnp.float32)
        for which in range(experts)
    ]
    for slot in range(ids_ref.shape[1]):
        chosen = ids_ref[:, slot : slot + 1]
        picked = sums[0]
        for which in range(1, experts):
            picked = jnp.where(chosen == which, sums[which], picked)
        out_ref[:, slot * width : (slot + 1) * width] = picked.astype(out_ref.dtype)


def down_kernel(count, place_ref, ids_ref, hid_ref, own_ref, *refs):
    pieces, (out_ref, held, sems) = (None,) + refs[: count - 1], refs[count - 1 :]

    @pl.when(pl.program_id(0) == 0)
    def _():
        fill(place_ref, own_ref, pieces, held, sems)

    experts, _, width = held.shape
    total = None
    for which in range(experts):
        mine = jnp.zeros((hid_ref.shape[0], width), hid_ref.dtype)
        for slot in range(ids_ref.shape[1]):
            part = hid_ref[:, slot * width : (slot + 1) * width]
            mine = jnp.where(ids_ref[:, slot : slot + 1] == which, part, mine)
        term = lax.dot_general(
            mine, held[which], (((1,), (1,)), ((), ())), preferred_element_type=jnp.float32
        )
        total = term if total is None else total + term
    out_ref[...] = total.astype(out_ref.dtype)


def multiply(kernel, place, ids, left, own, pieces, out_width, width):
    count, slots = ids.shape
    experts, depth, _ = own.shape
    blocks = len(pieces) + 1
    tile = 256
    return pl.pallas_call(
        functools.partial(kernel, blocks),
        grid=(count // tile,),
        in_specs=[
            pl.BlockSpec(memory_space=pltpu.SMEM),
            pl.BlockSpec((tile, slots), lambda i: (i, 0)),
            pl.BlockSpec((tile, left.shape[1]), lambda i: (i, 0)),
        ]
        + [pl.BlockSpec(memory_space=pl.ANY)] * blocks,
        out_specs=pl.BlockSpec((tile, out_width), lambda i: (i, 0)),
        out_shape=jax.ShapeDtypeStruct((count, out_width), jnp.bfloat16),
        scratch_shapes=[
            pltpu.VMEM((experts, blocks * depth, width), jnp.bfloat16),
            pltpu.SemaphoreType.DMA((blocks,)),
        ],
        cost_estimate=pl.CostEstimate(
            flops=2 * count * blocks * depth * width * experts,
            bytes_accessed=2 * (left.size + experts * blocks * depth * width + count * out_width),
            transcendentals=0,
        ),
        compiler_params=pltpu.CompilerParams(vmem_limit_bytes=VMEM_BYTES),
    )(place, ids, left, own, *pieces)


def local(tokens, expert_ids, gate_scores, gate_weight, up_weight, down_weight):
    n_expert, n_tensor = lax.axis_size("expert"), lax.axis_size("tensor")
    chips = n_expert // CORES
    rows, model = tokens.shape
    experts, depth, units = gate_weight.shape
    slots = expert_ids.shape[1]
    width = units // chips
    spot, level = lax.axis_index("expert"), lax.axis_index("tensor")
    q, c = spot // CORES, spot % CORES
    place = jnp.stack([q, c])

    def to_chip(value, step):
        pairs = [(s, s ^ (step * CORES)) for s in range(n_expert)]
        return lax.ppermute(value, "expert", pairs)

    def to_core(value):
        return lax.ppermute(value, "expert", [(s, s ^ 1) for s in range(n_expert)])

    def to_level(value, step):
        return lax.ppermute(value, "tensor", [(s, s ^ step) for s in range(n_tensor)])

    def serve(weight):
        def block(step):
            return lax.dynamic_slice_in_dim(weight, (q ^ step) * width, width, 2)

        same = [to_chip(block(step), step) for step in range(1, chips)]
        other = [to_core(value) for value in [block(0)] + same]
        return same + other

    cut = tokens.reshape(rows, n_expert, n_tensor, depth).transpose(2, 0, 1, 3)
    cut = cut.reshape(n_tensor, rows, n_expert * depth)

    def level_piece(step):
        return lax.dynamic_index_in_dim(cut, level ^ step, 0, keepdims=False)

    got = [level_piece(0)] + [to_level(level_piece(s), s) for s in range(1, n_tensor)]
    group = jnp.zeros((n_tensor, rows, n_expert * depth), tokens.dtype)
    for step, value in enumerate(got):
        group = lax.dynamic_update_index_in_dim(group, value, level ^ step, 0)
    group = group.reshape(n_tensor * rows, n_expert * depth)
    tok = jnp.concatenate([group] + [to_chip(group, s) for s in range(1, chips)])
    routing = jnp.concatenate([expert_ids, gate_scores], axis=1)
    routing = jnp.concatenate([routing] + [to_chip(routing, s) for s in range(1, chips)])
    ids, scores = routing[:, :slots], routing[:, slots:].astype(jnp.float32)

    gate_pieces = serve(gate_weight)
    tok, up_weight = lax.optimization_barrier((tok, up_weight))
    up_pieces = serve(up_weight)
    up_pieces, down_weight = lax.optimization_barrier((up_pieces, down_weight))
    down_pieces = serve(down_weight)

    def picked_sums(weight, pieces):
        part = multiply(pick_kernel, place, ids, tok, weight, pieces, slots * width, width)
        return lax.psum_scatter(part, "tensor", scatter_dimension=0, tiled=True)

    gate_sum = picked_sums(gate_weight, gate_pieces)
    up_sum = picked_sums(up_weight, up_pieces)

    count = gate_sum.shape[0]
    mine = lax.dynamic_slice_in_dim(scores, level * count, count, 0)
    combine = mine / jnp.sum(mine, axis=1, keepdims=True)
    combine = jnp.repeat(combine, width, axis=1)
    hidden = (
        jax.nn.silu(gate_sum.astype(jnp.float32)) * up_sum.astype(jnp.float32) * combine
    ).astype(jnp.bfloat16)
    hidden = lax.all_gather(hidden, "tensor", axis=0, tiled=True)

    part = multiply(
        down_kernel, place, ids, hidden, down_weight, down_pieces, n_expert * depth, width
    )
    part = part.reshape(chips, n_tensor * rows, n_expert * depth)
    total = part[0].astype(jnp.float32)
    for step in range(1, chips):
        total = total + to_chip(part[step], step).astype(jnp.float32)
    total = total.astype(jnp.bfloat16).reshape(n_tensor, rows, n_expert, depth)

    def row_piece(step):
        return lax.dynamic_index_in_dim(total, level ^ step, 0, keepdims=False)

    back = [row_piece(0)] + [to_level(row_piece(s), s) for s in range(1, n_tensor)]
    mixed = jnp.zeros((n_tensor, rows, n_expert, depth), tokens.dtype)
    for step, value in enumerate(back):
        mixed = lax.dynamic_update_index_in_dim(mixed, value, level ^ step, 0)
    return mixed.transpose(1, 2, 0, 3).reshape(rows, model)


def solution(mesh):
    return jax.shard_map(
        local,
        mesh=mesh,
        in_specs=(
            P(("expert", "tensor"), None),
            P("expert", None),
            P("expert", None),
            P(None, ("expert", "tensor"), None),
            P(None, ("expert", "tensor"), None),
            P(None, ("expert", "tensor"), None),
        ),
        out_specs=P(("expert", "tensor"), None),
        check_vma=False,
    )
```

```python
import functools

import jax
import jax.numpy as jnp
from jax import lax
from jax.experimental import pallas as pl
from jax.experimental.pallas import tpu as pltpu
from jax.sharding import PartitionSpec as P

VMEM_BYTES = 32 * 1024 * 1024
CORES = 2
HALVES = 2
TILE = 256
ROWS = 16

SMEM_SPEC = pl.BlockSpec(memory_space=pltpu.SMEM)
VMEM_SPEC = pl.BlockSpec(memory_space=pltpu.VMEM)
ANY_SPEC = pl.BlockSpec(memory_space=pl.ANY)
PARAMS = pltpu.CompilerParams(vmem_limit_bytes=VMEM_BYTES)


def bf16(*shape):
    return jax.ShapeDtypeStruct(shape, jnp.bfloat16)


def cut_kernel(depth, place_ref, tokens_ref, *refs):
    outs, held = refs[:-1], refs[-1]
    levels, _, wide = held.shape
    level = place_ref[2]
    tokens = tokens_ref[...]
    for other in range(levels):
        starts = [(block * levels + other) * depth for block in range(wide // depth)]
        piece = jnp.concatenate([tokens[:, s : s + depth] for s in starts], axis=1)
        held[jnp.bitwise_xor(level, other)] = piece
    for step, out_ref in enumerate(outs):
        out_ref[...] = held[step]


def cut_tokens(place, tokens, levels, depth):
    rows, model = tokens.shape
    shape = (rows, model // levels)
    return pl.pallas_call(
        functools.partial(cut_kernel, depth),
        in_specs=[SMEM_SPEC, VMEM_SPEC],
        out_specs=[VMEM_SPEC] * levels,
        out_shape=[bf16(*shape)] * levels,
        scratch_shapes=[pltpu.VMEM((levels,) + shape, jnp.bfloat16)],
        compiler_params=PARAMS,
    )(place, tokens)


def group_kernel(levels, place_ref, *refs):
    pieces, outs = refs[:levels], refs[levels:]
    rows = pieces[0].shape[0] // HALVES
    for step, piece in enumerate(pieces):
        start = pl.multiple_of(jnp.bitwise_xor(place_ref[2], step) * rows, rows)
        for half, out_ref in enumerate(outs):
            out_ref[pl.ds(start, rows), :] = piece[half * rows : (half + 1) * rows, :]


def group_tokens(place, pieces):
    rows, wide = pieces[0].shape
    levels = len(pieces)
    return pl.pallas_call(
        functools.partial(group_kernel, levels),
        in_specs=[SMEM_SPEC] + [VMEM_SPEC] * levels,
        out_specs=[VMEM_SPEC] * HALVES,
        out_shape=[bf16(levels * rows // HALVES, wide)] * HALVES,
        compiler_params=PARAMS,
    )(place, *pieces)


def finish_kernel(depth, levels, place_ref, *refs):
    pieces, (out_ref, held) = refs[:-2], refs[-2:]
    rows, wide = pieces[0].shape
    for index, piece in enumerate(pieces):
        half, step = index // levels, index % levels
        other = jnp.bitwise_xor(place_ref[2], step)
        held[other, half * rows : (half + 1) * rows, :] = piece[...]
    parts = []
    for block in range(wide // depth):
        for other in range(levels):
            parts.append(held[other, :, block * depth : (block + 1) * depth])
    out_ref[...] = jnp.concatenate(parts, axis=1)


def finish(place, pieces, levels, depth):
    rows, wide = pieces[0].shape
    rows = rows * HALVES
    return pl.pallas_call(
        functools.partial(finish_kernel, depth, levels),
        in_specs=[SMEM_SPEC] + [VMEM_SPEC] * len(pieces),
        out_specs=VMEM_SPEC,
        out_shape=bf16(rows, wide * levels),
        scratch_shapes=[pltpu.VMEM((levels, rows, wide), jnp.bfloat16)],
        compiler_params=PARAMS,
    )(place, *pieces)


def fill(place_ref, own_ref, pieces, held, sems, staged):
    experts, depth, _ = own_ref.shape
    width = held.shape[2]
    q, c = place_ref[0], place_ref[1]
    chips = (len(pieces) + 1) // CORES
    copies = []
    for which in range(experts):
        mine = []
        for index in range(CORES * chips):
            side, step = index // chips, index % chips
            if index == 0:
                columns = pl.ds(pl.multiple_of(q * width, width), width)
                source = own_ref.at[which, :, columns]
            else:
                source = pieces[index - 1].at[which]
            block = jnp.bitwise_xor(q, step) * CORES + jnp.bitwise_xor(c, side)
            if staged:
                target = staged[0].at[which, block]
            else:
                rows = pl.ds(pl.multiple_of(block * depth, ROWS), depth)
                target = held.at[which, rows, :]
            mine.append(pltpu.make_async_copy(source, target, sems.at[which, index]))
        copies.append(mine)
    for mine in copies:
        for copy in mine:
            copy.start()

    def ready(which):
        for copy in copies[which]:
            copy.wait()
        if staged:
            for block in range(CORES * chips):
                held[which, block * depth : (block + 1) * depth, :] = staged[0][which, block]

    return ready


def weight_scratch(experts, blocks, depth, width):
    scratch = [
        pltpu.VMEM((experts, blocks * depth, width), jnp.bfloat16),
        pltpu.SemaphoreType.DMA((experts, blocks)),
    ]
    if depth % ROWS:
        scratch.append(pltpu.VMEM((experts, blocks, depth, width), jnp.bfloat16))
    return scratch


def pick_kernel(chips, blocks, place_ref, ids_ref, *refs):
    toks, refs = refs[:chips], refs[chips:]
    own_ref, pieces, refs = refs[0], refs[1:blocks], refs[blocks:]
    out_ref, left, held, sems, *staged = refs
    ready = fill(place_ref, own_ref, pieces, held, sems, staged)
    rows = toks[0].shape[0]
    for step, tok in enumerate(toks):
        left[step * rows : (step + 1) * rows, :] = tok[...]
    experts, _, width = held.shape
    tile = min(TILE, width)
    for start in range(0, width, tile):
        sums = []
        for which in range(experts):
            if start == 0:
                ready(which)
            sums.append(
                jnp.dot(
                    left[...],
                    held[which, :, start : start + tile],
                    preferred_element_type=jnp.float32,
                )
            )
        for slot in range(ids_ref.shape[1]):
            chosen = ids_ref[:, slot : slot + 1]
            picked = sums[0]
            for which in range(1, experts):
                picked = jnp.where(chosen == which, sums[which], picked)
            first = slot * width + start
            out_ref[:, first : first + tile] = picked.astype(out_ref.dtype)


def picked_sums(place, ids, toks, own, pieces):
    count, slots = ids.shape
    experts, depth, _ = own.shape
    blocks = len(pieces) + 1
    width = pieces[0].shape[2]
    wide = blocks * depth
    return pl.pallas_call(
        functools.partial(pick_kernel, len(toks), blocks),
        in_specs=[SMEM_SPEC, VMEM_SPEC] + [VMEM_SPEC] * len(toks) + [ANY_SPEC] * blocks,
        out_specs=VMEM_SPEC,
        out_shape=bf16(count, slots * width),
        scratch_shapes=[
            pltpu.VMEM((count, wide), jnp.bfloat16),
            *weight_scratch(experts, blocks, depth, width),
        ],
        cost_estimate=pl.CostEstimate(
            flops=2 * count * wide * width * experts,
            bytes_accessed=2 * (count * wide + experts * wide * width + count * slots * width),
            transcendentals=0,
        ),
        compiler_params=PARAMS,
    )(place, ids, *toks, own, *pieces)


def down_kernel(chips, blocks, place_ref, ids_ref, hid_ref, *refs):
    own_ref, pieces, refs = refs[0], refs[1:blocks], refs[blocks:]
    outs, (left, held, sems, *staged) = refs[:chips], refs[chips:]
    ready = fill(place_ref, own_ref, pieces, held, sems, staged)
    experts, wide, width = held.shape
    for which in range(experts):
        mine = jnp.zeros((hid_ref.shape[0], width), hid_ref.dtype)
        for slot in range(ids_ref.shape[1]):
            part = hid_ref[:, slot * width : (slot + 1) * width]
            mine = jnp.where(ids_ref[:, slot : slot + 1] == which, part, mine)
        left[which] = mine
    for which in range(experts):
        ready(which)
    rows = outs[0].shape[0]
    for start in range(0, wide, TILE):
        tile = min(TILE, wide - start)
        total = None
        for which in range(experts):
            term = lax.dot_general(
                left[which],
                held[which, start : start + tile, :],
                (((1,), (1,)), ((), ())),
                preferred_element_type=jnp.float32,
            )
            total = term if total is None else total + term
        for step, out_ref in enumerate(outs):
            part = total[step * rows : (step + 1) * rows]
            out_ref[:, start : start + tile] = part.astype(out_ref.dtype)


def down_sums(place, ids, hidden, own, pieces):
    count = ids.shape[0]
    experts, depth, _ = own.shape
    blocks = len(pieces) + 1
    width = pieces[0].shape[2]
    wide, chips = blocks * depth, blocks // CORES
    return pl.pallas_call(
        functools.partial(down_kernel, chips, blocks),
        in_specs=[SMEM_SPEC, VMEM_SPEC, VMEM_SPEC] + [ANY_SPEC] * blocks,
        out_specs=[VMEM_SPEC] * chips,
        out_shape=[bf16(count // chips, wide)] * chips,
        scratch_shapes=[
            pltpu.VMEM((experts, count, width), jnp.bfloat16),
            *weight_scratch(experts, blocks, depth, width),
        ],
        cost_estimate=pl.CostEstimate(
            flops=2 * count * wide * width * experts,
            bytes_accessed=2 * (hidden.size + experts * wide * width + count * wide),
            transcendentals=0,
        ),
        compiler_params=PARAMS,
    )(place, ids, hidden, own, *pieces)


def after(values, others):
    return lax.optimization_barrier((values, others))[0]


def local(tokens, expert_ids, gate_scores, gate_weight, up_weight, down_weight):
    n_expert, n_tensor = lax.axis_size("expert"), lax.axis_size("tensor")
    chips = n_expert // CORES
    rows = tokens.shape[0]
    depth, units = gate_weight.shape[1:]
    slots = expert_ids.shape[1]
    width = units // chips
    spot, level = lax.axis_index("expert"), lax.axis_index("tensor")
    q, c = spot // CORES, spot % CORES
    place = jnp.stack([q, c, level])

    def to_chip(value, step):
        pairs = [(s, s ^ (step * CORES)) for s in range(n_expert)]
        return lax.ppermute(value, "expert", pairs)

    def to_core(value):
        return lax.ppermute(value, "expert", [(s, s ^ 1) for s in range(n_expert)])

    def to_level(value, step):
        return lax.ppermute(value, "tensor", [(s, s ^ step) for s in range(n_tensor)])

    def blocks_of(weight):
        return [
            lax.dynamic_slice_in_dim(weight, (q ^ step) * width, width, 2)
            for step in range(chips)
        ]

    def chip_exchange(blocks):
        return [to_chip(blocks[step], step) for step in range(1, chips)]

    def core_exchange(blocks, same):
        return same + [to_core(value) for value in [blocks[0]] + same]

    gate_blocks = blocks_of(gate_weight)
    gate_same = chip_exchange(gate_blocks)
    cut = cut_tokens(place, after(tokens, gate_blocks), n_tensor, depth)
    cut = [cut[0]] + [to_level(cut[step], step) for step in range(1, n_tensor)]
    groups = group_tokens(place, cut)
    gate_pieces = core_exchange(gate_blocks, gate_same)

    routing = jnp.concatenate([expert_ids, gate_scores], axis=1)
    routing = lax.all_gather(routing, "expert", axis=0)
    order = jnp.stack([(q ^ step) * CORES + c for step in range(chips)])
    routing = jnp.take(routing, order, axis=0)
    routing = routing.reshape(chips, n_tensor, HALVES, rows // HALVES, 2 * slots)
    routing = [routing[:, :, half].reshape(-1, 2 * slots) for half in range(HALVES)]

    toks, barrier = [], gate_same
    for half in range(HALVES):
        group = after(groups[half], barrier)
        toks.append([group] + [to_chip(group, step) for step in range(1, chips)])
        barrier = toks[-1][1:]
    up_blocks = after(blocks_of(up_weight), barrier)
    up_pieces = core_exchange(up_blocks, chip_exchange(up_blocks))
    down_blocks = after(blocks_of(down_weight), up_pieces)
    down_pieces = core_exchange(down_blocks, chip_exchange(down_blocks))

    sums, part = [], place
    for weight, pieces in ((gate_weight, gate_pieces), (up_weight, up_pieces)):
        for half in range(HALVES):
            ids = routing[half][:, :slots]
            part = picked_sums(place, ids, after(toks[half], part), weight, pieces)
            sums.append(lax.psum_scatter(part, "tensor", scatter_dimension=0, tiled=True))
    gate_sums, up_sums = sums[:HALVES], sums[HALVES:]

    hiddens = []
    for half in range(HALVES):
        count = gate_sums[half].shape[0]
        scores = routing[half][:, slots:].astype(jnp.float32)
        scores = lax.dynamic_slice_in_dim(scores, level * count, count, 0)
        combine = scores / jnp.sum(scores, axis=1, keepdims=True)
        combine = jnp.repeat(combine, width, axis=1)
        gate_sum = gate_sums[half].astype(jnp.float32)
        up_sum = up_sums[half].astype(jnp.float32)
        hidden = (jax.nn.silu(gate_sum) * up_sum * combine).astype(jnp.bfloat16)
        hiddens.append(lax.all_gather(hidden, "tensor", axis=0, tiled=True))

    backs = []
    for half in range(HALVES):
        ids = routing[half][:, :slots]
        parts = down_sums(place, ids, hiddens[half], down_weight, down_pieces)
        total = parts[0].astype(jnp.float32)
        for step in range(1, chips):
            total = total + to_chip(parts[step], step).astype(jnp.float32)
        total = total.astype(jnp.bfloat16).reshape(n_tensor, rows // HALVES, -1)
        for step in range(n_tensor):
            piece = lax.dynamic_index_in_dim(total, level ^ step, 0, keepdims=False)
            backs.append(to_level(piece, step) if step else piece)
    return finish(place, backs, n_tensor, depth)


def solution(mesh):
    return jax.shard_map(
        local,
        mesh=mesh,
        in_specs=(
            P(("expert", "tensor"), None),
            P("expert", None),
            P("expert", None),
            P(None, ("expert", "tensor"), None),
            P(None, ("expert", "tensor"), None),
            P(None, ("expert", "tensor"), None),
        ),
        out_specs=P(("expert", "tensor"), None),
        check_vma=False,
    )
```

```python
import functools

import jax
import jax.numpy as jnp
from jax import lax
from jax.experimental import pallas as pl
from jax.experimental.pallas import tpu as pltpu
from jax.sharding import PartitionSpec as P

VMEM_BYTES = 22 * 1024 * 1024
CORES = 2
HALVES = 2
TILE = 256
ROWS = 16

SMEM_SPEC = pl.BlockSpec(memory_space=pltpu.SMEM)
VMEM_SPEC = pl.BlockSpec(memory_space=pltpu.VMEM)
ANY_SPEC = pl.BlockSpec(memory_space=pl.ANY)
PARAMS = pltpu.CompilerParams(vmem_limit_bytes=VMEM_BYTES)


def bf16(*shape):
    return jax.ShapeDtypeStruct(shape, jnp.bfloat16)


def cut_kernel(depth, place_ref, tokens_ref, *refs):
    outs, held = refs[:-1], refs[-1]
    levels, _, wide = held.shape
    level = place_ref[2]
    tokens = tokens_ref[...]
    for other in range(levels):
        starts = [(block * levels + other) * depth for block in range(wide // depth)]
        piece = jnp.concatenate([tokens[:, s : s + depth] for s in starts], axis=1)
        held[jnp.bitwise_xor(level, other)] = piece
    for step, out_ref in enumerate(outs):
        out_ref[...] = held[step]


def cut_tokens(place, tokens, levels, depth):
    rows, model = tokens.shape
    shape = (rows, model // levels)
    return pl.pallas_call(
        functools.partial(cut_kernel, depth),
        in_specs=[SMEM_SPEC, VMEM_SPEC],
        out_specs=[VMEM_SPEC] * levels,
        out_shape=[bf16(*shape)] * levels,
        scratch_shapes=[pltpu.VMEM((levels,) + shape, jnp.bfloat16)],
        compiler_params=PARAMS,
    )(place, tokens)


def group_kernel(levels, place_ref, *refs):
    pieces, outs = refs[:levels], refs[levels:]
    rows = pieces[0].shape[0] // HALVES
    for step, piece in enumerate(pieces):
        start = pl.multiple_of(jnp.bitwise_xor(place_ref[2], step) * rows, rows)
        for half, out_ref in enumerate(outs):
            out_ref[pl.ds(start, rows), :] = piece[half * rows : (half + 1) * rows, :]


def group_tokens(place, pieces):
    rows, wide = pieces[0].shape
    levels = len(pieces)
    return pl.pallas_call(
        functools.partial(group_kernel, levels),
        in_specs=[SMEM_SPEC] + [VMEM_SPEC] * levels,
        out_specs=[VMEM_SPEC] * HALVES,
        out_shape=[bf16(levels * rows // HALVES, wide)] * HALVES,
        compiler_params=PARAMS,
    )(place, *pieces)


def finish_kernel(depth, levels, place_ref, *refs):
    pieces, (out_ref, held) = refs[:-2], refs[-2:]
    rows, wide = pieces[0].shape
    for index, piece in enumerate(pieces):
        half, step = index // levels, index % levels
        other = jnp.bitwise_xor(place_ref[2], step)
        held[other, half * rows : (half + 1) * rows, :] = piece[...]
    parts = []
    for block in range(wide // depth):
        for other in range(levels):
            parts.append(held[other, :, block * depth : (block + 1) * depth])
    out_ref[...] = jnp.concatenate(parts, axis=1)


def finish(place, pieces, levels, depth):
    rows, wide = pieces[0].shape
    rows = rows * HALVES
    return pl.pallas_call(
        functools.partial(finish_kernel, depth, levels),
        in_specs=[SMEM_SPEC] + [VMEM_SPEC] * len(pieces),
        out_specs=VMEM_SPEC,
        out_shape=bf16(rows, wide * levels),
        scratch_shapes=[pltpu.VMEM((levels, rows, wide), jnp.bfloat16)],
        compiler_params=PARAMS,
    )(place, *pieces)


def fill(place_ref, own_ref, pieces, held, sems, staged):
    experts, depth, _ = own_ref.shape
    width = held.shape[2]
    q, c = place_ref[0], place_ref[1]
    chips = (len(pieces) + 1) // CORES
    copies = []
    for which in range(experts):
        mine = []
        for index in range(CORES * chips):
            side, step = index // chips, index % chips
            if index == 0:
                columns = pl.ds(pl.multiple_of(q * width, width), width)
                source = own_ref.at[which, :, columns]
            else:
                source = pieces[index - 1].at[which]
            block = jnp.bitwise_xor(q, step) * CORES + jnp.bitwise_xor(c, side)
            if staged:
                target = staged[0].at[which, block]
            else:
                rows = pl.ds(pl.multiple_of(block * depth, ROWS), depth)
                target = held.at[which, rows, :]
            mine.append(pltpu.make_async_copy(source, target, sems.at[which, index]))
        copies.append(mine)
    for mine in copies:
        for copy in mine:
            copy.start()

    def ready(which):
        for copy in copies[which]:
            copy.wait()
        if staged:
            for block in range(CORES * chips):
                held[which, block * depth : (block + 1) * depth, :] = staged[0][which, block]

    return ready


def weight_scratch(experts, blocks, depth, width):
    scratch = [
        pltpu.VMEM((experts, blocks * depth, width), jnp.bfloat16),
        pltpu.SemaphoreType.DMA((experts, blocks)),
    ]
    if depth % ROWS:
        scratch.append(pltpu.VMEM((experts, blocks, depth, width), jnp.bfloat16))
    return scratch


def rows_of(block, rows):
    return pl.ds(pl.multiple_of(block * rows, rows), rows)


def pick_kernel(chips, blocks, place_ref, ids_ref, *refs):
    toks, refs = refs[:chips], refs[chips:]
    own_ref, pieces, refs = refs[0], refs[1:blocks], refs[blocks:]
    outs, (left, held, sems, *staged) = refs[:chips], refs[chips:]
    ready = fill(place_ref, own_ref, pieces, held, sems, staged)
    level = place_ref[2]
    rows, slots = ids_ref.shape[1], ids_ref.shape[2]
    for step, tok in enumerate(toks):
        left[rows_of(jnp.bitwise_xor(step, level), rows), :] = tok[...]
    experts, _, width = held.shape
    tile = min(TILE, width)
    for start in range(0, width, tile):
        sums = []
        for which in range(experts):
            if start == 0:
                ready(which)
            sums.append(
                jnp.dot(
                    left[...],
                    held[which, :, start : start + tile],
                    preferred_element_type=jnp.float32,
                )
            )
        for step, out_ref in enumerate(outs):
            ids = ids_ref[jnp.bitwise_xor(step, level)]
            for slot in range(slots):
                picked = sums[0][step * rows : (step + 1) * rows]
                for which in range(1, experts):
                    other = sums[which][step * rows : (step + 1) * rows]
                    picked = jnp.where(ids[:, slot : slot + 1] == which, other, picked)
                first = slot * width + start
                out_ref[:, first : first + tile] = picked.astype(out_ref.dtype)


def picked_sums(place, ids, toks, own, pieces):
    chips, rows, slots = ids.shape
    experts, depth, _ = own.shape
    blocks = len(pieces) + 1
    width = pieces[0].shape[2]
    wide, count = blocks * depth, chips * rows
    return pl.pallas_call(
        functools.partial(pick_kernel, chips, blocks),
        in_specs=[SMEM_SPEC, VMEM_SPEC] + [VMEM_SPEC] * chips + [ANY_SPEC] * blocks,
        out_specs=[VMEM_SPEC] * chips,
        out_shape=[bf16(rows, slots * width)] * chips,
        scratch_shapes=[
            pltpu.VMEM((count, wide), jnp.bfloat16),
            *weight_scratch(experts, blocks, depth, width),
        ],
        cost_estimate=pl.CostEstimate(
            flops=2 * count * wide * width * experts,
            bytes_accessed=2 * (count * wide + experts * wide * width + count * slots * width),
            transcendentals=0,
        ),
        compiler_params=PARAMS,
    )(place, ids, *toks, own, *pieces)


def hidden_kernel(terms, place_ref, scores_ref, *refs):
    gates, ups, out_ref = refs[:terms], refs[terms : 2 * terms], refs[2 * terms]
    scores = scores_ref[place_ref[2]].astype(jnp.float32)
    slots = scores.shape[1]
    combine = scores / jnp.sum(scores, axis=1, keepdims=True)
    width = out_ref.shape[1] // slots
    for slot in range(slots):
        columns = slice(slot * width, (slot + 1) * width)
        gate_sum = sum(ref[:, columns].astype(jnp.float32) for ref in gates)
        up_sum = sum(ref[:, columns].astype(jnp.float32) for ref in ups)
        value = gate_sum / (1.0 + jnp.exp(-gate_sum)) * up_sum * combine[:, slot : slot + 1]
        out_ref[:, columns] = value.astype(out_ref.dtype)


def hidden_rows(place, scores, gates, ups):
    return pl.pallas_call(
        functools.partial(hidden_kernel, len(gates)),
        in_specs=[SMEM_SPEC] + [VMEM_SPEC] * (1 + 2 * len(gates)),
        out_specs=VMEM_SPEC,
        out_shape=bf16(*gates[0].shape),
        compiler_params=PARAMS,
    )(place, scores, *gates, *ups)


def down_kernel(chips, blocks, place_ref, ids_ref, *refs):
    hids, refs = refs[:chips], refs[chips:]
    own_ref, pieces, refs = refs[0], refs[1:blocks], refs[blocks:]
    outs, (left, held, sems, *staged) = refs[:chips], refs[chips:]
    ready = fill(place_ref, own_ref, pieces, held, sems, staged)
    experts, wide, width = held.shape
    rows, slots = ids_ref.shape[1], ids_ref.shape[2]
    for step, hid_ref in enumerate(hids):
        block = jnp.bitwise_xor(step, place_ref[2])
        ids = ids_ref[block]
        for which in range(experts):
            mine = jnp.zeros((rows, width), hid_ref.dtype)
            for slot in range(slots):
                part = hid_ref[:, slot * width : (slot + 1) * width]
                mine = jnp.where(ids[:, slot : slot + 1] == which, part, mine)
            left[which, rows_of(block, rows), :] = mine
    for which in range(experts):
        ready(which)
    for start in range(0, wide, TILE):
        tile = min(TILE, wide - start)
        total = None
        for which in range(experts):
            term = lax.dot_general(
                left[which],
                held[which, start : start + tile, :],
                (((1,), (1,)), ((), ())),
                preferred_element_type=jnp.float32,
            )
            total = term if total is None else total + term
        for step, out_ref in enumerate(outs):
            part = total[step * rows : (step + 1) * rows]
            out_ref[:, start : start + tile] = part.astype(out_ref.dtype)


def down_sums(place, ids, hids, own, pieces):
    chips, rows, slots = ids.shape
    experts, depth, _ = own.shape
    blocks = len(pieces) + 1
    width = pieces[0].shape[2]
    wide, count = blocks * depth, chips * rows
    return pl.pallas_call(
        functools.partial(down_kernel, chips, blocks),
        in_specs=[SMEM_SPEC, VMEM_SPEC] + [VMEM_SPEC] * chips + [ANY_SPEC] * blocks,
        out_specs=[VMEM_SPEC] * chips,
        out_shape=[bf16(rows, wide)] * chips,
        scratch_shapes=[
            pltpu.VMEM((experts, count, width), jnp.bfloat16),
            *weight_scratch(experts, blocks, depth, width),
        ],
        cost_estimate=pl.CostEstimate(
            flops=2 * count * wide * width * experts,
            bytes_accessed=2 * (count * slots * width + experts * wide * width + count * wide),
            transcendentals=0,
        ),
        compiler_params=PARAMS,
    )(place, ids, *hids, own, *pieces)


def after(values, others):
    return lax.optimization_barrier((values, others))[0]


def local(tokens, expert_ids, gate_scores, gate_weight, up_weight, down_weight):
    n_expert, n_tensor = lax.axis_size("expert"), lax.axis_size("tensor")
    chips = n_expert // CORES
    rows = tokens.shape[0]
    depth, units = gate_weight.shape[1:]
    slots = expert_ids.shape[1]
    width = units // chips
    spot, level = lax.axis_index("expert"), lax.axis_index("tensor")
    q, c = spot // CORES, spot % CORES
    place = jnp.stack([q, c, level])

    def to_chip(value, step):
        pairs = [(s, s ^ (step * CORES)) for s in range(n_expert)]
        return lax.ppermute(value, "expert", pairs)

    def to_core(value):
        return lax.ppermute(value, "expert", [(s, s ^ 1) for s in range(n_expert)])

    def to_level(value, step):
        return lax.ppermute(value, "tensor", [(s, s ^ step) for s in range(n_tensor)])

    def blocks_of(weight):
        return [
            lax.dynamic_slice_in_dim(weight, (q ^ step) * width, width, 2)
            for step in range(chips)
        ]

    def chip_exchange(blocks):
        return [to_chip(blocks[step], step) for step in range(1, chips)]

    def core_exchange(blocks, same):
        return same + [to_core(value) for value in [blocks[0]] + same]

    def level_sums(parts):
        terms, bit = [[part] for part in parts], 1
        while bit < n_tensor:
            for step in range(n_tensor - bit, 0, -2 * bit):
                value = terms[step][0]
                if len(terms[step]) > 1:
                    value = sum(term.astype(jnp.float32) for term in terms[step])
                terms[step - bit].append(to_level(value.astype(jnp.bfloat16), bit))
            bit *= 2
        return terms[0]

    def level_copies(value):
        held, bit = {0: value}, n_tensor // 2
        while bit:
            for step in sorted(held):
                held[step + bit] = to_level(held[step], bit)
            bit //= 2
        return [held[step] for step in range(n_tensor)]

    routing = jnp.concatenate([expert_ids, gate_scores], axis=1)
    routing = [routing] + [to_chip(routing, step) for step in range(1, chips)]
    gate_blocks = after(blocks_of(gate_weight), routing)
    routing = jnp.stack(routing).reshape(chips, n_tensor, HALVES, rows // HALVES, 2 * slots)
    routing = routing.transpose(2, 0, 1, 3, 4).reshape(HALVES, chips, -1, 2 * slots)
    ids, scores = routing[..., :slots], routing[..., slots:]

    cut = cut_tokens(place, tokens, n_tensor, depth)
    cut = [cut[0]] + [to_level(cut[step], step) for step in range(1, n_tensor)]
    groups = group_tokens(place, cut)
    gate_same = chip_exchange(gate_blocks)
    gate_pieces = core_exchange(gate_blocks, gate_same)

    toks, barrier = [], gate_same
    for half in range(HALVES):
        group = after(groups[half], barrier)
        toks.append([group] + [to_chip(group, step) for step in range(1, chips)])
        barrier = toks[-1][1:]
    up_blocks = after(blocks_of(up_weight), barrier)
    up_pieces = core_exchange(up_blocks, chip_exchange(up_blocks))
    down_blocks = after(blocks_of(down_weight), up_pieces)
    down_pieces = core_exchange(down_blocks, chip_exchange(down_blocks))

    sums, parts = [], place
    for weight, pieces in ((gate_weight, gate_pieces), (up_weight, up_pieces)):
        for half in range(HALVES):
            left = after(toks[half], parts)
            parts = picked_sums(place, ids[half], left, weight, pieces)
            sums.append(level_sums(parts))

    hiddens = []
    for half in range(HALVES):
        hidden = hidden_rows(place, scores[half], sums[half], sums[HALVES + half])
        hiddens.append(level_copies(hidden))

    backs = []
    for half in range(HALVES):
        parts = down_sums(place, ids[half], hiddens[half], down_weight, down_pieces)
        total = parts[0].astype(jnp.float32)
        for step in range(1, chips):
            total = total + to_chip(parts[step], step).astype(jnp.float32)
        total = total.astype(jnp.bfloat16).reshape(n_tensor, rows // HALVES, -1)
        for step in range(n_tensor):
            piece = lax.dynamic_index_in_dim(total, level ^ step, 0, keepdims=False)
            backs.append(to_level(piece, step) if step else piece)
    return finish(place, backs, n_tensor, depth)


def solution(mesh):
    return jax.shard_map(
        local,
        mesh=mesh,
        in_specs=(
            P(("expert", "tensor"), None),
            P("expert", None),
            P("expert", None),
            P(None, ("expert", "tensor"), None),
            P(None, ("expert", "tensor"), None),
            P(None, ("expert", "tensor"), None),
        ),
        out_specs=P(("expert", "tensor"), None),
        check_vma=False,
    )
```

```python
import functools

import jax
import jax.numpy as jnp
from jax import lax
from jax.experimental import pallas as pl
from jax.experimental.pallas import tpu as pltpu
from jax.sharding import PartitionSpec as P

VMEM_BYTES = 22 * 1024 * 1024
CORES = 2
HALVES = 2
TILE = 256
LANES = 128

SMEM_SPEC = pl.BlockSpec(memory_space=pltpu.SMEM)
VMEM_SPEC = pl.BlockSpec(memory_space=pltpu.VMEM)
ANY_SPEC = pl.BlockSpec(memory_space=pl.ANY)
PARAMS = pltpu.CompilerParams(vmem_limit_bytes=VMEM_BYTES)


def bf16(*shape):
    return jax.ShapeDtypeStruct(shape, jnp.bfloat16)


def cost(flops, elements):
    return pl.CostEstimate(flops=flops, bytes_accessed=2 * elements, transcendentals=0)


def rows_of(block, rows):
    return pl.ds(pl.multiple_of(block * rows, rows), rows)


def cut_kernel(depth, place_ref, tokens_ref, *refs):
    outs, held = refs[:-1], refs[-1]
    levels, _, wide = held.shape
    core, level = place_ref[1], place_ref[2]
    tokens = tokens_ref[...]
    for other in range(levels):
        sides = []
        for side in range(CORES):
            blocks = range(side, wide // depth, CORES)
            starts = [(block * levels + other) * depth for block in blocks]
            sides.append(jnp.concatenate([tokens[:, s : s + depth] for s in starts], axis=1))
        swapped = jnp.concatenate(sides[::-1], axis=1)
        piece = jnp.where(core == 0, jnp.concatenate(sides, axis=1), swapped)
        held[jnp.bitwise_xor(level, other)] = piece
    for step, out_ref in enumerate(outs):
        out_ref[...] = held[step]


def cut_tokens(place, tokens, levels, depth):
    rows, model = tokens.shape
    shape = (rows, model // levels)
    return pl.pallas_call(
        functools.partial(cut_kernel, depth),
        in_specs=[SMEM_SPEC, VMEM_SPEC],
        out_specs=[VMEM_SPEC] * levels,
        out_shape=[bf16(*shape)] * levels,
        scratch_shapes=[pltpu.VMEM((levels,) + shape, jnp.bfloat16)],
        compiler_params=PARAMS,
    )(place, tokens)


def group_kernel(levels, place_ref, routing_ref, *refs):
    pieces, outs = refs[:levels], refs[levels:]
    wide = pieces[0].shape[1]
    rows = pieces[0].shape[0] // HALVES
    for step, piece in enumerate(pieces):
        target = rows_of(jnp.bitwise_xor(place_ref[2], step), rows)
        for half, out_ref in enumerate(outs):
            out_ref[target, :wide] = piece[half * rows : (half + 1) * rows, :]
    for level in range(levels):
        for half, out_ref in enumerate(outs):
            first = (level * HALVES + half) * rows
            out_ref[level * rows : (level + 1) * rows, wide:] = routing_ref[first : first + rows, :]


def group_tokens(place, routing, pieces):
    rows, wide = pieces[0].shape
    levels = len(pieces)
    return pl.pallas_call(
        functools.partial(group_kernel, levels),
        in_specs=[SMEM_SPEC, VMEM_SPEC] + [VMEM_SPEC] * levels,
        out_specs=[VMEM_SPEC] * HALVES,
        out_shape=[bf16(levels * rows // HALVES, wide + LANES)] * HALVES,
        compiler_params=PARAMS,
    )(place, routing, *pieces)


def finish_kernel(depth, levels, place_ref, *refs):
    pieces, (out_ref, held) = refs[:-2], refs[-2:]
    rows, wide = pieces[0].shape
    for index, piece in enumerate(pieces):
        half, step = index // levels, index % levels
        other = jnp.bitwise_xor(place_ref[2], step)
        held[other, half * rows : (half + 1) * rows, :] = piece[...]
    chips = wide // depth // CORES
    first, second = [], []
    for chip in range(chips):
        for side in range(CORES):
            for other in range(levels):
                for parts, place in ((first, side), (second, 1 - side)):
                    start = (place * chips + chip) * depth
                    parts.append(held[other, :, start : start + depth])
    first, second = jnp.concatenate(first, axis=1), jnp.concatenate(second, axis=1)
    out_ref[...] = jnp.where(place_ref[1] == 0, first, second)


def finish(place, pieces, levels, depth):
    rows, wide = pieces[0].shape
    rows = rows * HALVES
    return pl.pallas_call(
        functools.partial(finish_kernel, depth, levels),
        in_specs=[SMEM_SPEC] + [VMEM_SPEC] * len(pieces),
        out_specs=VMEM_SPEC,
        out_shape=bf16(rows, wide * levels),
        scratch_shapes=[pltpu.VMEM((levels, rows, wide), jnp.bfloat16)],
        compiler_params=PARAMS,
    )(place, *pieces)


def join_kernel(chips, place_ref, own_ref, *refs):
    pieces, (out_ref, sems) = refs[: chips - 1], refs[chips - 1 :]
    width = out_ref.shape[3]
    chip = place_ref[0]
    columns = pl.ds(pl.multiple_of(chip * width, width), width)
    sources = [own_ref.at[:, :, columns]] + list(pieces)
    copies = [
        pltpu.make_async_copy(source, out_ref.at[:, jnp.bitwise_xor(chip, step)], sems.at[step])
        for step, source in enumerate(sources)
    ]
    for copy in copies:
        copy.start()
    for copy in copies:
        copy.wait()


def join_blocks(place, own, pieces):
    experts, depth, units = own.shape
    chips = len(pieces) + 1
    shape = (experts, chips, depth, units // chips)
    return pl.pallas_call(
        functools.partial(join_kernel, chips),
        in_specs=[SMEM_SPEC] + [ANY_SPEC] * chips,
        out_specs=VMEM_SPEC,
        out_shape=bf16(*shape),
        scratch_shapes=[pltpu.SemaphoreType.DMA((chips,))],
        cost_estimate=cost(0, 2 * own.size),
        compiler_params=PARAMS,
    )(place, own, *pieces)


def pick_kernel(chips, place_ref, *refs):
    toks, refs = refs[:chips], refs[chips:]
    weights, (keep_ref, send_ref, routing_ref, left) = refs[:CORES], refs[CORES:]
    experts, depth, width = weights[0].shape
    rows = toks[0].shape[0]
    for step, tok in enumerate(toks):
        block = jnp.bitwise_xor(step, place_ref[2])
        left[rows_of(block, rows), :] = tok[:, : CORES * depth]
        routing_ref[block] = tok[:, CORES * depth :]
    slots = keep_ref.shape[2] // width
    tile = min(TILE, width)
    for start in range(0, width, tile):
        sums = []
        for which in range(experts):
            total = None
            for side, weight in enumerate(weights):
                term = jnp.dot(
                    left[:, side * depth : (side + 1) * depth],
                    weight[which, :, start : start + tile],
                    preferred_element_type=jnp.float32,
                )
                total = term if total is None else total + term
            sums.append(total)
        for step in range(chips):
            out_ref = (keep_ref, send_ref)[step % 2]
            ids = routing_ref[step].astype(jnp.float32)
            for slot in range(slots):
                chosen = ids[:, slot : slot + 1]
                picked = sums[0][step * rows : (step + 1) * rows]
                for which in range(1, experts):
                    other = sums[which][step * rows : (step + 1) * rows]
                    picked = jnp.where(chosen == which, other, picked)
                first = slot * width + start
                out_ref[step // 2, :, first : first + tile] = picked.astype(out_ref.dtype)


def picked_sums(place, toks, weights, slots):
    chips, rows = len(toks), toks[0].shape[0]
    experts, depth, width = weights[0].shape
    wide = CORES * depth
    count = chips * rows
    return pl.pallas_call(
        functools.partial(pick_kernel, chips),
        in_specs=[SMEM_SPEC] + [VMEM_SPEC] * (chips + CORES),
        out_specs=[VMEM_SPEC] * 3,
        out_shape=[bf16(chips // 2, rows, slots * width)] * 2 + [bf16(chips, rows, LANES)],
        scratch_shapes=[pltpu.VMEM((count, wide), jnp.bfloat16)],
        cost_estimate=cost(
            2 * count * wide * width * experts,
            count * wide + experts * wide * width + count * slots * width,
        ),
        compiler_params=PARAMS,
    )(place, *toks, *weights)


def hidden_kernel(terms, slots, routing_ref, *refs):
    gates, ups, out_ref = refs[:terms], refs[terms : 2 * terms], refs[2 * terms]
    scores = routing_ref[0].astype(jnp.float32)[:, slots : 2 * slots]
    combine = scores / jnp.sum(scores, axis=1, keepdims=True)
    width = out_ref.shape[1] // slots
    for slot in range(slots):
        columns = slice(slot * width, (slot + 1) * width)
        gate_sum = sum(ref[0, :, columns].astype(jnp.float32) for ref in gates)
        up_sum = sum(ref[0, :, columns].astype(jnp.float32) for ref in ups)
        value = gate_sum / (1.0 + jnp.exp(-gate_sum)) * up_sum * combine[:, slot : slot + 1]
        out_ref[:, columns] = value.astype(out_ref.dtype)


def hidden_rows(routing, gates, ups, slots):
    return pl.pallas_call(
        functools.partial(hidden_kernel, len(gates), slots),
        in_specs=[VMEM_SPEC] * (1 + 2 * len(gates)),
        out_specs=VMEM_SPEC,
        out_shape=bf16(*gates[0].shape[1:]),
        compiler_params=PARAMS,
    )(routing, *gates, *ups)


def down_kernel(step, slots, routing_ref, hid_ref, *refs):
    weights, (out_ref,) = refs[:CORES], refs[CORES:]
    experts, depth, width = weights[0].shape
    ids = routing_ref[step].astype(jnp.float32)
    lefts = []
    for which in range(experts):
        mine = jnp.zeros((hid_ref.shape[0], width), jnp.float32)
        for slot in range(slots):
            part = hid_ref[:, slot * width : (slot + 1) * width].astype(jnp.float32)
            mine = jnp.where(ids[:, slot : slot + 1] == which, part, mine)
        lefts.append(mine.astype(hid_ref.dtype))
    for side, weight in enumerate(weights):
        total = None
        for which in range(experts):
            term = lax.dot_general(
                lefts[which],
                weight[which],
                (((1,), (1,)), ((), ())),
                preferred_element_type=jnp.float32,
            )
            total = term if total is None else total + term
        out_ref[:, side * depth : (side + 1) * depth] = total.astype(out_ref.dtype)


def down_sums(routing, hidden, weights, step, slots):
    rows = hidden.shape[0]
    experts, depth, width = weights[0].shape
    wide = CORES * depth
    return pl.pallas_call(
        functools.partial(down_kernel, step, slots),
        in_specs=[VMEM_SPEC] * (2 + CORES),
        out_specs=VMEM_SPEC,
        out_shape=bf16(rows, wide),
        cost_estimate=cost(
            2 * rows * wide * width * experts,
            rows * slots * width + experts * wide * width + rows * wide,
        ),
        compiler_params=PARAMS,
    )(routing, hidden, *weights)


def after(values, others):
    return lax.optimization_barrier((values, others))[0]


def local(tokens, expert_ids, gate_scores, gate_weight, up_weight, down_weight):
    n_expert, n_tensor = lax.axis_size("expert"), lax.axis_size("tensor")
    chips = n_expert // CORES
    rows = tokens.shape[0]
    depth, units = gate_weight.shape[1:]
    slots = expert_ids.shape[1]
    width = units // chips
    spot, level = lax.axis_index("expert"), lax.axis_index("tensor")
    q, c = spot // CORES, spot % CORES
    place = jnp.stack([q, c, level])

    def to_chip(value, step):
        pairs = [(s, s ^ (step * CORES)) for s in range(n_expert)]
        return lax.ppermute(value, "expert", pairs)

    def to_core(value):
        return lax.ppermute(value, "expert", [(s, s ^ 1) for s in range(n_expert)])

    def to_level(value, step):
        return lax.ppermute(value, "tensor", [(s, s ^ step) for s in range(n_tensor)])

    def to_owner(value, step):
        pairs = [
            (s * n_tensor + t, (s ^ ((t ^ step) * CORES)) * n_tensor + t)
            for s in range(n_expert)
            for t in range(n_tensor)
        ]
        return lax.ppermute(value, ("expert", "tensor"), pairs)

    def copies(value, send, bits):
        held = {0: value}
        for bit in bits:
            for step in sorted(held):
                held[step + bit] = send(held[step], bit)
        return [held[step] for step in range(len(held))]

    def level_sums(keep, send):
        terms, bit = [keep], 1
        while True:
            terms.append(to_level(send, bit))
            bit *= 2
            if bit == n_tensor:
                return terms
            send = sum(term[1::2].astype(jnp.float32) for term in terms).astype(jnp.bfloat16)
            terms = [term[::2] for term in terms]

    def blocks_of(weight):
        return [
            lax.dynamic_slice_in_dim(weight, (q ^ step) * width, width, 2)
            for step in range(1, chips)
        ]

    def chip_exchange(blocks):
        return [to_chip(block, step) for step, block in enumerate(blocks, 1)]

    def core_exchange(joined):
        pair = [joined, to_core(joined)]
        return [side.reshape(side.shape[0], chips * depth, width) for side in pair]

    routing = jnp.concatenate([expert_ids, gate_scores], axis=1).astype(jnp.bfloat16)
    routing = jnp.pad(routing, ((0, 0), (0, LANES - 2 * slots)))
    gate_same = chip_exchange(blocks_of(gate_weight))
    cut = cut_tokens(place, tokens, n_tensor, depth)
    cut = [cut[0]] + [to_level(cut[step], step) for step in range(1, n_tensor)]
    groups = group_tokens(place, routing, cut)

    gate_joined = join_blocks(place, gate_weight, after(gate_same, groups))
    gate_pair = core_exchange(gate_joined)
    groups = after(groups, gate_joined)
    bits = [1 << bit for bit in range(chips.bit_length() - 1)]
    toks = []
    for half in range(HALVES):
        turn = (half + 1) % len(bits)
        toks.append(copies(groups[half], to_chip, bits[turn:] + bits[:turn]))
    up_same = chip_exchange(after(blocks_of(up_weight), toks))

    def products(weights, parts):
        routings, sends = [], []
        for half in range(HALVES):
            left = after(toks[half], parts)
            *parts, routing = picked_sums(place, left, weights, slots)
            routings.append(routing)
            sends.append(parts)
        sums = [level_sums(*parts) for parts in sends]
        return routings, sums

    routings, gate_sums = products(gate_pair, place)
    up_joined = join_blocks(place, up_weight, after(up_same, [terms[:-1] for terms in gate_sums]))
    up_pair = core_exchange(up_joined)
    down_same = chip_exchange(after(blocks_of(down_weight), up_joined))
    _, up_sums = products(up_pair, gate_sums)
    hiddens = [
        hidden_rows(routings[half], gate_sums[half], up_sums[half], slots)
        for half in range(HALVES)
    ]
    down_joined = join_blocks(place, down_weight, after(down_same, hiddens[0]))
    down_pair = core_exchange(down_joined)

    backs = []
    bits = [1 << bit for bit in range(n_tensor.bit_length() - 1)]
    for half in range(HALVES):
        routing = routings[half]
        blocks = copies(hiddens[half], to_level, bits[::-1])
        total = 0.0
        for step in range(n_tensor):
            part = down_sums(routing, blocks[step], down_pair, step, slots)
            total = total + to_owner(part, step).astype(jnp.float32)
        total = total.astype(jnp.bfloat16).reshape(n_tensor, rows // HALVES, -1)
        for step in range(n_tensor):
            piece = lax.dynamic_index_in_dim(total, level ^ step, 0, keepdims=False)
            backs.append(to_level(piece, step) if step else piece)
    return finish(place, backs, n_tensor, depth)


def solution(mesh):
    return jax.shard_map(
        local,
        mesh=mesh,
        in_specs=(
            P(("expert", "tensor"), None),
            P("expert", None),
            P("expert", None),
            P(None, ("expert", "tensor"), None),
            P(None, ("expert", "tensor"), None),
            P(None, ("expert", "tensor"), None),
        ),
        out_specs=P(("expert", "tensor"), None),
        check_vma=False,
    )
```

```python
import functools

import jax
import jax.numpy as jnp
from jax import lax
from jax.experimental import pallas as pl
from jax.experimental.pallas import tpu as pltpu
from jax.sharding import PartitionSpec as P

VMEM_BYTES = 22 * 1024 * 1024
CORES = 2
HALVES = 2
TILE = 256
LANES = 128

SMEM_SPEC = pl.BlockSpec(memory_space=pltpu.SMEM)
VMEM_SPEC = pl.BlockSpec(memory_space=pltpu.VMEM)
ANY_SPEC = pl.BlockSpec(memory_space=pl.ANY)
PARAMS = pltpu.CompilerParams(vmem_limit_bytes=VMEM_BYTES)


def bf16(*shape):
    return jax.ShapeDtypeStruct(shape, jnp.bfloat16)


def cost(flops, elements):
    return pl.CostEstimate(flops=flops, bytes_accessed=2 * elements, transcendentals=0)


def rows_of(block, rows):
    return pl.ds(pl.multiple_of(block * rows, rows), rows)


def cut_kernel(depth, place_ref, tokens_ref, *refs):
    outs, held = refs[:-1], refs[-1]
    levels, _, wide = held.shape
    core, level = place_ref[1], place_ref[2]
    tokens = tokens_ref[...]
    for other in range(levels):
        sides = []
        for side in range(CORES):
            blocks = range(side, wide // depth, CORES)
            starts = [(block * levels + other) * depth for block in blocks]
            sides.append(jnp.concatenate([tokens[:, s : s + depth] for s in starts], axis=1))
        swapped = jnp.concatenate(sides[::-1], axis=1)
        piece = jnp.where(core == 0, jnp.concatenate(sides, axis=1), swapped)
        held[jnp.bitwise_xor(level, other)] = piece
    for step, out_ref in enumerate(outs):
        out_ref[...] = held[step]


def cut_tokens(place, tokens, levels, depth):
    rows, model = tokens.shape
    shape = (rows, model // levels)
    return pl.pallas_call(
        functools.partial(cut_kernel, depth),
        in_specs=[SMEM_SPEC, VMEM_SPEC],
        out_specs=[VMEM_SPEC] * levels,
        out_shape=[bf16(*shape)] * levels,
        scratch_shapes=[pltpu.VMEM((levels,) + shape, jnp.bfloat16)],
        compiler_params=PARAMS,
    )(place, tokens)


def group_kernel(levels, place_ref, routing_ref, *refs):
    pieces, outs = refs[:levels], refs[levels:]
    wide = pieces[0].shape[1]
    rows = pieces[0].shape[0] // HALVES
    for step, piece in enumerate(pieces):
        target = rows_of(jnp.bitwise_xor(place_ref[2], step), rows)
        for half, out_ref in enumerate(outs):
            out_ref[target, :wide] = piece[half * rows : (half + 1) * rows, :]
    for level in range(levels):
        for half, out_ref in enumerate(outs):
            first = (level * HALVES + half) * rows
            out_ref[level * rows : (level + 1) * rows, wide:] = routing_ref[first : first + rows, :]


def group_tokens(place, routing, pieces):
    rows, wide = pieces[0].shape
    levels = len(pieces)
    return pl.pallas_call(
        functools.partial(group_kernel, levels),
        in_specs=[SMEM_SPEC, VMEM_SPEC] + [VMEM_SPEC] * levels,
        out_specs=[VMEM_SPEC] * HALVES,
        out_shape=[bf16(levels * rows // HALVES, wide + LANES)] * HALVES,
        compiler_params=PARAMS,
    )(place, routing, *pieces)


def finish_kernel(depth, levels, place_ref, *refs):
    pieces, (out_ref, held) = refs[:-2], refs[-2:]
    rows, wide = pieces[0].shape
    for index, piece in enumerate(pieces):
        half, step = index // levels, index % levels
        other = jnp.bitwise_xor(place_ref[2], step)
        held[other, half * rows : (half + 1) * rows, :] = piece[...]
    chips = wide // depth // CORES
    first, second = [], []
    for chip in range(chips):
        for side in range(CORES):
            for other in range(levels):
                for parts, place in ((first, side), (second, 1 - side)):
                    start = (place * chips + chip) * depth
                    parts.append(held[other, :, start : start + depth])
    first, second = jnp.concatenate(first, axis=1), jnp.concatenate(second, axis=1)
    out_ref[...] = jnp.where(place_ref[1] == 0, first, second)


def finish(place, pieces, levels, depth):
    rows, wide = pieces[0].shape
    rows = rows * HALVES
    return pl.pallas_call(
        functools.partial(finish_kernel, depth, levels),
        in_specs=[SMEM_SPEC] + [VMEM_SPEC] * len(pieces),
        out_specs=VMEM_SPEC,
        out_shape=bf16(rows, wide * levels),
        scratch_shapes=[pltpu.VMEM((levels, rows, wide), jnp.bfloat16)],
        compiler_params=PARAMS,
    )(place, *pieces)


def join_kernel(chips, place_ref, own_ref, *refs):
    pieces, (out_ref, sems) = refs[: chips - 1], refs[chips - 1 :]
    width = out_ref.shape[3]
    chip = place_ref[0]
    columns = pl.ds(pl.multiple_of(chip * width, width), width)
    sources = [own_ref.at[:, :, columns]] + list(pieces)
    copies = [
        pltpu.make_async_copy(source, out_ref.at[:, jnp.bitwise_xor(chip, step)], sems.at[step])
        for step, source in enumerate(sources)
    ]
    for copy in copies:
        copy.start()
    for copy in copies:
        copy.wait()


def join_blocks(place, own, pieces):
    experts, depth, units = own.shape
    chips = len(pieces) + 1
    shape = (experts, chips, depth, units // chips)
    return pl.pallas_call(
        functools.partial(join_kernel, chips),
        in_specs=[SMEM_SPEC] + [ANY_SPEC] * chips,
        out_specs=VMEM_SPEC,
        out_shape=bf16(*shape),
        scratch_shapes=[pltpu.SemaphoreType.DMA((chips,))],
        cost_estimate=cost(0, 2 * own.size),
        compiler_params=PARAMS,
    )(place, own, *pieces)


def pick_kernel(chips, place_ref, *refs):
    toks, refs = refs[:chips], refs[chips:]
    weights, (keep_ref, send_ref, routing_ref, left) = refs[:CORES], refs[CORES:]
    experts, depth, width = weights[0].shape
    rows = toks[0].shape[0]
    for step, tok in enumerate(toks):
        block = jnp.bitwise_xor(step, place_ref[2])
        left[rows_of(block, rows), :] = tok[:, : CORES * depth]
        routing_ref[block] = tok[:, CORES * depth :]
    slots = keep_ref.shape[2] // width
    tile = min(TILE, width)
    for start in range(0, width, tile):
        sums = []
        for which in range(experts):
            total = None
            for side, weight in enumerate(weights):
                term = jnp.dot(
                    left[:, side * depth : (side + 1) * depth],
                    weight[which, :, start : start + tile],
                    preferred_element_type=jnp.float32,
                )
                total = term if total is None else total + term
            sums.append(total)
        for step in range(chips):
            out_ref = (keep_ref, send_ref)[step % 2]
            ids = routing_ref[step].astype(jnp.float32)
            for slot in range(slots):
                chosen = ids[:, slot : slot + 1]
                picked = sums[0][step * rows : (step + 1) * rows]
                for which in range(1, experts):
                    other = sums[which][step * rows : (step + 1) * rows]
                    picked = jnp.where(chosen == which, other, picked)
                first = slot * width + start
                out_ref[step // 2, :, first : first + tile] = picked.astype(out_ref.dtype)


def picked_sums(place, toks, weights, slots):
    chips, rows = len(toks), toks[0].shape[0]
    experts, depth, width = weights[0].shape
    wide = CORES * depth
    count = chips * rows
    return pl.pallas_call(
        functools.partial(pick_kernel, chips),
        in_specs=[SMEM_SPEC] + [VMEM_SPEC] * (chips + CORES),
        out_specs=[VMEM_SPEC] * 3,
        out_shape=[bf16(chips // 2, rows, slots * width)] * 2 + [bf16(chips, rows, LANES)],
        scratch_shapes=[pltpu.VMEM((count, wide), jnp.bfloat16)],
        cost_estimate=cost(
            2 * count * wide * width * experts,
            count * wide + experts * wide * width + count * slots * width,
        ),
        compiler_params=PARAMS,
    )(place, *toks, *weights)


def hidden_kernel(terms, slots, routing_ref, *refs):
    gates, ups, out_ref = refs[:terms], refs[terms : 2 * terms], refs[2 * terms]
    scores = routing_ref[0].astype(jnp.float32)[:, slots : 2 * slots]
    combine = scores / jnp.sum(scores, axis=1, keepdims=True)
    width = out_ref.shape[1] // slots
    for slot in range(slots):
        columns = slice(slot * width, (slot + 1) * width)
        gate_sum = sum(ref[0, :, columns].astype(jnp.float32) for ref in gates)
        up_sum = sum(ref[0, :, columns].astype(jnp.float32) for ref in ups)
        value = gate_sum / (1.0 + jnp.exp(-gate_sum)) * up_sum * combine[:, slot : slot + 1]
        out_ref[:, columns] = value.astype(out_ref.dtype)


def hidden_rows(routing, gates, ups, slots):
    return pl.pallas_call(
        functools.partial(hidden_kernel, len(gates), slots),
        in_specs=[VMEM_SPEC] * (1 + 2 * len(gates)),
        out_specs=VMEM_SPEC,
        out_shape=bf16(*gates[0].shape[1:]),
        compiler_params=PARAMS,
    )(routing, *gates, *ups)


def down_kernel(step, slots, routing_ref, hid_ref, *refs):
    weights, (out_ref,) = refs[:CORES], refs[CORES:]
    experts, depth, width = weights[0].shape
    ids = routing_ref[step].astype(jnp.float32)
    lefts = []
    for which in range(experts):
        mine = jnp.zeros((hid_ref.shape[0], width), jnp.float32)
        for slot in range(slots):
            part = hid_ref[:, slot * width : (slot + 1) * width].astype(jnp.float32)
            mine = jnp.where(ids[:, slot : slot + 1] == which, part, mine)
        lefts.append(mine.astype(hid_ref.dtype))
    for side, weight in enumerate(weights):
        total = None
        for which in range(experts):
            term = lax.dot_general(
                lefts[which],
                weight[which],
                (((1,), (1,)), ((), ())),
                preferred_element_type=jnp.float32,
            )
            total = term if total is None else total + term
        out_ref[:, side * depth : (side + 1) * depth] = total.astype(out_ref.dtype)


def down_sums(routing, hidden, weights, step, slots):
    rows = hidden.shape[0]
    experts, depth, width = weights[0].shape
    wide = CORES * depth
    return pl.pallas_call(
        functools.partial(down_kernel, step, slots),
        in_specs=[VMEM_SPEC] * (2 + CORES),
        out_specs=VMEM_SPEC,
        out_shape=bf16(rows, wide),
        cost_estimate=cost(
            2 * rows * wide * width * experts,
            rows * slots * width + experts * wide * width + rows * wide,
        ),
        compiler_params=PARAMS,
    )(routing, hidden, *weights)


def after(values, others):
    return lax.optimization_barrier((values, others))[0]


def local(tokens, expert_ids, gate_scores, gate_weight, up_weight, down_weight):
    n_expert, n_tensor = lax.axis_size("expert"), lax.axis_size("tensor")
    chips = n_expert // CORES
    rows = tokens.shape[0]
    depth, units = gate_weight.shape[1:]
    slots = expert_ids.shape[1]
    width = units // chips
    spot, level = lax.axis_index("expert"), lax.axis_index("tensor")
    q, c = spot // CORES, spot % CORES
    place = jnp.stack([q, c, level])

    def to_chip(value, step):
        pairs = [(s, s ^ (step * CORES)) for s in range(n_expert)]
        return lax.ppermute(value, "expert", pairs)

    def to_core(value):
        return lax.ppermute(value, "expert", [(s, s ^ 1) for s in range(n_expert)])

    def to_level(value, step):
        return lax.ppermute(value, "tensor", [(s, s ^ step) for s in range(n_tensor)])

    def to_owner(value, step):
        pairs = [
            (s * n_tensor + t, (s ^ ((t ^ step) * CORES)) * n_tensor + t)
            for s in range(n_expert)
            for t in range(n_tensor)
        ]
        return lax.ppermute(value, ("expert", "tensor"), pairs)

    def copies(value, send, bits, behind=()):
        held = {0: value}
        for bit in bits:
            for step in sorted(held):
                held[step + bit] = send(after(held[step], behind), bit)
            behind = ()
        return [held[step] for step in range(len(held))]

    def level_sums(keep, send, behind):
        terms, marks, bit = [keep], [], 1
        send = after(send, behind[:1])
        while True:
            terms.append(to_level(send, bit))
            bit *= 2
            if bit == n_tensor:
                return terms, marks + [terms[-1]]
            send = sum(term[1::2].astype(jnp.float32) for term in terms).astype(jnp.bfloat16)
            terms = [term[::2] for term in terms]
            send = after(send, behind[len(marks) + 1 : len(marks) + 2])
            marks.append(send)

    def blocks_of(weight):
        return [
            lax.dynamic_slice_in_dim(weight, (q ^ step) * width, width, 2)
            for step in range(1, chips)
        ]

    def chip_exchange(blocks):
        return [to_chip(block, step) for step, block in enumerate(blocks, 1)]

    def core_exchange(joined):
        pair = [joined, to_core(joined)]
        return [side.reshape(side.shape[0], chips * depth, width) for side in pair]

    routing = jnp.concatenate([expert_ids, gate_scores], axis=1).astype(jnp.bfloat16)
    routing = jnp.pad(routing, ((0, 0), (0, LANES - 2 * slots)))
    gate_same = chip_exchange(blocks_of(gate_weight))
    cut = cut_tokens(place, tokens, n_tensor, depth)
    cut = [cut[0]] + [to_level(cut[step], step) for step in range(1, n_tensor)]
    groups = group_tokens(place, routing, cut)

    gate_joined = join_blocks(place, gate_weight, after(gate_same, groups))
    gate_pair = core_exchange(gate_joined)
    bits = [1 << bit for bit in range(chips.bit_length() - 1)]
    toks = []
    for half in range(HALVES):
        turn = (half + 1) % len(bits)
        toks.append(copies(groups[half], to_chip, bits[turn:] + bits[:turn]))
    near = [tok[bit] for tok in toks for bit in bits]
    up_same = chip_exchange(after(blocks_of(up_weight), near))

    def products(weights, before, late):
        sums, routings, parts = [], [], []
        behind = before[-1][1] if before else []
        for half in range(HALVES):
            others = [parts, behind[:1], [marks for _, marks in before[half : half + 1]]]
            others += late if half else []
            *parts, routing = picked_sums(place, after(toks[half], others), weights, slots)
            terms, behind = level_sums(*parts, behind)
            sums.append((terms, behind))
            routings.append(routing)
        return sums, routings

    gate_sums, routings = products(gate_pair, [], up_same[: chips // 2])
    up_joined = join_blocks(place, up_weight, after(up_same, gate_sums[-1][1][0]))
    up_pair = core_exchange(up_joined)
    down_same = chip_exchange(after(blocks_of(down_weight), up_joined))
    up_sums, _ = products(up_pair, gate_sums, [])
    hiddens, near, far = [], [], up_sums[-1][1][-1]
    bits = [1 << bit for bit in range(n_tensor.bit_length() - 1)]
    for half in range(HALVES):
        up_terms = after(up_sums[half][0], [up_sums[-1][1][0], near])
        hidden = hidden_rows(routings[half], gate_sums[half][0], up_terms, slots)
        hiddens.append(copies(hidden, to_level, bits[::-1], far))
        near, far = hiddens[-1][1], hiddens[-1][n_tensor // 2]
    down_joined = join_blocks(place, down_weight, after(down_same, [h[0] for h in hiddens]))
    down_pair = core_exchange(down_joined)

    backs, part = [], []
    for half in range(HALVES):
        routing, blocks = routings[half], after(hiddens[half], part)
        if half + 1 < HALVES:
            blocks[-1] = after(blocks[-1], hiddens[half + 1][n_tensor // 2])
        total = 0.0
        for step in range(n_tensor):
            part = down_sums(routing, blocks[step], down_pair, step, slots)
            total = total + to_owner(part, step).astype(jnp.float32)
        total = total.astype(jnp.bfloat16).reshape(n_tensor, rows // HALVES, -1)
        for step in range(n_tensor):
            piece = lax.dynamic_index_in_dim(total, level ^ step, 0, keepdims=False)
            backs.append(to_level(piece, step) if step else piece)
    return finish(place, backs, n_tensor, depth)


def solution(mesh):
    return jax.shard_map(
        local,
        mesh=mesh,
        in_specs=(
            P(("expert", "tensor"), None),
            P("expert", None),
            P("expert", None),
            P(None, ("expert", "tensor"), None),
            P(None, ("expert", "tensor"), None),
            P(None, ("expert", "tensor"), None),
        ),
        out_specs=P(("expert", "tensor"), None),
        check_vma=False,
    )
```

```python
import functools

import jax
import jax.numpy as jnp
from jax import lax
from jax.experimental import pallas as pl
from jax.experimental.pallas import tpu as pltpu
from jax.sharding import PartitionSpec as P

VMEM_BYTES = 22 * 1024 * 1024
CORES = 2
HALVES = 2
TILE = 256
LANES = 128

SMEM_SPEC = pl.BlockSpec(memory_space=pltpu.SMEM)
VMEM_SPEC = pl.BlockSpec(memory_space=pltpu.VMEM)
ANY_SPEC = pl.BlockSpec(memory_space=pl.ANY)
PARAMS = pltpu.CompilerParams(vmem_limit_bytes=VMEM_BYTES)


def bf16(*shape):
    return jax.ShapeDtypeStruct(shape, jnp.bfloat16)


def cost(flops, elements):
    return pl.CostEstimate(flops=flops, bytes_accessed=2 * elements, transcendentals=0)


def rows_of(block, rows):
    return pl.ds(pl.multiple_of(block * rows, rows), rows)


def cut_kernel(depth, place_ref, tokens_ref, *refs):
    outs, held = refs[:-1], refs[-1]
    levels, _, wide = held.shape
    core, level = place_ref[1], place_ref[2]
    tokens = tokens_ref[...]
    for other in range(levels):
        sides = []
        for side in range(CORES):
            blocks = range(side, wide // depth, CORES)
            starts = [(block * levels + other) * depth for block in blocks]
            sides.append(jnp.concatenate([tokens[:, s : s + depth] for s in starts], axis=1))
        swapped = jnp.concatenate(sides[::-1], axis=1)
        piece = jnp.where(core == 0, jnp.concatenate(sides, axis=1), swapped)
        held[jnp.bitwise_xor(level, other)] = piece
    for step, out_ref in enumerate(outs):
        out_ref[...] = held[step]


def cut_tokens(place, tokens, levels, depth):
    rows, model = tokens.shape
    shape = (rows, model // levels)
    return pl.pallas_call(
        functools.partial(cut_kernel, depth),
        in_specs=[SMEM_SPEC, VMEM_SPEC],
        out_specs=[VMEM_SPEC] * levels,
        out_shape=[bf16(*shape)] * levels,
        scratch_shapes=[pltpu.VMEM((levels,) + shape, jnp.bfloat16)],
        compiler_params=PARAMS,
    )(place, tokens)


def group_kernel(levels, place_ref, routing_ref, *refs):
    pieces, outs = refs[:levels], refs[levels:]
    wide = pieces[0].shape[1]
    rows = pieces[0].shape[0] // HALVES
    for step, piece in enumerate(pieces):
        target = rows_of(jnp.bitwise_xor(place_ref[2], step), rows)
        for half, out_ref in enumerate(outs):
            out_ref[target, :wide] = piece[half * rows : (half + 1) * rows, :]
    for level in range(levels):
        for half, out_ref in enumerate(outs):
            first = (level * HALVES + half) * rows
            out_ref[level * rows : (level + 1) * rows, wide:] = routing_ref[first : first + rows, :]


def group_tokens(place, routing, pieces):
    rows, wide = pieces[0].shape
    levels = len(pieces)
    return pl.pallas_call(
        functools.partial(group_kernel, levels),
        in_specs=[SMEM_SPEC, VMEM_SPEC] + [VMEM_SPEC] * levels,
        out_specs=[VMEM_SPEC] * HALVES,
        out_shape=[bf16(levels * rows // HALVES, wide + LANES)] * HALVES,
        compiler_params=PARAMS,
    )(place, routing, *pieces)


def finish_kernel(depth, levels, place_ref, *refs):
    pieces, (out_ref, held) = refs[:-2], refs[-2:]
    rows, wide = pieces[0].shape
    for index, piece in enumerate(pieces):
        half, step = index // levels, index % levels
        other = jnp.bitwise_xor(place_ref[2], step)
        held[other, half * rows : (half + 1) * rows, :] = piece[...]
    chips = wide // depth // CORES
    first, second = [], []
    for chip in range(chips):
        for side in range(CORES):
            for other in range(levels):
                for parts, place in ((first, side), (second, 1 - side)):
                    start = (place * chips + chip) * depth
                    parts.append(held[other, :, start : start + depth])
    first, second = jnp.concatenate(first, axis=1), jnp.concatenate(second, axis=1)
    out_ref[...] = jnp.where(place_ref[1] == 0, first, second)


def finish(place, pieces, levels, depth):
    rows, wide = pieces[0].shape
    rows = rows * HALVES
    return pl.pallas_call(
        functools.partial(finish_kernel, depth, levels),
        in_specs=[SMEM_SPEC] + [VMEM_SPEC] * len(pieces),
        out_specs=VMEM_SPEC,
        out_shape=bf16(rows, wide * levels),
        scratch_shapes=[pltpu.VMEM((levels, rows, wide), jnp.bfloat16)],
        compiler_params=PARAMS,
    )(place, *pieces)


def join_kernel(chips, place_ref, own_ref, *refs):
    pieces, (out_ref, sems) = refs[: chips - 1], refs[chips - 1 :]
    width = out_ref.shape[3]
    chip = place_ref[0]
    columns = pl.ds(pl.multiple_of(chip * width, width), width)
    sources = [own_ref.at[:, :, columns]] + list(pieces)
    copies = [
        pltpu.make_async_copy(source, out_ref.at[:, jnp.bitwise_xor(chip, step)], sems.at[step])
        for step, source in enumerate(sources)
    ]
    for copy in copies:
        copy.start()
    for copy in copies:
        copy.wait()


def join_blocks(place, own, pieces):
    experts, depth, units = own.shape
    chips = len(pieces) + 1
    shape = (experts, chips, depth, units // chips)
    return pl.pallas_call(
        functools.partial(join_kernel, chips),
        in_specs=[SMEM_SPEC] + [ANY_SPEC] * chips,
        out_specs=VMEM_SPEC,
        out_shape=bf16(*shape),
        scratch_shapes=[pltpu.SemaphoreType.DMA((chips,))],
        cost_estimate=cost(0, 2 * own.size),
        compiler_params=PARAMS,
    )(place, own, *pieces)


def pick_kernel(chips, place_ref, *refs):
    toks, refs = refs[: chips * HALVES], refs[chips * HALVES :]
    weights, (*outs, routing_ref, left, ids_ref) = refs[:CORES], refs[CORES:]
    experts, depth, width = weights[0].shape
    rows = toks[0].shape[0]
    for index, tok in enumerate(toks):
        chip, half = index // HALVES, index % HALVES
        routing_ref[index * rows : (index + 1) * rows, :] = tok[:, CORES * depth :]
        block = jnp.bitwise_xor(chip, place_ref[2]) if len(outs) > 1 else chip
        target = rows_of(block * HALVES + half, rows)
        left[target, :] = tok[:, : CORES * depth]
        ids_ref[target, :] = tok[:, CORES * depth :]
    rows *= HALVES
    slots = outs[0].shape[-1] // width
    tile = min(TILE, width)
    for start in range(0, width, tile):
        sums = []
        for which in range(experts):
            total = None
            for side, weight in enumerate(weights):
                term = jnp.dot(
                    left[:, side * depth : (side + 1) * depth],
                    weight[which, :, start : start + tile],
                    preferred_element_type=jnp.float32,
                )
                total = term if total is None else total + term
            sums.append(total)
        ids = ids_ref[...].astype(jnp.float32)
        for slot in range(slots):
            chosen = ids[:, slot : slot + 1]
            picked = sums[0]
            for which in range(1, experts):
                picked = jnp.where(chosen == which, sums[which], picked)
            picked = picked.astype(left.dtype)
            first = slot * width + start
            for step in range(chips):
                part = picked[step * rows : (step + 1) * rows]
                out_ref = outs[step % len(outs)]
                out_ref[step // len(outs), :, first : first + tile] = part


def picked_sums(place, toks, weights, slots, split):
    experts, depth, width = weights[0].shape
    wide, chips = CORES * depth, len(toks) // HALVES
    rows = HALVES * toks[0].shape[0]
    count = chips * rows
    return pl.pallas_call(
        functools.partial(pick_kernel, chips),
        in_specs=[SMEM_SPEC] + [VMEM_SPEC] * (len(toks) + CORES),
        out_specs=[VMEM_SPEC] * (split + 1),
        out_shape=[bf16(chips // split, rows, slots * width)] * split + [bf16(count, LANES)],
        scratch_shapes=[
            pltpu.VMEM((count, wide), jnp.bfloat16),
            pltpu.VMEM((count, LANES), jnp.bfloat16),
        ],
        cost_estimate=cost(
            2 * count * wide * width * experts,
            count * wide + experts * wide * width + count * slots * width,
        ),
        compiler_params=PARAMS,
    )(place, *toks, *weights)


def hidden_kernel(slots, place_ref, routing_ref, up_ref, *refs):
    gates, out_ref = refs[:-1], refs[-1]
    rows, wide = out_ref.shape
    scores = routing_ref[rows_of(place_ref[2], rows), :].astype(jnp.float32)
    scores = scores[:, slots : 2 * slots]
    combine = scores / jnp.sum(scores, axis=1, keepdims=True)
    width = wide // slots
    for slot in range(slots):
        columns = slice(slot * width, (slot + 1) * width)
        gate_sum = sum(ref[0, :, columns].astype(jnp.float32) for ref in gates)
        up_sum = up_ref[:, columns].astype(jnp.float32)
        value = gate_sum / (1.0 + jnp.exp(-gate_sum)) * up_sum * combine[:, slot : slot + 1]
        out_ref[:, columns] = value.astype(out_ref.dtype)


def hidden_rows(place, routing, gate_terms, up_sum, slots):
    return pl.pallas_call(
        functools.partial(hidden_kernel, slots),
        in_specs=[SMEM_SPEC] + [VMEM_SPEC] * (2 + len(gate_terms)),
        out_specs=VMEM_SPEC,
        out_shape=bf16(*up_sum.shape),
        compiler_params=PARAMS,
    )(place, routing, up_sum, *gate_terms)


def down_kernel(step, part, parts, slots, place_ref, routing_ref, hid_ref, *refs):
    weights, (out_ref,) = refs[:CORES], refs[CORES:]
    experts, depth, width = weights[0].shape
    rows = hid_ref.shape[0]
    block = jnp.bitwise_xor(place_ref[2], step) * parts + part
    ids = routing_ref[rows_of(block, rows), :].astype(jnp.float32)
    lefts = []
    for which in range(experts):
        mine = jnp.zeros((rows, width), jnp.float32)
        for slot in range(slots):
            value = hid_ref[:, slot * width : (slot + 1) * width].astype(jnp.float32)
            mine = jnp.where(ids[:, slot : slot + 1] == which, value, mine)
        lefts.append(mine.astype(hid_ref.dtype))
    for side, weight in enumerate(weights):
        total = None
        for which in range(experts):
            term = lax.dot_general(
                lefts[which],
                weight[which],
                (((1,), (1,)), ((), ())),
                preferred_element_type=jnp.float32,
            )
            total = term if total is None else total + term
        out_ref[:, side * depth : (side + 1) * depth] = total.astype(out_ref.dtype)


def down_sums(place, routing, hidden, weights, step, part, parts, slots):
    rows = hidden.shape[0]
    experts, depth, width = weights[0].shape
    wide = CORES * depth
    return pl.pallas_call(
        functools.partial(down_kernel, step, part, parts, slots),
        in_specs=[SMEM_SPEC] + [VMEM_SPEC] * (2 + CORES),
        out_specs=VMEM_SPEC,
        out_shape=bf16(rows, wide),
        cost_estimate=cost(
            2 * rows * wide * width * experts,
            rows * slots * width + experts * wide * width + rows * wide,
        ),
        compiler_params=PARAMS,
    )(place, routing, hidden, *weights)


def after(values, others):
    return lax.optimization_barrier((values, others))[0]


def local(tokens, expert_ids, gate_scores, gate_weight, up_weight, down_weight):
    n_expert, n_tensor = lax.axis_size("expert"), lax.axis_size("tensor")
    chips = n_expert // CORES
    rows = tokens.shape[0]
    depth, units = gate_weight.shape[1:]
    slots = expert_ids.shape[1]
    width = units // chips
    spot, level = lax.axis_index("expert"), lax.axis_index("tensor")
    q, c = spot // CORES, spot % CORES
    place = jnp.stack([q, c, level])

    def to_chip(value, step):
        pairs = [(s, s ^ (step * CORES)) for s in range(n_expert)]
        return lax.ppermute(value, "expert", pairs)

    def to_core(value):
        return lax.ppermute(value, "expert", [(s, s ^ 1) for s in range(n_expert)])

    def to_level(value, step):
        return lax.ppermute(value, "tensor", [(s, s ^ step) for s in range(n_tensor)])

    def to_owner(value, step):
        pairs = [
            (s * n_tensor + t, (s ^ ((t ^ step) * CORES)) * n_tensor + t)
            for s in range(n_expert)
            for t in range(n_tensor)
        ]
        return lax.ppermute(value, ("expert", "tensor"), pairs)

    def copies(value, send, bits):
        held = {0: value}
        for bit in bits:
            for step in sorted(held):
                held[step + bit] = send(held[step], bit)
        return [held[step] for step in range(len(held))]

    def blocks_of(weight):
        return [
            lax.dynamic_slice_in_dim(weight, (q ^ step) * width, width, 2)
            for step in range(1, chips)
        ]

    def chip_exchange(blocks):
        return [to_chip(block, step) for step, block in enumerate(blocks, 1)]

    def core_exchange(joined):
        pair = [joined, to_core(joined)]
        return [side.reshape(side.shape[0], chips * depth, width) for side in pair]

    routing = jnp.concatenate([expert_ids, gate_scores], axis=1).astype(jnp.bfloat16)
    routing = jnp.pad(routing, ((0, 0), (0, LANES - 2 * slots)))
    gate_same = chip_exchange(blocks_of(gate_weight))
    cut = cut_tokens(place, tokens, n_tensor, depth)
    cut = [cut[0]] + [to_level(cut[step], step) for step in range(1, n_tensor)]
    groups = group_tokens(place, routing, cut)

    gate_joined = join_blocks(place, gate_weight, after(gate_same, groups))
    gate_pair = core_exchange(gate_joined)
    groups = after(groups, gate_joined)
    bits = [1 << bit for bit in range(chips.bit_length() - 1)]
    toks = []
    for half in range(HALVES):
        turn = (half + 1) % len(bits)
        toks.append(copies(groups[half], to_chip, bits[turn:] + bits[:turn]))

    left = [toks[half][step] for step in range(chips) for half in range(HALVES)]
    up_same = chip_exchange(after(blocks_of(up_weight), toks))
    keep, send, routing = picked_sums(place, left, gate_pair, slots, 2)
    gate_terms, bit = [keep], 1
    while True:
        gate_terms.append(to_level(send, bit))
        bit *= 2
        if bit == n_tensor:
            break
        send = sum(term[1::2].astype(jnp.float32) for term in gate_terms).astype(jnp.bfloat16)
        gate_terms = [term[::2] for term in gate_terms]
    up_joined = join_blocks(place, up_weight, after(up_same, send))
    up_pair = core_exchange(up_joined)
    down_same = chip_exchange(after(blocks_of(down_weight), up_joined))
    left = after(left, gate_terms[-1])
    part, _ = picked_sums(place, left, up_pair, slots, 1)
    part = part.reshape(-1, part.shape[2])
    up_sum = lax.psum_scatter(part, "tensor", scatter_dimension=0, tiled=True)
    down_joined = join_blocks(place, down_weight, after(down_same, up_sum))
    down_pair = core_exchange(down_joined)
    hidden = hidden_rows(place, routing, gate_terms, up_sum, slots)

    count = hidden.shape[0] // HALVES
    blocks, bit = {0: hidden}, n_tensor // 2
    while bit:
        for step in sorted(blocks):
            if step + bit < n_tensor - 1:
                blocks[step + bit] = to_level(blocks[step], bit)
        bit //= 2
    last = [blocks[n_tensor - 2][half * count : (half + 1) * count] for half in range(HALVES)]
    last = [to_level(value, 1) for value in last]
    blocks[n_tensor - 2] = after(blocks[n_tensor - 2], last[0])
    terms, part = [[] for _ in range(HALVES)], []
    for step in range(n_tensor - 1):
        block = after(blocks[step], part)
        part = down_sums(place, routing, block, down_pair, step, 0, 1, slots)
        term = to_owner(part, step)
        for half in range(HALVES):
            terms[half].append(term[half * count : (half + 1) * count])
    backs, step, total = [], n_tensor - 1, []
    for half in range(HALVES):
        block = after(last[half], part)
        part = down_sums(place, routing, block, down_pair, step, half, HALVES, slots)
        terms[half].append(to_owner(part, step))
        total = sum(term.astype(jnp.float32) for term in after(terms[half], total))
        total = total.astype(jnp.bfloat16).reshape(n_tensor, rows // HALVES, -1)
        for other in range(n_tensor):
            piece = lax.dynamic_index_in_dim(total, level ^ other, 0, keepdims=False)
            backs.append(to_level(piece, other) if other else piece)
    return finish(place, backs, n_tensor, depth)


def solution(mesh):
    return jax.shard_map(
        local,
        mesh=mesh,
        in_specs=(
            P(("expert", "tensor"), None),
            P("expert", None),
            P("expert", None),
            P(None, ("expert", "tensor"), None),
            P(None, ("expert", "tensor"), None),
            P(None, ("expert", "tensor"), None),
        ),
        out_specs=P(("expert", "tensor"), None),
        check_vma=False,
    )
```

```python
import functools

import jax
import jax.numpy as jnp
from jax import lax
from jax.experimental import pallas as pl
from jax.experimental.pallas import tpu as pltpu
from jax.sharding import PartitionSpec as P

VMEM_BYTES = 22 * 1024 * 1024
CORES = 2
HALVES = 2
TILE = 256
LANES = 128

SMEM_SPEC = pl.BlockSpec(memory_space=pltpu.SMEM)
VMEM_SPEC = pl.BlockSpec(memory_space=pltpu.VMEM)
ANY_SPEC = pl.BlockSpec(memory_space=pl.ANY)
PARAMS = pltpu.CompilerParams(vmem_limit_bytes=VMEM_BYTES)


def bf16(*shape):
    return jax.ShapeDtypeStruct(shape, jnp.bfloat16)


def cost(flops, elements):
    return pl.CostEstimate(flops=flops, bytes_accessed=2 * elements, transcendentals=0)


def rows_of(block, rows):
    return pl.ds(pl.multiple_of(block * rows, rows), rows)


def cut_kernel(depth, place_ref, tokens_ref, *refs):
    outs, held = refs[:-1], refs[-1]
    levels, _, wide = held.shape
    core, level = place_ref[1], place_ref[2]
    tokens = tokens_ref[...]
    for other in range(levels):
        sides = []
        for side in range(CORES):
            blocks = range(side, wide // depth, CORES)
            starts = [(block * levels + other) * depth for block in blocks]
            sides.append(jnp.concatenate([tokens[:, s : s + depth] for s in starts], axis=1))
        swapped = jnp.concatenate(sides[::-1], axis=1)
        piece = jnp.where(core == 0, jnp.concatenate(sides, axis=1), swapped)
        held[jnp.bitwise_xor(level, other)] = piece
    for step, out_ref in enumerate(outs):
        out_ref[...] = held[step]


def cut_tokens(place, tokens, levels, depth):
    rows, model = tokens.shape
    shape = (rows, model // levels)
    return pl.pallas_call(
        functools.partial(cut_kernel, depth),
        in_specs=[SMEM_SPEC, VMEM_SPEC],
        out_specs=[VMEM_SPEC] * levels,
        out_shape=[bf16(*shape)] * levels,
        scratch_shapes=[pltpu.VMEM((levels,) + shape, jnp.bfloat16)],
        compiler_params=PARAMS,
    )(place, tokens)


def group_kernel(levels, place_ref, routing_ref, *refs):
    pieces, outs = refs[:levels], refs[levels:]
    wide = pieces[0].shape[1]
    rows = pieces[0].shape[0] // HALVES
    for step, piece in enumerate(pieces):
        target = rows_of(jnp.bitwise_xor(place_ref[2], step), rows)
        for half, out_ref in enumerate(outs):
            out_ref[target, :wide] = piece[half * rows : (half + 1) * rows, :]
    for level in range(levels):
        for half, out_ref in enumerate(outs):
            first = (level * HALVES + half) * rows
            out_ref[level * rows : (level + 1) * rows, wide:] = routing_ref[first : first + rows, :]


def group_tokens(place, routing, pieces):
    rows, wide = pieces[0].shape
    levels = len(pieces)
    return pl.pallas_call(
        functools.partial(group_kernel, levels),
        in_specs=[SMEM_SPEC, VMEM_SPEC] + [VMEM_SPEC] * levels,
        out_specs=[VMEM_SPEC] * HALVES,
        out_shape=[bf16(levels * rows // HALVES, wide + LANES)] * HALVES,
        compiler_params=PARAMS,
    )(place, routing, *pieces)


def finish_kernel(depth, levels, place_ref, *refs):
    pieces, (out_ref, held) = refs[:-2], refs[-2:]
    rows, wide = pieces[0].shape
    for index, piece in enumerate(pieces):
        half, step = index // levels, index % levels
        other = jnp.bitwise_xor(place_ref[2], step)
        held[other, half * rows : (half + 1) * rows, :] = piece[...]
    chips = wide // depth // CORES
    first, second = [], []
    for chip in range(chips):
        for side in range(CORES):
            for other in range(levels):
                for parts, place in ((first, side), (second, 1 - side)):
                    start = (place * chips + chip) * depth
                    parts.append(held[other, :, start : start + depth])
    first, second = jnp.concatenate(first, axis=1), jnp.concatenate(second, axis=1)
    out_ref[...] = jnp.where(place_ref[1] == 0, first, second)


def finish(place, pieces, levels, depth):
    rows, wide = pieces[0].shape
    rows = rows * HALVES
    return pl.pallas_call(
        functools.partial(finish_kernel, depth, levels),
        in_specs=[SMEM_SPEC] + [VMEM_SPEC] * len(pieces),
        out_specs=VMEM_SPEC,
        out_shape=bf16(rows, wide * levels),
        scratch_shapes=[pltpu.VMEM((levels, rows, wide), jnp.bfloat16)],
        compiler_params=PARAMS,
    )(place, *pieces)


def join_kernel(chips, place_ref, own_ref, *refs):
    pieces, (out_ref, sems) = refs[: chips - 1], refs[chips - 1 :]
    width = out_ref.shape[3]
    chip = place_ref[0]
    columns = pl.ds(pl.multiple_of(chip * width, width), width)
    sources = [own_ref.at[:, :, columns]] + list(pieces)
    copies = [
        pltpu.make_async_copy(source, out_ref.at[:, jnp.bitwise_xor(chip, step)], sems.at[step])
        for step, source in enumerate(sources)
    ]
    for copy in copies:
        copy.start()
    for copy in copies:
        copy.wait()


def join_blocks(place, own, pieces):
    experts, depth, units = own.shape
    chips = len(pieces) + 1
    shape = (experts, chips, depth, units // chips)
    return pl.pallas_call(
        functools.partial(join_kernel, chips),
        in_specs=[SMEM_SPEC] + [ANY_SPEC] * chips,
        out_specs=VMEM_SPEC,
        out_shape=bf16(*shape),
        scratch_shapes=[pltpu.SemaphoreType.DMA((chips,))],
        cost_estimate=cost(0, 2 * own.size),
        compiler_params=PARAMS,
    )(place, own, *pieces)


def pick_kernel(tokens, *refs):
    toks, refs = refs[:tokens], refs[tokens:]
    weights, (out_ref, routing_ref, left) = refs[:CORES], refs[CORES:]
    experts, depth, width = weights[0].shape
    rows = toks[0].shape[0]
    for step, tok in enumerate(toks):
        left[step * rows : (step + 1) * rows, :] = tok[:, : CORES * depth]
        routing_ref[step * rows : (step + 1) * rows, :] = tok[:, CORES * depth :]
    slots = out_ref.shape[1] // width
    tile = min(TILE, width)
    for start in range(0, width, tile):
        sums = []
        for which in range(experts):
            total = None
            for side, weight in enumerate(weights):
                term = jnp.dot(
                    left[:, side * depth : (side + 1) * depth],
                    weight[which, :, start : start + tile],
                    preferred_element_type=jnp.float32,
                )
                total = term if total is None else total + term
            sums.append(total)
        ids = routing_ref[...].astype(jnp.float32)
        for slot in range(slots):
            chosen = ids[:, slot : slot + 1]
            picked = sums[0]
            for which in range(1, experts):
                picked = jnp.where(chosen == which, sums[which], picked)
            first = slot * width + start
            out_ref[:, first : first + tile] = picked.astype(out_ref.dtype)


def picked_sums(toks, weights, slots):
    experts, depth, width = weights[0].shape
    wide = CORES * depth
    count = len(toks) * toks[0].shape[0]
    return pl.pallas_call(
        functools.partial(pick_kernel, len(toks)),
        in_specs=[VMEM_SPEC] * (len(toks) + CORES),
        out_specs=[VMEM_SPEC] * 2,
        out_shape=[bf16(count, slots * width), bf16(count, LANES)],
        scratch_shapes=[pltpu.VMEM((count, wide), jnp.bfloat16)],
        cost_estimate=cost(
            2 * count * wide * width * experts,
            count * wide + experts * wide * width + count * slots * width,
        ),
        compiler_params=PARAMS,
    )(*toks, *weights)


def hidden_kernel(slots, place_ref, routing_ref, gate_ref, up_ref, *outs):
    rows, wide = outs[0].shape
    width = wide // slots
    for half, out_ref in enumerate(outs):
        target = slice(half * rows, (half + 1) * rows)
        scores = routing_ref[rows_of(place_ref[2] * HALVES + half, rows), :]
        scores = scores.astype(jnp.float32)[:, slots : 2 * slots]
        combine = scores / jnp.sum(scores, axis=1, keepdims=True)
        for slot in range(slots):
            columns = slice(slot * width, (slot + 1) * width)
            gate_sum = gate_ref[target, columns].astype(jnp.float32)
            up_sum = up_ref[target, columns].astype(jnp.float32)
            value = gate_sum / (1.0 + jnp.exp(-gate_sum)) * up_sum * combine[:, slot : slot + 1]
            out_ref[:, columns] = value.astype(out_ref.dtype)


def hidden_rows(place, routing, gate_sum, up_sum, slots):
    rows, wide = gate_sum.shape
    return pl.pallas_call(
        functools.partial(hidden_kernel, slots),
        in_specs=[SMEM_SPEC] + [VMEM_SPEC] * 3,
        out_specs=[VMEM_SPEC] * HALVES,
        out_shape=[bf16(rows // HALVES, wide)] * HALVES,
        compiler_params=PARAMS,
    )(place, routing, gate_sum, up_sum)


def down_kernel(half, slots, levels, place_ref, routing_ref, *refs):
    hids, refs = refs[:levels], refs[levels:]
    weights, (*outs, left) = refs[:CORES], refs[CORES:]
    experts, depth, width = weights[0].shape
    rows = hids[0].shape[0]
    for step, hid_ref in enumerate(hids):
        block = jnp.bitwise_xor(place_ref[2], step)
        ids = routing_ref[rows_of(block * HALVES + half, rows), :].astype(jnp.float32)
        for which in range(experts):
            mine = jnp.zeros((rows, width), jnp.float32)
            for slot in range(slots):
                value = hid_ref[:, slot * width : (slot + 1) * width].astype(jnp.float32)
                mine = jnp.where(ids[:, slot : slot + 1] == which, value, mine)
            left[which, rows_of(block, rows), :] = mine.astype(left.dtype)
    for side, weight in enumerate(weights):
        total = None
        for which in range(experts):
            term = lax.dot_general(
                left[which],
                weight[which],
                (((1,), (1,)), ((), ())),
                preferred_element_type=jnp.float32,
            )
            total = term if total is None else total + term
        for step, out_ref in enumerate(outs):
            part = total[step * rows : (step + 1) * rows]
            out_ref[:, side * depth : (side + 1) * depth] = part.astype(out_ref.dtype)


def down_sums(place, routing, hids, weights, half, slots):
    rows, levels = hids[0].shape[0], len(hids)
    experts, depth, width = weights[0].shape
    wide, count = CORES * depth, levels * rows
    return pl.pallas_call(
        functools.partial(down_kernel, half, slots, levels),
        in_specs=[SMEM_SPEC] + [VMEM_SPEC] * (1 + levels + CORES),
        out_specs=[VMEM_SPEC] * levels,
        out_shape=[bf16(rows, wide)] * levels,
        scratch_shapes=[pltpu.VMEM((experts, count, width), jnp.bfloat16)],
        cost_estimate=cost(
            2 * count * wide * width * experts,
            count * slots * width + experts * wide * width + count * wide,
        ),
        compiler_params=PARAMS,
    )(place, routing, *hids, *weights)


def after(values, others):
    return lax.optimization_barrier((values, others))[0]


def local(tokens, expert_ids, gate_scores, gate_weight, up_weight, down_weight):
    n_expert, n_tensor = lax.axis_size("expert"), lax.axis_size("tensor")
    chips = n_expert // CORES
    rows = tokens.shape[0]
    depth, units = gate_weight.shape[1:]
    slots = expert_ids.shape[1]
    width = units // chips
    spot, level = lax.axis_index("expert"), lax.axis_index("tensor")
    q, c = spot // CORES, spot % CORES
    place = jnp.stack([q, c, level])

    def to_chip(value, step):
        pairs = [(s, s ^ (step * CORES)) for s in range(n_expert)]
        return lax.ppermute(value, "expert", pairs)

    def to_core(value):
        return lax.ppermute(value, "expert", [(s, s ^ 1) for s in range(n_expert)])

    def to_level(value, step):
        return lax.ppermute(value, "tensor", [(s, s ^ step) for s in range(n_tensor)])

    def copies(value, send, bits, behind=()):
        held = {0: value}
        for bit in bits:
            for step in sorted(held):
                held[step + bit] = send(after(held[step], behind), bit)
            behind = ()
        return [held[step] for step in range(len(held))]

    def blocks_of(weight):
        return [
            lax.dynamic_slice_in_dim(weight, (q ^ step) * width, width, 2)
            for step in range(1, chips)
        ]

    def chip_exchange(blocks):
        return [to_chip(block, step) for step, block in enumerate(blocks, 1)]

    def core_exchange(joined):
        pair = [joined, to_core(joined)]
        return [side.reshape(side.shape[0], chips * depth, width) for side in pair]

    routing = jnp.concatenate([expert_ids, gate_scores], axis=1).astype(jnp.bfloat16)
    routing = jnp.pad(routing, ((0, 0), (0, LANES - 2 * slots)))
    gate_same = chip_exchange(blocks_of(gate_weight))
    cut = cut_tokens(place, tokens, n_tensor, depth)
    cut = [cut[0]] + [to_level(cut[step], step) for step in range(1, n_tensor)]
    groups = group_tokens(place, routing, cut)

    gate_joined = join_blocks(place, gate_weight, after(gate_same, groups))
    gate_pair = core_exchange(gate_joined)
    groups = after(groups, gate_joined)
    bits = [1 << bit for bit in range(chips.bit_length() - 1)]
    toks = []
    for half in range(HALVES):
        turn = (half + 1) % len(bits)
        toks.append(copies(groups[half], to_chip, bits[turn:] + bits[:turn]))

    def reduced(part):
        return lax.psum_scatter(part, "tensor", scatter_dimension=0, tiled=True)

    left = [toks[half][step] for step in range(chips) for half in range(HALVES)]
    up_same = chip_exchange(after(blocks_of(up_weight), toks))
    part, routing = picked_sums(left, gate_pair, slots)
    gate_sum = reduced(part)
    up_joined = join_blocks(place, up_weight, after(up_same, gate_sum))
    up_pair = core_exchange(up_joined)
    down_same = chip_exchange(after(blocks_of(down_weight), up_joined))
    part, _ = picked_sums(left, up_pair, slots)
    up_sum = reduced(part)
    hidden = hidden_rows(place, routing, gate_sum, up_sum, slots)
    down_joined = join_blocks(place, down_weight, after(down_same, hidden))
    down_pair = core_exchange(down_joined)

    backs, far = [], ()
    bits = [1 << bit for bit in range(n_tensor.bit_length() - 1)]
    for half in range(HALVES):
        hids = copies(hidden[half], to_level, bits[::-1], far)
        far = [hids[bit] for bit in bits]
        parts = down_sums(place, routing, hids, down_pair, half, slots)
        total = parts[0].astype(jnp.float32)
        for step in range(1, chips):
            total = total + to_chip(parts[step], step).astype(jnp.float32)
        total = total.astype(jnp.bfloat16).reshape(n_tensor, rows // HALVES, -1)
        for other in range(n_tensor):
            piece = lax.dynamic_index_in_dim(total, level ^ other, 0, keepdims=False)
            backs.append(to_level(piece, other) if other else piece)
    return finish(place, backs, n_tensor, depth)


def solution(mesh):
    return jax.shard_map(
        local,
        mesh=mesh,
        in_specs=(
            P(("expert", "tensor"), None),
            P("expert", None),
            P("expert", None),
            P(None, ("expert", "tensor"), None),
            P(None, ("expert", "tensor"), None),
            P(None, ("expert", "tensor"), None),
        ),
        out_specs=P(("expert", "tensor"), None),
        check_vma=False,
    )
```

```python
import functools

import jax
import jax.numpy as jnp
from jax import lax
from jax.experimental import pallas as pl
from jax.experimental.pallas import tpu as pltpu
from jax.sharding import PartitionSpec as P

VMEM_BYTES = 22 * 1024 * 1024
CORES = 2
HALVES = 2
TILE = 256
LANES = 128

SMEM_SPEC = pl.BlockSpec(memory_space=pltpu.SMEM)
VMEM_SPEC = pl.BlockSpec(memory_space=pltpu.VMEM)
ANY_SPEC = pl.BlockSpec(memory_space=pl.ANY)
PARAMS = pltpu.CompilerParams(vmem_limit_bytes=VMEM_BYTES)


def bf16(*shape):
    return jax.ShapeDtypeStruct(shape, jnp.bfloat16)


def cost(flops, elements):
    return pl.CostEstimate(flops=flops, bytes_accessed=2 * elements, transcendentals=0)


def rows_of(block, rows):
    return pl.ds(pl.multiple_of(block * rows, rows), rows)


def cut_kernel(depth, place_ref, tokens_ref, *refs):
    outs, held = refs[:-1], refs[-1]
    levels, _, wide = held.shape
    core, level = place_ref[1], place_ref[2]
    tokens = tokens_ref[...]
    for other in range(levels):
        sides = []
        for side in range(CORES):
            blocks = range(side, wide // depth, CORES)
            starts = [(block * levels + other) * depth for block in blocks]
            sides.append(jnp.concatenate([tokens[:, s : s + depth] for s in starts], axis=1))
        swapped = jnp.concatenate(sides[::-1], axis=1)
        piece = jnp.where(core == 0, jnp.concatenate(sides, axis=1), swapped)
        held[jnp.bitwise_xor(level, other)] = piece
    for step, out_ref in enumerate(outs):
        out_ref[...] = held[step]


def cut_tokens(place, tokens, levels, depth):
    rows, model = tokens.shape
    shape = (rows, model // levels)
    return pl.pallas_call(
        functools.partial(cut_kernel, depth),
        in_specs=[SMEM_SPEC, VMEM_SPEC],
        out_specs=[VMEM_SPEC] * levels,
        out_shape=[bf16(*shape)] * levels,
        scratch_shapes=[pltpu.VMEM((levels,) + shape, jnp.bfloat16)],
        compiler_params=PARAMS,
    )(place, tokens)


def group_kernel(levels, place_ref, routing_ref, *refs):
    pieces, outs = refs[:levels], refs[levels:]
    wide = pieces[0].shape[1]
    rows = pieces[0].shape[0] // HALVES
    for step, piece in enumerate(pieces):
        target = rows_of(jnp.bitwise_xor(place_ref[2], step), rows)
        for half, out_ref in enumerate(outs):
            out_ref[target, :wide] = piece[half * rows : (half + 1) * rows, :]
    for level in range(levels):
        for half, out_ref in enumerate(outs):
            first = (level * HALVES + half) * rows
            out_ref[level * rows : (level + 1) * rows, wide:] = routing_ref[first : first + rows, :]


def group_tokens(place, routing, pieces):
    rows, wide = pieces[0].shape
    levels = len(pieces)
    return pl.pallas_call(
        functools.partial(group_kernel, levels),
        in_specs=[SMEM_SPEC, VMEM_SPEC] + [VMEM_SPEC] * levels,
        out_specs=[VMEM_SPEC] * HALVES,
        out_shape=[bf16(levels * rows // HALVES, wide + LANES)] * HALVES,
        compiler_params=PARAMS,
    )(place, routing, *pieces)


def finish_kernel(depth, levels, place_ref, *refs):
    pieces, (out_ref, held) = refs[:-2], refs[-2:]
    rows, wide = pieces[0].shape
    for index, piece in enumerate(pieces):
        half, step = index // levels, index % levels
        other = jnp.bitwise_xor(place_ref[2], step)
        held[other, half * rows : (half + 1) * rows, :] = piece[...]
    chips = wide // depth // CORES
    first, second = [], []
    for chip in range(chips):
        for side in range(CORES):
            for other in range(levels):
                for parts, place in ((first, side), (second, 1 - side)):
                    start = (place * chips + chip) * depth
                    parts.append(held[other, :, start : start + depth])
    first, second = jnp.concatenate(first, axis=1), jnp.concatenate(second, axis=1)
    out_ref[...] = jnp.where(place_ref[1] == 0, first, second)


def finish(place, pieces, levels, depth):
    rows, wide = pieces[0].shape
    rows = rows * HALVES
    return pl.pallas_call(
        functools.partial(finish_kernel, depth, levels),
        in_specs=[SMEM_SPEC] + [VMEM_SPEC] * len(pieces),
        out_specs=VMEM_SPEC,
        out_shape=bf16(rows, wide * levels),
        scratch_shapes=[pltpu.VMEM((levels, rows, wide), jnp.bfloat16)],
        compiler_params=PARAMS,
    )(place, *pieces)


def join_kernel(chips, place_ref, own_ref, *refs):
    pieces, (out_ref, sems) = refs[: chips - 1], refs[chips - 1 :]
    width = out_ref.shape[3]
    chip = place_ref[0]
    columns = pl.ds(pl.multiple_of(chip * width, width), width)
    sources = [own_ref.at[:, :, columns]] + list(pieces)
    copies = [
        pltpu.make_async_copy(source, out_ref.at[:, jnp.bitwise_xor(chip, step)], sems.at[step])
        for step, source in enumerate(sources)
    ]
    for copy in copies:
        copy.start()
    for copy in copies:
        copy.wait()


def join_blocks(place, own, pieces):
    experts, depth, units = own.shape
    chips = len(pieces) + 1
    shape = (experts, chips, depth, units // chips)
    return pl.pallas_call(
        functools.partial(join_kernel, chips),
        in_specs=[SMEM_SPEC] + [ANY_SPEC] * chips,
        out_specs=VMEM_SPEC,
        out_shape=bf16(*shape),
        scratch_shapes=[pltpu.SemaphoreType.DMA((chips,))],
        cost_estimate=cost(0, 2 * own.size),
        compiler_params=PARAMS,
    )(place, own, *pieces)


def pick_kernel(chips, place_ref, *refs):
    toks, refs = refs[:chips], refs[chips:]
    weights, (keep_ref, send_ref, routing_ref, left) = refs[:CORES], refs[CORES:]
    experts, depth, width = weights[0].shape
    rows = toks[0].shape[0]
    for step, tok in enumerate(toks):
        block = jnp.bitwise_xor(step, place_ref[2])
        left[rows_of(block, rows), :] = tok[:, : CORES * depth]
        routing_ref[block] = tok[:, CORES * depth :]
    slots = keep_ref.shape[2] // width
    tile = min(TILE, width)
    for start in range(0, width, tile):
        sums = []
        for which in range(experts):
            total = None
            for side, weight in enumerate(weights):
                term = jnp.dot(
                    left[:, side * depth : (side + 1) * depth],
                    weight[which, :, start : start + tile],
                    preferred_element_type=jnp.float32,
                )
                total = term if total is None else total + term
            sums.append(total)
        for step in range(chips):
            out_ref = (keep_ref, send_ref)[step % 2]
            ids = routing_ref[step].astype(jnp.float32)
            for slot in range(slots):
                chosen = ids[:, slot : slot + 1]
                picked = sums[0][step * rows : (step + 1) * rows]
                for which in range(1, experts):
                    other = sums[which][step * rows : (step + 1) * rows]
                    picked = jnp.where(chosen == which, other, picked)
                first = slot * width + start
                out_ref[step // 2, :, first : first + tile] = picked.astype(out_ref.dtype)


def picked_sums(place, toks, weights, slots):
    chips, rows = len(toks), toks[0].shape[0]
    experts, depth, width = weights[0].shape
    wide = CORES * depth
    count = chips * rows
    return pl.pallas_call(
        functools.partial(pick_kernel, chips),
        in_specs=[SMEM_SPEC] + [VMEM_SPEC] * (chips + CORES),
        out_specs=[VMEM_SPEC] * 3,
        out_shape=[bf16(chips // 2, rows, slots * width)] * 2 + [bf16(chips, rows, LANES)],
        scratch_shapes=[pltpu.VMEM((count, wide), jnp.bfloat16)],
        cost_estimate=cost(
            2 * count * wide * width * experts,
            count * wide + experts * wide * width + count * slots * width,
        ),
        compiler_params=PARAMS,
    )(place, *toks, *weights)


def hidden_kernel(terms, slots, routing_ref, *refs):
    gates, ups, out_ref = refs[:terms], refs[terms : 2 * terms], refs[2 * terms]
    scores = routing_ref[0].astype(jnp.float32)[:, slots : 2 * slots]
    combine = scores / jnp.sum(scores, axis=1, keepdims=True)
    width = out_ref.shape[1] // slots
    for slot in range(slots):
        columns = slice(slot * width, (slot + 1) * width)
        gate_sum = sum(ref[0, :, columns].astype(jnp.float32) for ref in gates)
        up_sum = sum(ref[0, :, columns].astype(jnp.float32) for ref in ups)
        value = gate_sum / (1.0 + jnp.exp(-gate_sum)) * up_sum * combine[:, slot : slot + 1]
        out_ref[:, columns] = value.astype(out_ref.dtype)


def hidden_rows(routing, gates, ups, slots):
    return pl.pallas_call(
        functools.partial(hidden_kernel, len(gates), slots),
        in_specs=[VMEM_SPEC] * (1 + 2 * len(gates)),
        out_specs=VMEM_SPEC,
        out_shape=bf16(*gates[0].shape[1:]),
        compiler_params=PARAMS,
    )(routing, *gates, *ups)


def down_kernel(slots, levels, place_ref, routing_ref, *refs):
    hids, refs = refs[:levels], refs[levels:]
    weights, (*outs, left) = refs[:CORES], refs[CORES:]
    experts, depth, width = weights[0].shape
    rows = hids[0].shape[0]
    for step, hid_ref in enumerate(hids):
        block = jnp.bitwise_xor(place_ref[2], step)
        ids = routing_ref[step].astype(jnp.float32)
        for which in range(experts):
            mine = jnp.zeros((rows, width), jnp.float32)
            for slot in range(slots):
                value = hid_ref[:, slot * width : (slot + 1) * width].astype(jnp.float32)
                mine = jnp.where(ids[:, slot : slot + 1] == which, value, mine)
            left[which, rows_of(block, rows), :] = mine.astype(left.dtype)
    for side, weight in enumerate(weights):
        total = None
        for which in range(experts):
            term = lax.dot_general(
                left[which],
                weight[which],
                (((1,), (1,)), ((), ())),
                preferred_element_type=jnp.float32,
            )
            total = term if total is None else total + term
        for step, out_ref in enumerate(outs):
            part = total[step * rows : (step + 1) * rows]
            out_ref[:, side * depth : (side + 1) * depth] = part.astype(out_ref.dtype)


def down_sums(place, routing, hids, weights, slots):
    rows, levels = hids[0].shape[0], len(hids)
    experts, depth, width = weights[0].shape
    wide, count = CORES * depth, levels * rows
    return pl.pallas_call(
        functools.partial(down_kernel, slots, levels),
        in_specs=[SMEM_SPEC] + [VMEM_SPEC] * (1 + levels + CORES),
        out_specs=[VMEM_SPEC] * levels,
        out_shape=[bf16(rows, wide)] * levels,
        scratch_shapes=[pltpu.VMEM((experts, count, width), jnp.bfloat16)],
        cost_estimate=cost(
            2 * count * wide * width * experts,
            count * slots * width + experts * wide * width + count * wide,
        ),
        compiler_params=PARAMS,
    )(place, routing, *hids, *weights)


def after(values, others):
    return lax.optimization_barrier((values, others))[0]


def local(tokens, expert_ids, gate_scores, gate_weight, up_weight, down_weight):
    n_expert, n_tensor = lax.axis_size("expert"), lax.axis_size("tensor")
    chips = n_expert // CORES
    rows = tokens.shape[0]
    depth, units = gate_weight.shape[1:]
    slots = expert_ids.shape[1]
    width = units // chips
    spot, level = lax.axis_index("expert"), lax.axis_index("tensor")
    q, c = spot // CORES, spot % CORES
    place = jnp.stack([q, c, level])

    def to_chip(value, step):
        pairs = [(s, s ^ (step * CORES)) for s in range(n_expert)]
        return lax.ppermute(value, "expert", pairs)

    def to_core(value):
        return lax.ppermute(value, "expert", [(s, s ^ 1) for s in range(n_expert)])

    def to_level(value, step):
        return lax.ppermute(value, "tensor", [(s, s ^ step) for s in range(n_tensor)])

    def copies(value, send, bits, behind=()):
        held = {0: value}
        for bit in bits:
            for step in sorted(held):
                held[step + bit] = send(after(held[step], behind), bit)
            behind = ()
        return [held[step] for step in range(len(held))]

    def level_sums(keep, send, behind):
        terms, marks, bit = [keep], [], 1
        send = after(send, behind[:1])
        while True:
            terms.append(to_level(send, bit))
            bit *= 2
            if bit == n_tensor:
                return terms, marks + [terms[-1]]
            send = sum(term[1::2].astype(jnp.float32) for term in terms).astype(jnp.bfloat16)
            terms = [term[::2] for term in terms]
            send = after(send, behind[len(marks) + 1 : len(marks) + 2])
            marks.append(send)

    def blocks_of(weight):
        return [
            lax.dynamic_slice_in_dim(weight, (q ^ step) * width, width, 2)
            for step in range(1, chips)
        ]

    def chip_exchange(blocks):
        return [to_chip(block, step) for step, block in enumerate(blocks, 1)]

    def core_exchange(joined):
        pair = [joined, to_core(joined)]
        return [side.reshape(side.shape[0], chips * depth, width) for side in pair]

    routing = jnp.concatenate([expert_ids, gate_scores], axis=1).astype(jnp.bfloat16)
    routing = jnp.pad(routing, ((0, 0), (0, LANES - 2 * slots)))
    gate_same = chip_exchange(blocks_of(gate_weight))
    cut = cut_tokens(place, tokens, n_tensor, depth)
    cut = [cut[0]] + [to_level(cut[step], step) for step in range(1, n_tensor)]
    groups = group_tokens(place, routing, cut)

    gate_joined = join_blocks(place, gate_weight, after(gate_same, groups))
    gate_pair = core_exchange(gate_joined)
    bits = [1 << bit for bit in range(chips.bit_length() - 1)]
    toks = []
    for half in range(HALVES):
        turn = (half + 1) % len(bits)
        toks.append(copies(groups[half], to_chip, bits[turn:] + bits[:turn]))
    up_blocks = blocks_of(up_weight)
    toks = after(toks, up_blocks)
    up_same = chip_exchange(after(up_blocks, toks))

    def products(weights, behind, parts):
        sums, routings = [], []
        for half in range(HALVES):
            left = after(toks[half], parts)
            *parts, routing = picked_sums(place, left, weights, slots)
            terms, behind = level_sums(*parts, behind)
            sums.append((terms, behind))
            routings.append(routing)
        return sums, routings

    gate_sums, routings = products(gate_pair, [], [])
    up_joined = join_blocks(place, up_weight, after(up_same, gate_sums[-1][1][0]))
    up_pair = core_exchange(up_joined)
    down_same = chip_exchange(after(blocks_of(down_weight), up_joined))
    up_sums, _ = products(up_pair, [], gate_sums[-1][1])

    hiddens, near, far = [], [], up_sums[-1][1][-1]
    bits = [1 << bit for bit in range(n_tensor.bit_length() - 1)]
    for half in range(HALVES):
        up_terms = after(up_sums[half][0], [up_sums[-1][1][0], near])
        hidden = hidden_rows(routings[half], gate_sums[half][0], up_terms, slots)
        hiddens.append(copies(hidden, to_level, bits[::-1], far))
        near, far = hiddens[-1][1], hiddens[-1][n_tensor // 2]
    down_joined = join_blocks(place, down_weight, after(down_same, [h[0] for h in hiddens]))
    down_pair = core_exchange(down_joined)
    backs, parts = [], []
    for half in range(HALVES):
        hids = after(hiddens[half], parts)
        parts = down_sums(place, routings[half], hids, down_pair, slots)
        total = parts[0].astype(jnp.float32)
        for step in range(1, chips):
            total = total + to_chip(parts[step], step).astype(jnp.float32)
        total = total.astype(jnp.bfloat16).reshape(n_tensor, rows // HALVES, -1)
        for other in range(n_tensor):
            piece = lax.dynamic_index_in_dim(total, level ^ other, 0, keepdims=False)
            backs.append(to_level(piece, other) if other else piece)
    return finish(place, backs, n_tensor, depth)


def solution(mesh):
    return jax.shard_map(
        local,
        mesh=mesh,
        in_specs=(
            P(("expert", "tensor"), None),
            P("expert", None),
            P("expert", None),
            P(None, ("expert", "tensor"), None),
            P(None, ("expert", "tensor"), None),
            P(None, ("expert", "tensor"), None),
        ),
        out_specs=P(("expert", "tensor"), None),
        check_vma=False,
    )
```

```python
import functools

import jax
import jax.numpy as jnp
from jax import lax
from jax.experimental import pallas as pl
from jax.experimental.pallas import tpu as pltpu
from jax.sharding import PartitionSpec as P

VMEM_BYTES = 22 * 1024 * 1024
CORES = 2
HALVES = 2
TILE = 256
LANES = 128

SMEM_SPEC = pl.BlockSpec(memory_space=pltpu.SMEM)
VMEM_SPEC = pl.BlockSpec(memory_space=pltpu.VMEM)
ANY_SPEC = pl.BlockSpec(memory_space=pl.ANY)
PARAMS = pltpu.CompilerParams(vmem_limit_bytes=VMEM_BYTES)


def bf16(*shape):
    return jax.ShapeDtypeStruct(shape, jnp.bfloat16)


def cost(flops, elements):
    return pl.CostEstimate(flops=flops, bytes_accessed=2 * elements, transcendentals=0)


def rows_of(block, rows):
    return pl.ds(pl.multiple_of(block * rows, rows), rows)


def cut_kernel(depth, place_ref, tokens_ref, *refs):
    outs, held = refs[:-1], refs[-1]
    levels, _, wide = held.shape
    core, level = place_ref[1], place_ref[2]
    tokens = tokens_ref[...]
    for other in range(levels):
        sides = []
        for side in range(CORES):
            blocks = range(side, wide // depth, CORES)
            starts = [(block * levels + other) * depth for block in blocks]
            sides.append(jnp.concatenate([tokens[:, s : s + depth] for s in starts], axis=1))
        swapped = jnp.concatenate(sides[::-1], axis=1)
        piece = jnp.where(core == 0, jnp.concatenate(sides, axis=1), swapped)
        held[jnp.bitwise_xor(level, other)] = piece
    for step, out_ref in enumerate(outs):
        out_ref[...] = held[step]


def cut_tokens(place, tokens, levels, depth):
    rows, model = tokens.shape
    shape = (rows, model // levels)
    return pl.pallas_call(
        functools.partial(cut_kernel, depth),
        in_specs=[SMEM_SPEC, VMEM_SPEC],
        out_specs=[VMEM_SPEC] * levels,
        out_shape=[bf16(*shape)] * levels,
        scratch_shapes=[pltpu.VMEM((levels,) + shape, jnp.bfloat16)],
        compiler_params=PARAMS,
    )(place, tokens)


def group_kernel(levels, place_ref, routing_ref, *refs):
    pieces, outs = refs[:levels], refs[levels:]
    wide = pieces[0].shape[1]
    rows = pieces[0].shape[0] // HALVES
    for step, piece in enumerate(pieces):
        target = rows_of(jnp.bitwise_xor(place_ref[2], step), rows)
        for half, out_ref in enumerate(outs):
            out_ref[target, :wide] = piece[half * rows : (half + 1) * rows, :]
    for level in range(levels):
        for half, out_ref in enumerate(outs):
            first = (level * HALVES + half) * rows
            out_ref[level * rows : (level + 1) * rows, wide:] = routing_ref[first : first + rows, :]


def group_tokens(place, routing, pieces):
    rows, wide = pieces[0].shape
    levels = len(pieces)
    return pl.pallas_call(
        functools.partial(group_kernel, levels),
        in_specs=[SMEM_SPEC, VMEM_SPEC] + [VMEM_SPEC] * levels,
        out_specs=[VMEM_SPEC] * HALVES,
        out_shape=[bf16(levels * rows // HALVES, wide + LANES)] * HALVES,
        compiler_params=PARAMS,
    )(place, routing, *pieces)


def finish_kernel(depth, levels, place_ref, *refs):
    pieces, (out_ref, held) = refs[:-2], refs[-2:]
    rows, wide = pieces[0].shape
    for index, piece in enumerate(pieces):
        half, step = index // levels, index % levels
        other = jnp.bitwise_xor(place_ref[2], step)
        held[other, half * rows : (half + 1) * rows, :] = piece[...]
    chips = wide // depth // CORES
    first, second = [], []
    for chip in range(chips):
        for side in range(CORES):
            for other in range(levels):
                for parts, place in ((first, side), (second, 1 - side)):
                    start = (place * chips + chip) * depth
                    parts.append(held[other, :, start : start + depth])
    first, second = jnp.concatenate(first, axis=1), jnp.concatenate(second, axis=1)
    out_ref[...] = jnp.where(place_ref[1] == 0, first, second)


def finish(place, pieces, levels, depth):
    rows, wide = pieces[0].shape
    rows = rows * HALVES
    return pl.pallas_call(
        functools.partial(finish_kernel, depth, levels),
        in_specs=[SMEM_SPEC] + [VMEM_SPEC] * len(pieces),
        out_specs=VMEM_SPEC,
        out_shape=bf16(rows, wide * levels),
        scratch_shapes=[pltpu.VMEM((levels, rows, wide), jnp.bfloat16)],
        compiler_params=PARAMS,
    )(place, *pieces)


def join_kernel(chips, place_ref, own_ref, *refs):
    pieces, (out_ref, sems) = refs[: chips - 1], refs[chips - 1 :]
    width = out_ref.shape[3]
    chip = place_ref[0]
    columns = pl.ds(pl.multiple_of(chip * width, width), width)
    sources = [own_ref.at[:, :, columns]] + list(pieces)
    copies = [
        pltpu.make_async_copy(source, out_ref.at[:, jnp.bitwise_xor(chip, step)], sems.at[step])
        for step, source in enumerate(sources)
    ]
    for copy in copies:
        copy.start()
    for copy in copies:
        copy.wait()


def join_blocks(place, own, pieces):
    experts, depth, units = own.shape
    chips = len(pieces) + 1
    shape = (experts, chips, depth, units // chips)
    return pl.pallas_call(
        functools.partial(join_kernel, chips),
        in_specs=[SMEM_SPEC] + [ANY_SPEC] * chips,
        out_specs=VMEM_SPEC,
        out_shape=bf16(*shape),
        scratch_shapes=[pltpu.SemaphoreType.DMA((chips,))],
        cost_estimate=cost(0, 2 * own.size),
        compiler_params=PARAMS,
    )(place, own, *pieces)


def pick_kernel(chips, place_ref, *refs):
    toks, refs = refs[:chips], refs[chips:]
    weights, (keep_ref, send_ref, routing_ref, left) = refs[:CORES], refs[CORES:]
    experts, depth, width = weights[0].shape
    rows = toks[0].shape[0]
    for step, tok in enumerate(toks):
        block = jnp.bitwise_xor(step, place_ref[2])
        left[rows_of(block, rows), :] = tok[:, : CORES * depth]
        routing_ref[block] = tok[:, CORES * depth :]
    slots = keep_ref.shape[2] // width
    tile = min(TILE, width)
    for start in range(0, width, tile):
        sums = []
        for which in range(experts):
            total = None
            for side, weight in enumerate(weights):
                term = jnp.dot(
                    left[:, side * depth : (side + 1) * depth],
                    weight[which, :, start : start + tile],
                    preferred_element_type=jnp.float32,
                )
                total = term if total is None else total + term
            sums.append(total)
        for step in range(chips):
            out_ref = (keep_ref, send_ref)[step % 2]
            ids = routing_ref[step].astype(jnp.float32)
            for slot in range(slots):
                chosen = ids[:, slot : slot + 1]
                picked = sums[0][step * rows : (step + 1) * rows]
                for which in range(1, experts):
                    other = sums[which][step * rows : (step + 1) * rows]
                    picked = jnp.where(chosen == which, other, picked)
                first = slot * width + start
                out_ref[step // 2, :, first : first + tile] = picked.astype(out_ref.dtype)


def picked_sums(place, toks, weights, slots):
    chips, rows = len(toks), toks[0].shape[0]
    experts, depth, width = weights[0].shape
    wide = CORES * depth
    count = chips * rows
    return pl.pallas_call(
        functools.partial(pick_kernel, chips),
        in_specs=[SMEM_SPEC] + [VMEM_SPEC] * (chips + CORES),
        out_specs=[VMEM_SPEC] * 3,
        out_shape=[bf16(chips // 2, rows, slots * width)] * 2 + [bf16(chips, rows, LANES)],
        scratch_shapes=[pltpu.VMEM((count, wide), jnp.bfloat16)],
        cost_estimate=cost(
            2 * count * wide * width * experts,
            count * wide + experts * wide * width + count * slots * width,
        ),
        compiler_params=PARAMS,
    )(place, *toks, *weights)


def hidden_kernel(terms, slots, routing_ref, *refs):
    gates, ups, out_ref = refs[:terms], refs[terms : 2 * terms], refs[2 * terms]
    scores = routing_ref[0].astype(jnp.float32)[:, slots : 2 * slots]
    combine = scores / jnp.sum(scores, axis=1, keepdims=True)
    width = out_ref.shape[1] // slots
    for slot in range(slots):
        columns = slice(slot * width, (slot + 1) * width)
        gate_sum = sum(ref[0, :, columns].astype(jnp.float32) for ref in gates)
        up_sum = sum(ref[0, :, columns].astype(jnp.float32) for ref in ups)
        value = gate_sum / (1.0 + jnp.exp(-gate_sum)) * up_sum * combine[:, slot : slot + 1]
        out_ref[:, columns] = value.astype(out_ref.dtype)


def hidden_rows(routing, gates, ups, slots):
    return pl.pallas_call(
        functools.partial(hidden_kernel, len(gates), slots),
        in_specs=[VMEM_SPEC] * (1 + 2 * len(gates)),
        out_specs=VMEM_SPEC,
        out_shape=bf16(*gates[0].shape[1:]),
        compiler_params=PARAMS,
    )(routing, *gates, *ups)


def down_kernel(slots, levels, place_ref, routing_ref, *refs):
    hids, refs = refs[:levels], refs[levels:]
    weights, (*outs, left) = refs[:CORES], refs[CORES:]
    experts, depth, width = weights[0].shape
    rows = hids[0].shape[0]
    for step, hid_ref in enumerate(hids):
        block = jnp.bitwise_xor(place_ref[2], step)
        ids = routing_ref[step].astype(jnp.float32)
        for which in range(experts):
            mine = jnp.zeros((rows, width), jnp.float32)
            for slot in range(slots):
                value = hid_ref[:, slot * width : (slot + 1) * width].astype(jnp.float32)
                mine = jnp.where(ids[:, slot : slot + 1] == which, value, mine)
            left[which, rows_of(block, rows), :] = mine.astype(left.dtype)
    for side, weight in enumerate(weights):
        total = None
        for which in range(experts):
            term = lax.dot_general(
                left[which],
                weight[which],
                (((1,), (1,)), ((), ())),
                preferred_element_type=jnp.float32,
            )
            total = term if total is None else total + term
        for step, out_ref in enumerate(outs):
            part = total[step * rows : (step + 1) * rows]
            out_ref[:, side * depth : (side + 1) * depth] = part.astype(out_ref.dtype)


def down_sums(place, routing, hids, weights, slots):
    rows, levels = hids[0].shape[0], len(hids)
    experts, depth, width = weights[0].shape
    wide, count = CORES * depth, levels * rows
    return pl.pallas_call(
        functools.partial(down_kernel, slots, levels),
        in_specs=[SMEM_SPEC] + [VMEM_SPEC] * (1 + levels + CORES),
        out_specs=[VMEM_SPEC] * levels,
        out_shape=[bf16(rows, wide)] * levels,
        scratch_shapes=[pltpu.VMEM((experts, count, width), jnp.bfloat16)],
        cost_estimate=cost(
            2 * count * wide * width * experts,
            count * slots * width + experts * wide * width + count * wide,
        ),
        compiler_params=PARAMS,
    )(place, routing, *hids, *weights)


def after(values, others):
    return lax.optimization_barrier((values, others))[0]


def local(tokens, expert_ids, gate_scores, gate_weight, up_weight, down_weight):
    n_expert, n_tensor = lax.axis_size("expert"), lax.axis_size("tensor")
    chips = n_expert // CORES
    rows = tokens.shape[0]
    depth, units = gate_weight.shape[1:]
    slots = expert_ids.shape[1]
    width = units // chips
    spot, level = lax.axis_index("expert"), lax.axis_index("tensor")
    q, c = spot // CORES, spot % CORES
    place = jnp.stack([q, c, level])

    def to_chip(value, step):
        pairs = [(s, s ^ (step * CORES)) for s in range(n_expert)]
        return lax.ppermute(value, "expert", pairs)

    def to_core(value):
        return lax.ppermute(value, "expert", [(s, s ^ 1) for s in range(n_expert)])

    def to_level(value, step):
        return lax.ppermute(value, "tensor", [(s, s ^ step) for s in range(n_tensor)])

    def copies(value, send, bits, behind=()):
        held = {0: value}
        for bit in bits:
            for step in sorted(held):
                held[step + bit] = send(after(held[step], behind), bit)
            behind = ()
        return [held[step] for step in range(len(held))]

    def level_sums(keep, send, behind):
        terms, marks, bit = [keep], [], 1
        send = after(send, behind[:1])
        while True:
            terms.append(to_level(send, bit))
            bit *= 2
            if bit == n_tensor:
                return terms, marks + [terms[-1]]
            send = sum(term[1::2].astype(jnp.float32) for term in terms).astype(jnp.bfloat16)
            terms = [term[::2] for term in terms]
            send = after(send, behind[len(marks) + 1 : len(marks) + 2])
            marks.append(send)

    def blocks_of(weight):
        return [
            lax.dynamic_slice_in_dim(weight, (q ^ step) * width, width, 2)
            for step in range(1, chips)
        ]

    def chip_exchange(blocks):
        return [to_chip(block, step) for step, block in enumerate(blocks, 1)]

    def core_exchange(joined):
        pair = [joined, to_core(joined)]
        return [side.reshape(side.shape[0], chips * depth, width) for side in pair]

    routing = jnp.concatenate([expert_ids, gate_scores], axis=1).astype(jnp.bfloat16)
    routing = jnp.pad(routing, ((0, 0), (0, LANES - 2 * slots)))
    gate_same = chip_exchange(blocks_of(gate_weight))
    cut = cut_tokens(place, tokens, n_tensor, depth)
    cut = [cut[0]] + [to_level(cut[step], step) for step in range(1, n_tensor)]
    groups = group_tokens(place, routing, cut)

    bits = [1 << bit for bit in range(chips.bit_length() - 1)]
    toks = []
    for half in range(HALVES):
        turn = (half + 1) % len(bits)
        toks.append(copies(groups[half], to_chip, bits[turn:] + bits[:turn]))
    near = [tok[bit] for tok in toks for bit in bits]
    gate_joined = join_blocks(place, gate_weight, after(gate_same, near))
    gate_pair = core_exchange(gate_joined)
    up_blocks = blocks_of(up_weight)
    toks = after(toks, up_blocks)
    up_same = chip_exchange(after(up_blocks, toks))

    def products(weights, behind, parts):
        sums, routings = [], []
        for half in range(HALVES):
            left = after(toks[half], parts)
            *parts, routing = picked_sums(place, left, weights, slots)
            terms, behind = level_sums(*parts, behind)
            sums.append((terms, behind))
            routings.append(routing)
        return sums, routings

    gate_sums, routings = products(gate_pair, [], [])
    up_joined = join_blocks(place, up_weight, after(up_same, gate_sums[-1][1]))
    up_pair = core_exchange(up_joined)
    down_same = chip_exchange(after(blocks_of(down_weight), up_joined))
    up_sums, _ = products(up_pair, [], gate_sums[-1][1])

    hiddens, near, far = [], [], ()
    bits = [1 << bit for bit in range(n_tensor.bit_length() - 1)]
    for half in range(HALVES):
        up_terms = after(up_sums[half][0], [up_sums[-1][1][0], near])
        hidden = hidden_rows(routings[half], gate_sums[half][0], up_terms, slots)
        hiddens.append(copies(hidden, to_level, bits[::-1], far))
        near, far = hiddens[-1][1], [hiddens[0][n_tensor // 2]]
    down_joined = join_blocks(place, down_weight, after(down_same, [hiddens[-1][0], far[0]]))
    down_pair = core_exchange(down_joined)
    backs, parts, got = [], [], []
    for half in range(HALVES):
        hids = after(hiddens[half], parts or hiddens[-1][1])
        parts = down_sums(place, routings[half], hids, down_pair, slots)
        got = [to_chip(part, step) for step, part in enumerate(after(parts, got)) if step]
        total = sum(part.astype(jnp.float32) for part in [parts[0], *got])
        total = total.astype(jnp.bfloat16).reshape(n_tensor, rows // HALVES, -1)
        for other in range(n_tensor):
            piece = lax.dynamic_index_in_dim(total, level ^ other, 0, keepdims=False)
            backs.append(to_level(piece, other) if other else piece)
    return finish(place, backs, n_tensor, depth)


def solution(mesh):
    return jax.shard_map(
        local,
        mesh=mesh,
        in_specs=(
            P(("expert", "tensor"), None),
            P("expert", None),
            P("expert", None),
            P(None, ("expert", "tensor"), None),
            P(None, ("expert", "tensor"), None),
            P(None, ("expert", "tensor"), None),
        ),
        out_specs=P(("expert", "tensor"), None),
        check_vma=False,
    )
```

```python
import functools

import jax
import jax.numpy as jnp
from jax import lax
from jax.experimental import pallas as pl
from jax.experimental.pallas import tpu as pltpu
from jax.sharding import PartitionSpec as P

VMEM_BYTES = 22 * 1024 * 1024
CORES = 2
HALVES = 2
TILE = 256
LANES = 128

SMEM_SPEC = pl.BlockSpec(memory_space=pltpu.SMEM)
VMEM_SPEC = pl.BlockSpec(memory_space=pltpu.VMEM)
ANY_SPEC = pl.BlockSpec(memory_space=pl.ANY)
PARAMS = pltpu.CompilerParams(vmem_limit_bytes=VMEM_BYTES)


def bf16(*shape):
    return jax.ShapeDtypeStruct(shape, jnp.bfloat16)


def cost(flops, elements):
    return pl.CostEstimate(flops=flops, bytes_accessed=2 * elements, transcendentals=0)


def rows_of(block, rows):
    return pl.ds(pl.multiple_of(block * rows, rows), rows)


def cut_kernel(depth, place_ref, tokens_ref, *refs):
    outs, held = refs[:-1], refs[-1]
    levels, _, wide = held.shape
    core, level = place_ref[1], place_ref[2]
    tokens = tokens_ref[...]
    for other in range(levels):
        sides = []
        for side in range(CORES):
            blocks = range(side, wide // depth, CORES)
            starts = [(block * levels + other) * depth for block in blocks]
            sides.append(jnp.concatenate([tokens[:, s : s + depth] for s in starts], axis=1))
        swapped = jnp.concatenate(sides[::-1], axis=1)
        piece = jnp.where(core == 0, jnp.concatenate(sides, axis=1), swapped)
        held[jnp.bitwise_xor(level, other)] = piece
    for step, out_ref in enumerate(outs):
        out_ref[...] = held[step]


def cut_tokens(place, tokens, levels, depth):
    rows, model = tokens.shape
    shape = (rows, model // levels)
    return pl.pallas_call(
        functools.partial(cut_kernel, depth),
        in_specs=[SMEM_SPEC, VMEM_SPEC],
        out_specs=[VMEM_SPEC] * levels,
        out_shape=[bf16(*shape)] * levels,
        scratch_shapes=[pltpu.VMEM((levels,) + shape, jnp.bfloat16)],
        compiler_params=PARAMS,
    )(place, tokens)


def group_kernel(levels, place_ref, routing_ref, *refs):
    pieces, outs = refs[:levels], refs[levels:]
    wide = pieces[0].shape[1]
    rows = pieces[0].shape[0] // HALVES
    for step, piece in enumerate(pieces):
        target = rows_of(jnp.bitwise_xor(place_ref[2], step), rows)
        for half, out_ref in enumerate(outs):
            out_ref[target, :wide] = piece[half * rows : (half + 1) * rows, :]
    for level in range(levels):
        for half, out_ref in enumerate(outs):
            first = (level * HALVES + half) * rows
            out_ref[level * rows : (level + 1) * rows, wide:] = routing_ref[first : first + rows, :]


def group_tokens(place, routing, pieces):
    rows, wide = pieces[0].shape
    levels = len(pieces)
    return pl.pallas_call(
        functools.partial(group_kernel, levels),
        in_specs=[SMEM_SPEC, VMEM_SPEC] + [VMEM_SPEC] * levels,
        out_specs=[VMEM_SPEC] * HALVES,
        out_shape=[bf16(levels * rows // HALVES, wide + LANES)] * HALVES,
        compiler_params=PARAMS,
    )(place, routing, *pieces)


def finish_kernel(depth, levels, place_ref, *refs):
    pieces, (out_ref, held) = refs[:-2], refs[-2:]
    rows, wide = pieces[0].shape
    for index, piece in enumerate(pieces):
        half, step = index // levels, index % levels
        other = jnp.bitwise_xor(place_ref[2], step)
        held[other, half * rows : (half + 1) * rows, :] = piece[...]
    chips = wide // depth // CORES
    first, second = [], []
    for chip in range(chips):
        for side in range(CORES):
            for other in range(levels):
                for parts, place in ((first, side), (second, 1 - side)):
                    start = (place * chips + chip) * depth
                    parts.append(held[other, :, start : start + depth])
    first, second = jnp.concatenate(first, axis=1), jnp.concatenate(second, axis=1)
    out_ref[...] = jnp.where(place_ref[1] == 0, first, second)


def finish(place, pieces, levels, depth):
    rows, wide = pieces[0].shape
    rows = rows * HALVES
    return pl.pallas_call(
        functools.partial(finish_kernel, depth, levels),
        in_specs=[SMEM_SPEC] + [VMEM_SPEC] * len(pieces),
        out_specs=VMEM_SPEC,
        out_shape=bf16(rows, wide * levels),
        scratch_shapes=[pltpu.VMEM((levels, rows, wide), jnp.bfloat16)],
        compiler_params=PARAMS,
    )(place, *pieces)


def join_kernel(chips, place_ref, own_ref, *refs):
    pieces, (out_ref, sems) = refs[: chips - 1], refs[chips - 1 :]
    width = out_ref.shape[3]
    chip = place_ref[0]
    columns = pl.ds(pl.multiple_of(chip * width, width), width)
    sources = [own_ref.at[:, :, columns]] + list(pieces)
    copies = [
        pltpu.make_async_copy(source, out_ref.at[:, jnp.bitwise_xor(chip, step)], sems.at[step])
        for step, source in enumerate(sources)
    ]
    for copy in copies:
        copy.start()
    for copy in copies:
        copy.wait()


def join_blocks(place, own, pieces):
    experts, depth, units = own.shape
    chips = len(pieces) + 1
    shape = (experts, chips, depth, units // chips)
    return pl.pallas_call(
        functools.partial(join_kernel, chips),
        in_specs=[SMEM_SPEC] + [ANY_SPEC] * chips,
        out_specs=VMEM_SPEC,
        out_shape=bf16(*shape),
        scratch_shapes=[pltpu.SemaphoreType.DMA((chips,))],
        cost_estimate=cost(0, 2 * own.size),
        compiler_params=PARAMS,
    )(place, own, *pieces)


def pick_kernel(chips, place_ref, *refs):
    toks, refs = refs[:chips], refs[chips:]
    weights, (keep_ref, send_ref, routing_ref, left) = refs[:CORES], refs[CORES:]
    experts, depth, width = weights[0].shape
    rows = toks[0].shape[0]
    for step, tok in enumerate(toks):
        block = jnp.bitwise_xor(step, place_ref[2])
        left[rows_of(block, rows), :] = tok[:, : CORES * depth]
        routing_ref[block] = tok[:, CORES * depth :]
    slots = keep_ref.shape[2] // width
    tile = min(TILE, width)
    for start in range(0, width, tile):
        sums = []
        for which in range(experts):
            total = None
            for side, weight in enumerate(weights):
                term = jnp.dot(
                    left[:, side * depth : (side + 1) * depth],
                    weight[which, :, start : start + tile],
                    preferred_element_type=jnp.float32,
                )
                total = term if total is None else total + term
            sums.append(total)
        for step in range(chips):
            out_ref = (keep_ref, send_ref)[step % 2]
            ids = routing_ref[step].astype(jnp.float32)
            for slot in range(slots):
                chosen = ids[:, slot : slot + 1]
                picked = sums[0][step * rows : (step + 1) * rows]
                for which in range(1, experts):
                    other = sums[which][step * rows : (step + 1) * rows]
                    picked = jnp.where(chosen == which, other, picked)
                first = slot * width + start
                out_ref[step // 2, :, first : first + tile] = picked.astype(out_ref.dtype)


def picked_sums(place, toks, weights, slots):
    chips, rows = len(toks), toks[0].shape[0]
    experts, depth, width = weights[0].shape
    wide = CORES * depth
    count = chips * rows
    return pl.pallas_call(
        functools.partial(pick_kernel, chips),
        in_specs=[SMEM_SPEC] + [VMEM_SPEC] * (chips + CORES),
        out_specs=[VMEM_SPEC] * 3,
        out_shape=[bf16(chips // 2, rows, slots * width)] * 2 + [bf16(chips, rows, LANES)],
        scratch_shapes=[pltpu.VMEM((count, wide), jnp.bfloat16)],
        cost_estimate=cost(
            2 * count * wide * width * experts,
            count * wide + experts * wide * width + count * slots * width,
        ),
        compiler_params=PARAMS,
    )(place, *toks, *weights)


def hidden_kernel(terms, slots, routing_ref, *refs):
    gates, ups, out_ref = refs[:terms], refs[terms : 2 * terms], refs[2 * terms]
    scores = routing_ref[0].astype(jnp.float32)[:, slots : 2 * slots]
    combine = scores / jnp.sum(scores, axis=1, keepdims=True)
    width = out_ref.shape[1] // slots
    for slot in range(slots):
        columns = slice(slot * width, (slot + 1) * width)
        gate_sum = sum(ref[0, :, columns].astype(jnp.float32) for ref in gates)
        up_sum = sum(ref[0, :, columns].astype(jnp.float32) for ref in ups)
        value = gate_sum / (1.0 + jnp.exp(-gate_sum)) * up_sum * combine[:, slot : slot + 1]
        out_ref[:, columns] = value.astype(out_ref.dtype)


def hidden_rows(routing, gates, ups, slots):
    return pl.pallas_call(
        functools.partial(hidden_kernel, len(gates), slots),
        in_specs=[VMEM_SPEC] * (1 + 2 * len(gates)),
        out_specs=VMEM_SPEC,
        out_shape=bf16(*gates[0].shape[1:]),
        compiler_params=PARAMS,
    )(routing, *gates, *ups)


def down_kernel(slots, levels, place_ref, routing_ref, *refs):
    hids, refs = refs[:levels], refs[levels:]
    weights, (*outs, left) = refs[:CORES], refs[CORES:]
    experts, depth, width = weights[0].shape
    rows = hids[0].shape[0]
    for step, hid_ref in enumerate(hids):
        block = jnp.bitwise_xor(place_ref[2], step)
        ids = routing_ref[step].astype(jnp.float32)
        for which in range(experts):
            mine = jnp.zeros((rows, width), jnp.float32)
            for slot in range(slots):
                value = hid_ref[:, slot * width : (slot + 1) * width].astype(jnp.float32)
                mine = jnp.where(ids[:, slot : slot + 1] == which, value, mine)
            left[which, rows_of(block, rows), :] = mine.astype(left.dtype)
    for side, weight in enumerate(weights):
        total = None
        for which in range(experts):
            term = lax.dot_general(
                left[which],
                weight[which],
                (((1,), (1,)), ((), ())),
                preferred_element_type=jnp.float32,
            )
            total = term if total is None else total + term
        for step, out_ref in enumerate(outs):
            part = total[step * rows : (step + 1) * rows]
            out_ref[:, side * depth : (side + 1) * depth] = part.astype(out_ref.dtype)


def down_sums(place, routing, hids, weights, slots):
    rows, levels = hids[0].shape[0], len(hids)
    experts, depth, width = weights[0].shape
    wide, count = CORES * depth, levels * rows
    return pl.pallas_call(
        functools.partial(down_kernel, slots, levels),
        in_specs=[SMEM_SPEC] + [VMEM_SPEC] * (1 + levels + CORES),
        out_specs=[VMEM_SPEC] * levels,
        out_shape=[bf16(rows, wide)] * levels,
        scratch_shapes=[pltpu.VMEM((experts, count, width), jnp.bfloat16)],
        cost_estimate=cost(
            2 * count * wide * width * experts,
            count * slots * width + experts * wide * width + count * wide,
        ),
        compiler_params=PARAMS,
    )(place, routing, *hids, *weights)


def after(values, others):
    return lax.optimization_barrier((values, others))[0]


def local(tokens, expert_ids, gate_scores, gate_weight, up_weight, down_weight):
    n_expert, n_tensor = lax.axis_size("expert"), lax.axis_size("tensor")
    chips = n_expert // CORES
    rows = tokens.shape[0]
    depth, units = gate_weight.shape[1:]
    slots = expert_ids.shape[1]
    width = units // chips
    spot, level = lax.axis_index("expert"), lax.axis_index("tensor")
    q, c = spot // CORES, spot % CORES
    place = jnp.stack([q, c, level])

    def to_chip(value, step):
        pairs = [(s, s ^ (step * CORES)) for s in range(n_expert)]
        return lax.ppermute(value, "expert", pairs)

    def to_core(value):
        return lax.ppermute(value, "expert", [(s, s ^ 1) for s in range(n_expert)])

    def to_level(value, step):
        return lax.ppermute(value, "tensor", [(s, s ^ step) for s in range(n_tensor)])

    def copies(held, send, bits):
        held = dict(held)
        for bit in bits:
            for step in sorted(held):
                held[step + bit] = send(held[step], bit)
        return [held[step] for step in range(len(held))]

    def level_sums(keep, send, behind):
        terms, marks, bit = [keep], [], 1
        send = after(send, behind[:1])
        while True:
            terms.append(to_level(send, bit))
            bit *= 2
            if bit == n_tensor:
                return terms, marks + [terms[-1]]
            send = sum(term[1::2].astype(jnp.float32) for term in terms).astype(jnp.bfloat16)
            terms = [term[::2] for term in terms]
            send = after(send, behind[len(marks) + 1 : len(marks) + 2])
            marks.append(send)

    def blocks_of(weight):
        return [
            lax.dynamic_slice_in_dim(weight, (q ^ step) * width, width, 2)
            for step in range(1, chips)
        ]

    def chip_exchange(blocks):
        return [to_chip(block, step) for step, block in enumerate(blocks, 1)]

    def core_exchange(joined):
        pair = [joined, to_core(joined)]
        return [side.reshape(side.shape[0], chips * depth, width) for side in pair]

    routing = jnp.concatenate([expert_ids, gate_scores], axis=1).astype(jnp.bfloat16)
    routing = jnp.pad(routing, ((0, 0), (0, LANES - 2 * slots)))
    gate_same = chip_exchange(blocks_of(gate_weight))
    cut = cut_tokens(place, tokens, n_tensor, depth)
    cut = [cut[0]] + [to_level(cut[step], step) for step in range(1, n_tensor)]
    groups = group_tokens(place, routing, cut)

    bits = [1 << bit for bit in range(chips.bit_length() - 1)]
    toks = []
    for half in range(HALVES):
        turn = (half + 1) % len(bits)
        toks.append(copies({0: groups[half]}, to_chip, bits[turn:] + bits[:turn]))
    near = [tok[bit] for tok in toks for bit in bits]
    gate_joined = join_blocks(place, gate_weight, after(gate_same, near))
    gate_pair = core_exchange(gate_joined)
    up_blocks = blocks_of(up_weight)
    toks = after(toks, up_blocks)
    up_same = chip_exchange(after(up_blocks, toks))

    def products(weights, behind, parts):
        sums, routings = [], []
        for half in range(HALVES):
            left = after(toks[half], parts)
            *parts, routing = picked_sums(place, left, weights, slots)
            terms, behind = level_sums(*parts, behind)
            sums.append((terms, behind))
            routings.append(routing)
        return sums, routings

    gate_sums, routings = products(gate_pair, [], [])
    up_joined = join_blocks(place, up_weight, after(up_same, gate_sums[-1][1]))
    up_pair = core_exchange(up_joined)
    down_same = chip_exchange(after(blocks_of(down_weight), up_joined))
    up_sums, _ = products(up_pair, [], gate_sums[-1][1])

    held, first = [], [up_sums[-1][1][0]]
    bits = [n_tensor >> bit for bit in range(1, n_tensor.bit_length())]
    for half in range(HALVES):
        up_terms = after(up_sums[half][0], first)
        hidden = hidden_rows(routings[half], gate_sums[half][0], up_terms, slots)
        held.append({0: hidden, bits[0]: to_level(after(hidden, first[1:]), bits[0])})
        if half == 0:
            blocks = copies(held[0], to_level, bits[1:])
            first = [first[0], blocks[1]]
    down_joined = join_blocks(place, down_weight, after(down_same, [hidden, blocks[bits[0]]]))
    down_pair = core_exchange(down_joined)
    backs, got = [], []
    for half in range(HALVES):
        if half:
            blocks = copies(after(held[half], parts), to_level, bits[1:])
        parts = down_sums(place, routings[half], blocks, down_pair, slots)
        got = [to_chip(part, step) for step, part in enumerate(after(parts, got)) if step]
        total = sum(part.astype(jnp.float32) for part in [parts[0], *got])
        total = total.astype(jnp.bfloat16).reshape(n_tensor, rows // HALVES, -1)
        for other in range(n_tensor):
            piece = lax.dynamic_index_in_dim(total, level ^ other, 0, keepdims=False)
            backs.append(to_level(piece, other) if other else piece)
    return finish(place, backs, n_tensor, depth)


def solution(mesh):
    return jax.shard_map(
        local,
        mesh=mesh,
        in_specs=(
            P(("expert", "tensor"), None),
            P("expert", None),
            P("expert", None),
            P(None, ("expert", "tensor"), None),
            P(None, ("expert", "tensor"), None),
            P(None, ("expert", "tensor"), None),
        ),
        out_specs=P(("expert", "tensor"), None),
        check_vma=False,
    )
```

```python
import functools

import jax
import jax.numpy as jnp
from jax import lax
from jax.experimental import pallas as pl
from jax.experimental.pallas import tpu as pltpu
from jax.sharding import PartitionSpec as P

VMEM_BYTES = 14 * 1024 * 1024
CORES = 2
HALVES = 2
TILE = 256
LANES = 128

SMEM_SPEC = pl.BlockSpec(memory_space=pltpu.SMEM)
VMEM_SPEC = pl.BlockSpec(memory_space=pltpu.VMEM)
ANY_SPEC = pl.BlockSpec(memory_space=pl.ANY)
PARAMS = pltpu.CompilerParams(vmem_limit_bytes=VMEM_BYTES)


def bf16(*shape):
    return jax.ShapeDtypeStruct(shape, jnp.bfloat16)


def cost(flops, elements):
    return pl.CostEstimate(flops=flops, bytes_accessed=2 * elements, transcendentals=0)


def rows_of(block, rows):
    return pl.ds(pl.multiple_of(block * rows, rows), rows)


def cut_kernel(depth, place_ref, tokens_ref, *refs):
    outs, held = refs[:-1], refs[-1]
    levels, _, wide = held.shape
    core, level = place_ref[1], place_ref[2]
    tokens = tokens_ref[...]
    for other in range(levels):
        sides = []
        for side in range(CORES):
            blocks = range(side, wide // depth, CORES)
            starts = [(block * levels + other) * depth for block in blocks]
            sides.append(jnp.concatenate([tokens[:, s : s + depth] for s in starts], axis=1))
        swapped = jnp.concatenate(sides[::-1], axis=1)
        piece = jnp.where(core == 0, jnp.concatenate(sides, axis=1), swapped)
        held[jnp.bitwise_xor(level, other)] = piece
    for step, out_ref in enumerate(outs):
        out_ref[...] = held[step]


def cut_tokens(place, tokens, levels, depth):
    rows, model = tokens.shape
    shape = (rows, model // levels)
    return pl.pallas_call(
        functools.partial(cut_kernel, depth),
        in_specs=[SMEM_SPEC, VMEM_SPEC],
        out_specs=[VMEM_SPEC] * levels,
        out_shape=[bf16(*shape)] * levels,
        scratch_shapes=[pltpu.VMEM((levels,) + shape, jnp.bfloat16)],
        compiler_params=PARAMS,
    )(place, tokens)


def group_kernel(levels, place_ref, routing_ref, *refs):
    pieces, outs = refs[:levels], refs[levels:]
    wide = pieces[0].shape[1]
    rows = pieces[0].shape[0] // HALVES
    for step, piece in enumerate(pieces):
        target = rows_of(jnp.bitwise_xor(place_ref[2], step), rows)
        for half, out_ref in enumerate(outs):
            out_ref[target, :wide] = piece[half * rows : (half + 1) * rows, :]
    for level in range(levels):
        for half, out_ref in enumerate(outs):
            first = (level * HALVES + half) * rows
            out_ref[level * rows : (level + 1) * rows, wide:] = routing_ref[first : first + rows, :]


def group_tokens(place, routing, pieces):
    rows, wide = pieces[0].shape
    levels = len(pieces)
    return pl.pallas_call(
        functools.partial(group_kernel, levels),
        in_specs=[SMEM_SPEC, VMEM_SPEC] + [VMEM_SPEC] * levels,
        out_specs=[VMEM_SPEC] * HALVES,
        out_shape=[bf16(levels * rows // HALVES, wide + LANES)] * HALVES,
        compiler_params=PARAMS,
    )(place, routing, *pieces)


def finish_kernel(depth, levels, place_ref, *refs):
    pieces, (out_ref, held) = refs[:-2], refs[-2:]
    rows, wide = pieces[0].shape
    for index, piece in enumerate(pieces):
        half, step = index // levels, index % levels
        other = jnp.bitwise_xor(place_ref[2], step)
        held[other, half * rows : (half + 1) * rows, :] = piece[...]
    chips = wide // depth // CORES
    first, second = [], []
    for chip in range(chips):
        for side in range(CORES):
            for other in range(levels):
                for parts, place in ((first, side), (second, 1 - side)):
                    start = (place * chips + chip) * depth
                    parts.append(held[other, :, start : start + depth])
    first, second = jnp.concatenate(first, axis=1), jnp.concatenate(second, axis=1)
    out_ref[...] = jnp.where(place_ref[1] == 0, first, second)


def finish(place, pieces, levels, depth):
    rows, wide = pieces[0].shape
    rows = rows * HALVES
    return pl.pallas_call(
        functools.partial(finish_kernel, depth, levels),
        in_specs=[SMEM_SPEC] + [VMEM_SPEC] * len(pieces),
        out_specs=VMEM_SPEC,
        out_shape=bf16(rows, wide * levels),
        scratch_shapes=[pltpu.VMEM((levels, rows, wide), jnp.bfloat16)],
        compiler_params=PARAMS,
    )(place, *pieces)


def join_kernel(chips, place_ref, own_ref, *refs):
    pieces, (out_ref, sems) = refs[: chips - 1], refs[chips - 1 :]
    width = out_ref.shape[3]
    chip = place_ref[0]
    columns = pl.ds(pl.multiple_of(chip * width, width), width)
    sources = [own_ref.at[:, :, columns]] + list(pieces)
    copies = [
        pltpu.make_async_copy(source, out_ref.at[:, jnp.bitwise_xor(chip, step)], sems.at[step])
        for step, source in enumerate(sources)
    ]
    for copy in copies:
        copy.start()
    for copy in copies:
        copy.wait()


def join_blocks(place, own, pieces):
    experts, depth, units = own.shape
    chips = len(pieces) + 1
    shape = (experts, chips, depth, units // chips)
    return pl.pallas_call(
        functools.partial(join_kernel, chips),
        in_specs=[SMEM_SPEC] + [ANY_SPEC] * chips,
        out_specs=VMEM_SPEC,
        out_shape=bf16(*shape),
        scratch_shapes=[pltpu.SemaphoreType.DMA((chips,))],
        cost_estimate=cost(0, 2 * own.size),
        compiler_params=PARAMS,
    )(place, own, *pieces)


def pick_kernel(chips, place_ref, *refs):
    toks, refs = refs[:chips], refs[chips:]
    weights, (keep_ref, send_ref, routing_ref, left) = refs[:CORES], refs[CORES:]
    experts, depth, width = weights[0].shape
    rows = toks[0].shape[0]
    for step, tok in enumerate(toks):
        block = jnp.bitwise_xor(step, place_ref[2])
        left[rows_of(block, rows), :] = tok[:, : CORES * depth]
        routing_ref[block] = tok[:, CORES * depth :]
    slots = keep_ref.shape[2] // width
    tile = min(TILE, width)
    for start in range(0, width, tile):
        sums = []
        for which in range(experts):
            total = None
            for side, weight in enumerate(weights):
                term = jnp.dot(
                    left[:, side * depth : (side + 1) * depth],
                    weight[which, :, start : start + tile],
                    preferred_element_type=jnp.float32,
                )
                total = term if total is None else total + term
            sums.append(total)
        for step in range(chips):
            out_ref = (keep_ref, send_ref)[step % 2]
            ids = routing_ref[step].astype(jnp.float32)
            for slot in range(slots):
                chosen = ids[:, slot : slot + 1]
                picked = sums[0][step * rows : (step + 1) * rows]
                for which in range(1, experts):
                    other = sums[which][step * rows : (step + 1) * rows]
                    picked = jnp.where(chosen == which, other, picked)
                first = slot * width + start
                out_ref[step // 2, :, first : first + tile] = picked.astype(out_ref.dtype)


def picked_sums(place, toks, weights, slots):
    chips, rows = len(toks), toks[0].shape[0]
    experts, depth, width = weights[0].shape
    wide = CORES * depth
    count = chips * rows
    return pl.pallas_call(
        functools.partial(pick_kernel, chips),
        in_specs=[SMEM_SPEC] + [VMEM_SPEC] * (chips + CORES),
        out_specs=[VMEM_SPEC] * 3,
        out_shape=[bf16(chips // 2, rows, slots * width)] * 2 + [bf16(chips, rows, LANES)],
        scratch_shapes=[pltpu.VMEM((count, wide), jnp.bfloat16)],
        cost_estimate=cost(
            2 * count * wide * width * experts,
            count * wide + experts * wide * width + count * slots * width,
        ),
        compiler_params=PARAMS,
    )(place, *toks, *weights)


def hidden_kernel(terms, slots, routing_ref, *refs):
    gates, ups, out_ref = refs[:terms], refs[terms : 2 * terms], refs[2 * terms]
    scores = routing_ref[0].astype(jnp.float32)[:, slots : 2 * slots]
    combine = scores / jnp.sum(scores, axis=1, keepdims=True)
    width = out_ref.shape[1] // slots
    for slot in range(slots):
        columns = slice(slot * width, (slot + 1) * width)
        gate_sum = sum(ref[0, :, columns].astype(jnp.float32) for ref in gates)
        up_sum = sum(ref[0, :, columns].astype(jnp.float32) for ref in ups)
        value = gate_sum / (1.0 + jnp.exp(-gate_sum)) * up_sum * combine[:, slot : slot + 1]
        out_ref[:, columns] = value.astype(out_ref.dtype)


def hidden_rows(routing, gates, ups, slots):
    return pl.pallas_call(
        functools.partial(hidden_kernel, len(gates), slots),
        in_specs=[VMEM_SPEC] * (1 + 2 * len(gates)),
        out_specs=VMEM_SPEC,
        out_shape=bf16(*gates[0].shape[1:]),
        compiler_params=PARAMS,
    )(routing, *gates, *ups)


def down_kernel(slots, levels, place_ref, routing_ref, *refs):
    hids, refs = refs[:levels], refs[levels:]
    weights, (*outs, left) = refs[:CORES], refs[CORES:]
    experts, depth, width = weights[0].shape
    rows = hids[0].shape[0]
    for step, hid_ref in enumerate(hids):
        block = jnp.bitwise_xor(place_ref[2], step)
        ids = routing_ref[step].astype(jnp.float32)
        values = hid_ref[...].astype(jnp.float32)
        values = [values[:, slot * width : (slot + 1) * width] for slot in range(slots)]
        for which in range(experts):
            mine = jnp.zeros((rows, width), jnp.float32)
            for slot in range(slots):
                mine = jnp.where(ids[:, slot : slot + 1] == which, values[slot], mine)
            left[rows_of(block, rows), which * width : (which + 1) * width] = mine.astype(
                left.dtype
            )
    for side, weight in enumerate(weights):
        joined = jnp.concatenate([weight[which] for which in range(experts)], axis=1)
        total = lax.dot_general(
            left[...], joined, (((1,), (1,)), ((), ())), preferred_element_type=jnp.float32
        )
        for step, out_ref in enumerate(outs):
            part = total[step * rows : (step + 1) * rows]
            out_ref[:, side * depth : (side + 1) * depth] = part.astype(out_ref.dtype)


def down_sums(place, routing, hids, weights, slots):
    rows, levels = hids[0].shape[0], len(hids)
    experts, depth, width = weights[0].shape
    wide, count = CORES * depth, levels * rows
    return pl.pallas_call(
        functools.partial(down_kernel, slots, levels),
        in_specs=[SMEM_SPEC] + [VMEM_SPEC] * (1 + levels + CORES),
        out_specs=[VMEM_SPEC] * levels,
        out_shape=[bf16(rows, wide)] * levels,
        scratch_shapes=[pltpu.VMEM((count, experts * width), jnp.bfloat16)],
        cost_estimate=cost(
            2 * count * wide * width * experts,
            count * slots * width + experts * wide * width + count * wide,
        ),
        compiler_params=PARAMS,
    )(place, routing, *hids, *weights)


def after(values, others):
    return lax.optimization_barrier((values, others))[0]


def local(tokens, expert_ids, gate_scores, gate_weight, up_weight, down_weight):
    n_expert, n_tensor = lax.axis_size("expert"), lax.axis_size("tensor")
    chips = n_expert // CORES
    rows = tokens.shape[0]
    depth, units = gate_weight.shape[1:]
    slots = expert_ids.shape[1]
    width = units // chips
    spot, level = lax.axis_index("expert"), lax.axis_index("tensor")
    q, c = spot // CORES, spot % CORES
    place = jnp.stack([q, c, level])

    def to_chip(value, step):
        pairs = [(s, s ^ (step * CORES)) for s in range(n_expert)]
        return lax.ppermute(value, "expert", pairs)

    def to_core(value):
        return lax.ppermute(value, "expert", [(s, s ^ 1) for s in range(n_expert)])

    def to_level(value, step):
        return lax.ppermute(value, "tensor", [(s, s ^ step) for s in range(n_tensor)])

    def copies(held, send, bits):
        held = dict(held)
        for bit in bits:
            for step in sorted(held):
                held[step + bit] = send(held[step], bit)
        return [held[step] for step in range(len(held))]

    def level_sums(keep, send, behind):
        terms, marks, bit = [keep], [], 1
        send = after(send, behind[:1])
        while True:
            terms.append(to_level(send, bit))
            bit *= 2
            if bit == n_tensor:
                return terms, marks + [terms[-1]]
            send = sum(term[1::2].astype(jnp.float32) for term in terms).astype(jnp.bfloat16)
            terms = [term[::2] for term in terms]
            send = after(send, behind[len(marks) + 1 : len(marks) + 2])
            marks.append(send)

    def blocks_of(weight):
        return [
            lax.dynamic_slice_in_dim(weight, (q ^ step) * width, width, 2)
            for step in range(1, chips)
        ]

    def chip_exchange(blocks):
        return [to_chip(block, step) for step, block in enumerate(blocks, 1)]

    def core_exchange(joined):
        pair = [joined, to_core(joined)]
        return [side.reshape(side.shape[0], chips * depth, width) for side in pair]

    routing = jnp.concatenate([expert_ids, gate_scores], axis=1).astype(jnp.bfloat16)
    routing = jnp.pad(routing, ((0, 0), (0, LANES - 2 * slots)))
    gate_same = chip_exchange(blocks_of(gate_weight))
    cut = cut_tokens(place, tokens, n_tensor, depth)
    cut = [cut[0]] + [to_level(cut[step], step) for step in range(1, n_tensor)]
    groups = group_tokens(place, routing, cut)

    bits = [1 << bit for bit in range(chips.bit_length() - 1)]
    toks = []
    for half in range(HALVES):
        turn = (half + 1) % len(bits)
        toks.append(copies({0: groups[half]}, to_chip, bits[turn:] + bits[:turn]))
    near = [tok[bit] for tok in toks for bit in bits]
    gate_joined = join_blocks(place, gate_weight, after(gate_same, near))
    gate_pair = core_exchange(gate_joined)
    up_blocks = blocks_of(up_weight)
    toks = after(toks, up_blocks)
    up_same = chip_exchange(after(up_blocks, toks))

    def products(weights, behind, parts):
        sums, routings = [], []
        for half in range(HALVES):
            left = after(toks[half], parts)
            *parts, routing = picked_sums(place, left, weights, slots)
            terms, behind = level_sums(*parts, behind)
            sums.append((terms, behind))
            routings.append(routing)
        return sums, routings

    gate_sums, routings = products(gate_pair, [], [])
    up_joined = join_blocks(place, up_weight, after(up_same, gate_sums[-1][1]))
    up_pair = core_exchange(up_joined)
    down_same = chip_exchange(after(blocks_of(down_weight), up_joined))
    up_sums, _ = products(up_pair, [], gate_sums[-1][1])

    held, first = [], [up_sums[-1][1][0]]
    bits = [n_tensor >> bit for bit in range(1, n_tensor.bit_length())]
    for half in range(HALVES):
        up_terms = after(up_sums[half][0], first)
        hidden = hidden_rows(routings[half], gate_sums[half][0], up_terms, slots)
        held.append({0: hidden, bits[0]: to_level(after(hidden, first[1:]), bits[0])})
        if half == 0:
            blocks = copies(held[0], to_level, bits[1:])
            first = [first[0], blocks[1]]
    down_joined = join_blocks(place, down_weight, after(down_same, [hidden, blocks[bits[0]]]))
    down_pair = core_exchange(down_joined)
    backs, got = [], []
    for half in range(HALVES):
        if half:
            blocks = copies(after(held[half], parts), to_level, bits[1:])
        parts = down_sums(place, routings[half], blocks, down_pair, slots)
        got = [to_chip(part, step) for step, part in enumerate(after(parts, got)) if step]
        total = sum(part.astype(jnp.float32) for part in [parts[0], *got])
        total = total.astype(jnp.bfloat16).reshape(n_tensor, rows // HALVES, -1)
        for other in range(n_tensor):
            piece = lax.dynamic_index_in_dim(total, level ^ other, 0, keepdims=False)
            backs.append(to_level(piece, other) if other else piece)
    return finish(place, backs, n_tensor, depth)


def solution(mesh):
    return jax.shard_map(
        local,
        mesh=mesh,
        in_specs=(
            P(("expert", "tensor"), None),
            P("expert", None),
            P("expert", None),
            P(None, ("expert", "tensor"), None),
            P(None, ("expert", "tensor"), None),
            P(None, ("expert", "tensor"), None),
        ),
        out_specs=P(("expert", "tensor"), None),
        check_vma=False,
    )
```

```python
import functools

import jax
import jax.numpy as jnp
from jax import lax
from jax.experimental import pallas as pl
from jax.experimental.pallas import tpu as pltpu
from jax.sharding import PartitionSpec as P

VMEM_BYTES = 14 * 1024 * 1024
CORES = 2
HALVES = 2
TILE = 256
LANES = 128

SMEM_SPEC = pl.BlockSpec(memory_space=pltpu.SMEM)
VMEM_SPEC = pl.BlockSpec(memory_space=pltpu.VMEM)
ANY_SPEC = pl.BlockSpec(memory_space=pl.ANY)
PARAMS = pltpu.CompilerParams(vmem_limit_bytes=VMEM_BYTES)


def bf16(*shape):
    return jax.ShapeDtypeStruct(shape, jnp.bfloat16)


def cost(flops, elements):
    return pl.CostEstimate(flops=flops, bytes_accessed=2 * elements, transcendentals=0)


def rows_of(block, rows):
    return pl.ds(pl.multiple_of(block * rows, rows), rows)


def cut_kernel(depth, place_ref, tokens_ref, *refs):
    outs, held = refs[:-1], refs[-1]
    levels, _, wide = held.shape
    core, level = place_ref[1], place_ref[2]
    tokens = tokens_ref[...]
    for other in range(levels):
        sides = []
        for side in range(CORES):
            blocks = range(side, wide // depth, CORES)
            starts = [(block * levels + other) * depth for block in blocks]
            sides.append(jnp.concatenate([tokens[:, s : s + depth] for s in starts], axis=1))
        swapped = jnp.concatenate(sides[::-1], axis=1)
        piece = jnp.where(core == 0, jnp.concatenate(sides, axis=1), swapped)
        held[jnp.bitwise_xor(level, other)] = piece
    for step, out_ref in enumerate(outs):
        out_ref[...] = held[step]


def cut_tokens(place, tokens, levels, depth):
    rows, model = tokens.shape
    shape = (rows, model // levels)
    return pl.pallas_call(
        functools.partial(cut_kernel, depth),
        in_specs=[SMEM_SPEC, VMEM_SPEC],
        out_specs=[VMEM_SPEC] * levels,
        out_shape=[bf16(*shape)] * levels,
        scratch_shapes=[pltpu.VMEM((levels,) + shape, jnp.bfloat16)],
        compiler_params=PARAMS,
    )(place, tokens)


def group_kernel(levels, place_ref, routing_ref, *refs):
    pieces, outs = refs[:levels], refs[levels:]
    wide = pieces[0].shape[1]
    rows = pieces[0].shape[0] // HALVES
    for step, piece in enumerate(pieces):
        target = rows_of(jnp.bitwise_xor(place_ref[2], step), rows)
        for half, out_ref in enumerate(outs):
            out_ref[target, :wide] = piece[half * rows : (half + 1) * rows, :]
    for level in range(levels):
        for half, out_ref in enumerate(outs):
            first = (level * HALVES + half) * rows
            out_ref[level * rows : (level + 1) * rows, wide:] = routing_ref[first : first + rows, :]


def group_tokens(place, routing, pieces):
    rows, wide = pieces[0].shape
    levels = len(pieces)
    return pl.pallas_call(
        functools.partial(group_kernel, levels),
        in_specs=[SMEM_SPEC, VMEM_SPEC] + [VMEM_SPEC] * levels,
        out_specs=[VMEM_SPEC] * HALVES,
        out_shape=[bf16(levels * rows // HALVES, wide + LANES)] * HALVES,
        compiler_params=PARAMS,
    )(place, routing, *pieces)


def finish_kernel(depth, levels, place_ref, *refs):
    pieces, (out_ref, held) = refs[:-2], refs[-2:]
    rows, wide = pieces[0].shape
    for index, piece in enumerate(pieces):
        half, step = index // levels, index % levels
        other = jnp.bitwise_xor(place_ref[2], step)
        held[other, half * rows : (half + 1) * rows, :] = piece[...]
    chips = wide // depth // CORES
    first, second = [], []
    for chip in range(chips):
        for side in range(CORES):
            for other in range(levels):
                for parts, place in ((first, side), (second, 1 - side)):
                    start = (place * chips + chip) * depth
                    parts.append(held[other, :, start : start + depth])
    first, second = jnp.concatenate(first, axis=1), jnp.concatenate(second, axis=1)
    out_ref[...] = jnp.where(place_ref[1] == 0, first, second)


def finish(place, pieces, levels, depth):
    rows, wide = pieces[0].shape
    rows = rows * HALVES
    return pl.pallas_call(
        functools.partial(finish_kernel, depth, levels),
        in_specs=[SMEM_SPEC] + [VMEM_SPEC] * len(pieces),
        out_specs=VMEM_SPEC,
        out_shape=bf16(rows, wide * levels),
        scratch_shapes=[pltpu.VMEM((levels, rows, wide), jnp.bfloat16)],
        compiler_params=PARAMS,
    )(place, *pieces)


def join_kernel(chips, place_ref, own_ref, *refs):
    pieces, (out_ref, sems) = refs[: chips - 1], refs[chips - 1 :]
    width = out_ref.shape[3]
    chip = place_ref[0]
    columns = pl.ds(pl.multiple_of(chip * width, width), width)
    sources = [own_ref.at[:, :, columns]] + list(pieces)
    copies = [
        pltpu.make_async_copy(source, out_ref.at[:, jnp.bitwise_xor(chip, step)], sems.at[step])
        for step, source in enumerate(sources)
    ]
    for copy in copies:
        copy.start()
    for copy in copies:
        copy.wait()


def join_blocks(place, own, pieces):
    experts, depth, units = own.shape
    chips = len(pieces) + 1
    shape = (experts, chips, depth, units // chips)
    return pl.pallas_call(
        functools.partial(join_kernel, chips),
        in_specs=[SMEM_SPEC] + [ANY_SPEC] * chips,
        out_specs=VMEM_SPEC,
        out_shape=bf16(*shape),
        scratch_shapes=[pltpu.SemaphoreType.DMA((chips,))],
        cost_estimate=cost(0, 2 * own.size),
        compiler_params=PARAMS,
    )(place, own, *pieces)


def pick_kernel(chips, place_ref, *refs):
    toks, refs = refs[:chips], refs[chips:]
    weights, (keep_ref, send_ref, routing_ref, left) = refs[:CORES], refs[CORES:]
    experts, depth, width = weights[0].shape
    rows = toks[0].shape[0]
    for step, tok in enumerate(toks):
        block = jnp.bitwise_xor(step, place_ref[2])
        left[rows_of(block, rows), :] = tok[:, : CORES * depth]
        routing_ref[block] = tok[:, CORES * depth :]
    slots = keep_ref.shape[2] // width
    tile = min(TILE, width)
    for start in range(0, width, tile):
        sums = []
        for which in range(experts):
            total = None
            for side, weight in enumerate(weights):
                term = jnp.dot(
                    left[:, side * depth : (side + 1) * depth],
                    weight[which, :, start : start + tile],
                    preferred_element_type=jnp.float32,
                )
                total = term if total is None else total + term
            sums.append(total)
        for step in range(chips):
            out_ref = (keep_ref, send_ref)[step % 2]
            ids = routing_ref[step].astype(jnp.float32)
            for slot in range(slots):
                chosen = ids[:, slot : slot + 1]
                picked = sums[0][step * rows : (step + 1) * rows]
                for which in range(1, experts):
                    other = sums[which][step * rows : (step + 1) * rows]
                    picked = jnp.where(chosen == which, other, picked)
                first = slot * width + start
                out_ref[step // 2, :, first : first + tile] = picked.astype(out_ref.dtype)


def picked_sums(place, toks, weights, slots):
    chips, rows = len(toks), toks[0].shape[0]
    experts, depth, width = weights[0].shape
    wide = CORES * depth
    count = chips * rows
    return pl.pallas_call(
        functools.partial(pick_kernel, chips),
        in_specs=[SMEM_SPEC] + [VMEM_SPEC] * (chips + CORES),
        out_specs=[VMEM_SPEC] * 3,
        out_shape=[bf16(chips // 2, rows, slots * width)] * 2 + [bf16(chips, rows, LANES)],
        scratch_shapes=[pltpu.VMEM((count, wide), jnp.bfloat16)],
        cost_estimate=cost(
            2 * count * wide * width * experts,
            count * wide + experts * wide * width + count * slots * width,
        ),
        compiler_params=PARAMS,
    )(place, *toks, *weights)


def hidden_kernel(terms, slots, routing_ref, *refs):
    gates, ups, out_ref = refs[:terms], refs[terms : 2 * terms], refs[2 * terms]
    scores = routing_ref[0].astype(jnp.float32)[:, slots : 2 * slots]
    combine = scores / jnp.sum(scores, axis=1, keepdims=True)
    width = out_ref.shape[1] // slots
    for slot in range(slots):
        columns = slice(slot * width, (slot + 1) * width)
        gate_sum = sum(ref[0, :, columns].astype(jnp.float32) for ref in gates)
        up_sum = sum(ref[0, :, columns].astype(jnp.float32) for ref in ups)
        value = gate_sum / (1.0 + jnp.exp(-gate_sum)) * up_sum * combine[:, slot : slot + 1]
        out_ref[:, columns] = value.astype(out_ref.dtype)


def hidden_rows(routing, gates, ups, slots):
    return pl.pallas_call(
        functools.partial(hidden_kernel, len(gates), slots),
        in_specs=[VMEM_SPEC] * (1 + 2 * len(gates)),
        out_specs=VMEM_SPEC,
        out_shape=bf16(*gates[0].shape[1:]),
        compiler_params=PARAMS,
    )(routing, *gates, *ups)


def down_kernel(slots, levels, place_ref, routing_ref, *refs):
    hids, refs = refs[:levels], refs[levels:]
    weights, (*outs, left) = refs[:CORES], refs[CORES:]
    experts, depth, width = weights[0].shape
    rows = hids[0].shape[0]
    for step, hid_ref in enumerate(hids):
        block = jnp.bitwise_xor(place_ref[2], step)
        ids = routing_ref[step].astype(jnp.float32)
        values = hid_ref[...].astype(jnp.float32)
        values = [values[:, slot * width : (slot + 1) * width] for slot in range(slots)]
        for which in range(experts):
            mine = jnp.zeros((rows, width), jnp.float32)
            for slot in range(slots):
                mine = jnp.where(ids[:, slot : slot + 1] == which, values[slot], mine)
            left[rows_of(block, rows), which * width : (which + 1) * width] = mine.astype(
                left.dtype
            )
    for side, weight in enumerate(weights):
        joined = jnp.concatenate([weight[which] for which in range(experts)], axis=1)
        total = lax.dot_general(
            left[...], joined, (((1,), (1,)), ((), ())), preferred_element_type=jnp.float32
        )
        for step, out_ref in enumerate(outs):
            part = total[step * rows : (step + 1) * rows]
            out_ref[:, side * depth : (side + 1) * depth] = part.astype(out_ref.dtype)


def down_sums(place, routing, hids, weights, slots):
    rows, levels = hids[0].shape[0], len(hids)
    experts, depth, width = weights[0].shape
    wide, count = CORES * depth, levels * rows
    return pl.pallas_call(
        functools.partial(down_kernel, slots, levels),
        in_specs=[SMEM_SPEC] + [VMEM_SPEC] * (1 + levels + CORES),
        out_specs=[VMEM_SPEC] * levels,
        out_shape=[bf16(rows, wide)] * levels,
        scratch_shapes=[pltpu.VMEM((count, experts * width), jnp.bfloat16)],
        cost_estimate=cost(
            2 * count * wide * width * experts,
            count * slots * width + experts * wide * width + count * wide,
        ),
        compiler_params=PARAMS,
    )(place, routing, *hids, *weights)


def after(values, others):
    return lax.optimization_barrier((values, others))[0]


def local(tokens, expert_ids, gate_scores, gate_weight, up_weight, down_weight):
    n_expert, n_tensor = lax.axis_size("expert"), lax.axis_size("tensor")
    chips = n_expert // CORES
    rows = tokens.shape[0]
    depth, units = gate_weight.shape[1:]
    slots = expert_ids.shape[1]
    width = units // chips
    spot, level = lax.axis_index("expert"), lax.axis_index("tensor")
    q, c = spot // CORES, spot % CORES
    place = jnp.stack([q, c, level])

    def to_chip(value, step):
        pairs = [(s, s ^ (step * CORES)) for s in range(n_expert)]
        return lax.ppermute(value, "expert", pairs)

    def to_core(value):
        return lax.ppermute(value, "expert", [(s, s ^ 1) for s in range(n_expert)])

    def to_level(value, step):
        return lax.ppermute(value, "tensor", [(s, s ^ step) for s in range(n_tensor)])

    def copies(held, send, bits):
        held = dict(held)
        for bit in bits:
            for step in sorted(held):
                held[step + bit] = send(held[step], bit)
        return [held[step] for step in range(len(held))]

    def level_sums(keep, send, behind):
        terms, marks, bit = [keep], [], 1
        send = after(send, behind[:1])
        while True:
            terms.append(to_level(send, bit))
            bit *= 2
            if bit == n_tensor:
                return terms, marks + [terms[-1]]
            send = sum(term[1::2].astype(jnp.float32) for term in terms).astype(jnp.bfloat16)
            terms = [term[::2] for term in terms]
            send = after(send, behind[len(marks) + 1 : len(marks) + 2])
            marks.append(send)

    def blocks_of(weight):
        return [
            lax.dynamic_slice_in_dim(weight, (q ^ step) * width, width, 2)
            for step in range(1, chips)
        ]

    def chip_exchange(blocks):
        return [to_chip(block, step) for step, block in enumerate(blocks, 1)]

    def core_exchange(joined):
        pair = [joined, to_core(joined)]
        return [side.reshape(side.shape[0], chips * depth, width) for side in pair]

    routing = jnp.concatenate([expert_ids, gate_scores], axis=1).astype(jnp.bfloat16)
    routing = jnp.pad(routing, ((0, 0), (0, LANES - 2 * slots)))
    gate_same = chip_exchange(blocks_of(gate_weight))
    cut = cut_tokens(place, tokens, n_tensor, depth)
    cut = [cut[0]] + [to_level(cut[step], step) for step in range(1, n_tensor)]
    groups = group_tokens(place, routing, cut)

    bits = [1 << bit for bit in range(chips.bit_length() - 1)]
    toks = []
    for half in range(HALVES):
        turn = (half + 1) % len(bits)
        toks.append(copies({0: groups[half]}, to_chip, bits[turn:] + bits[:turn]))
    near = [tok[bit] for tok in toks for bit in bits]
    gate_joined = join_blocks(place, gate_weight, after(gate_same, near))
    gate_pair = core_exchange(gate_joined)
    up_blocks = blocks_of(up_weight)
    toks = after(toks, up_blocks)
    up_same = chip_exchange(after(up_blocks, toks))

    def products(weights, chained, late):
        sums, routings, parts, behind = [], [], [], []
        for half in range(HALVES):
            left = after(toks[half], [parts, late if half else []])
            *parts, routing = picked_sums(place, left, weights, slots)
            terms, marks = level_sums(*parts, behind)
            behind = marks if chained else [(), *marks[1:]]
            sums.append((terms, marks))
            routings.append(routing)
        return sums, routings

    gate_sums, routings = products(gate_pair, False, [])
    ready = [gate_sums[0][1], gate_sums[-1][1][0]]
    up_joined = join_blocks(place, up_weight, after(up_same, ready))
    up_pair = core_exchange(up_joined)
    down_same = chip_exchange(after(blocks_of(down_weight), up_joined))
    up_sums, _ = products(up_pair, True, gate_sums[-1][1])

    held, first = [], [up_sums[-1][1][0]]
    bits = [n_tensor >> bit for bit in range(1, n_tensor.bit_length())]
    for half in range(HALVES):
        up_terms = after(up_sums[half][0], first)
        hidden = hidden_rows(routings[half], gate_sums[half][0], up_terms, slots)
        held.append({0: hidden, bits[0]: to_level(after(hidden, first[1:]), bits[0])})
        if half == 0:
            blocks = copies(held[0], to_level, bits[1:])
            first = [first[0], blocks[1]]
    down_joined = join_blocks(place, down_weight, after(down_same, [hidden, blocks[bits[0]]]))
    down_pair = core_exchange(down_joined)
    backs, got = [], []
    for half in range(HALVES):
        if half:
            blocks = copies(after(held[half], parts), to_level, bits[1:])
        parts = down_sums(place, routings[half], blocks, down_pair, slots)
        got = [to_chip(part, step) for step, part in enumerate(after(parts, got)) if step]
        total = sum(part.astype(jnp.float32) for part in [parts[0], *got])
        total = total.astype(jnp.bfloat16).reshape(n_tensor, rows // HALVES, -1)
        for other in range(n_tensor):
            piece = lax.dynamic_index_in_dim(total, level ^ other, 0, keepdims=False)
            backs.append(to_level(piece, other) if other else piece)
    return finish(place, backs, n_tensor, depth)


def solution(mesh):
    return jax.shard_map(
        local,
        mesh=mesh,
        in_specs=(
            P(("expert", "tensor"), None),
            P("expert", None),
            P("expert", None),
            P(None, ("expert", "tensor"), None),
            P(None, ("expert", "tensor"), None),
            P(None, ("expert", "tensor"), None),
        ),
        out_specs=P(("expert", "tensor"), None),
        check_vma=False,
    )
```

```python
import functools

import jax
import jax.numpy as jnp
from jax import lax
from jax.experimental import pallas as pl
from jax.experimental.pallas import tpu as pltpu
from jax.sharding import PartitionSpec as P

VMEM_BYTES = 14 * 1024 * 1024
CORES = 2
HALVES = 2
TILE = 256
LANES = 128

SMEM_SPEC = pl.BlockSpec(memory_space=pltpu.SMEM)
VMEM_SPEC = pl.BlockSpec(memory_space=pltpu.VMEM)
ANY_SPEC = pl.BlockSpec(memory_space=pl.ANY)
PARAMS = pltpu.CompilerParams(vmem_limit_bytes=VMEM_BYTES)


def bf16(*shape):
    return jax.ShapeDtypeStruct(shape, jnp.bfloat16)


def cost(flops, elements):
    return pl.CostEstimate(flops=flops, bytes_accessed=2 * elements, transcendentals=0)


def rows_of(block, rows):
    return pl.ds(pl.multiple_of(block * rows, rows), rows)


def cut_kernel(depth, place_ref, tokens_ref, *refs):
    outs, held = refs[:-1], refs[-1]
    levels, _, wide = held.shape
    core, level = place_ref[1], place_ref[2]
    tokens = tokens_ref[...]
    for other in range(levels):
        sides = []
        for side in range(CORES):
            blocks = range(side, wide // depth, CORES)
            starts = [(block * levels + other) * depth for block in blocks]
            sides.append(jnp.concatenate([tokens[:, s : s + depth] for s in starts], axis=1))
        swapped = jnp.concatenate(sides[::-1], axis=1)
        piece = jnp.where(core == 0, jnp.concatenate(sides, axis=1), swapped)
        held[jnp.bitwise_xor(level, other)] = piece
    for step, out_ref in enumerate(outs):
        out_ref[...] = held[step]


def cut_tokens(place, tokens, levels, depth):
    rows, model = tokens.shape
    shape = (rows, model // levels)
    return pl.pallas_call(
        functools.partial(cut_kernel, depth),
        in_specs=[SMEM_SPEC, VMEM_SPEC],
        out_specs=[VMEM_SPEC] * levels,
        out_shape=[bf16(*shape)] * levels,
        scratch_shapes=[pltpu.VMEM((levels,) + shape, jnp.bfloat16)],
        compiler_params=PARAMS,
    )(place, tokens)


def group_kernel(levels, place_ref, routing_ref, *refs):
    pieces, outs = refs[:levels], refs[levels:]
    wide = pieces[0].shape[1]
    rows = pieces[0].shape[0] // HALVES
    for step, piece in enumerate(pieces):
        target = rows_of(jnp.bitwise_xor(place_ref[2], step), rows)
        for half, out_ref in enumerate(outs):
            out_ref[target, :wide] = piece[half * rows : (half + 1) * rows, :]
    for level in range(levels):
        for half, out_ref in enumerate(outs):
            first = (level * HALVES + half) * rows
            out_ref[level * rows : (level + 1) * rows, wide:] = routing_ref[first : first + rows, :]


def group_tokens(place, routing, pieces):
    rows, wide = pieces[0].shape
    levels = len(pieces)
    return pl.pallas_call(
        functools.partial(group_kernel, levels),
        in_specs=[SMEM_SPEC, VMEM_SPEC] + [VMEM_SPEC] * levels,
        out_specs=[VMEM_SPEC] * HALVES,
        out_shape=[bf16(levels * rows // HALVES, wide + LANES)] * HALVES,
        compiler_params=PARAMS,
    )(place, routing, *pieces)


def finish_kernel(depth, levels, place_ref, *refs):
    pieces, (out_ref, held) = refs[:-2], refs[-2:]
    rows, wide = pieces[0].shape
    for index, piece in enumerate(pieces):
        half, step = index // levels, index % levels
        other = jnp.bitwise_xor(place_ref[2], step)
        held[other, half * rows : (half + 1) * rows, :] = piece[...]
    chips = wide // depth // CORES
    first, second = [], []
    for chip in range(chips):
        for side in range(CORES):
            for other in range(levels):
                for parts, place in ((first, side), (second, 1 - side)):
                    start = (place * chips + chip) * depth
                    parts.append(held[other, :, start : start + depth])
    first, second = jnp.concatenate(first, axis=1), jnp.concatenate(second, axis=1)
    out_ref[...] = jnp.where(place_ref[1] == 0, first, second)


def finish(place, pieces, levels, depth):
    rows, wide = pieces[0].shape
    rows = rows * HALVES
    return pl.pallas_call(
        functools.partial(finish_kernel, depth, levels),
        in_specs=[SMEM_SPEC] + [VMEM_SPEC] * len(pieces),
        out_specs=VMEM_SPEC,
        out_shape=bf16(rows, wide * levels),
        scratch_shapes=[pltpu.VMEM((levels, rows, wide), jnp.bfloat16)],
        compiler_params=PARAMS,
    )(place, *pieces)


def join_kernel(chips, place_ref, own_ref, *refs):
    pieces, (out_ref, sems) = refs[: chips - 1], refs[chips - 1 :]
    width = out_ref.shape[3]
    chip = place_ref[0]
    columns = pl.ds(pl.multiple_of(chip * width, width), width)
    sources = [own_ref.at[:, :, columns]] + list(pieces)
    copies = [
        pltpu.make_async_copy(source, out_ref.at[:, jnp.bitwise_xor(chip, step)], sems.at[step])
        for step, source in enumerate(sources)
    ]
    for copy in copies:
        copy.start()
    for copy in copies:
        copy.wait()


def join_blocks(place, own, pieces):
    experts, depth, units = own.shape
    chips = len(pieces) + 1
    shape = (experts, chips, depth, units // chips)
    return pl.pallas_call(
        functools.partial(join_kernel, chips),
        in_specs=[SMEM_SPEC] + [ANY_SPEC] * chips,
        out_specs=VMEM_SPEC,
        out_shape=bf16(*shape),
        scratch_shapes=[pltpu.SemaphoreType.DMA((chips,))],
        cost_estimate=cost(0, 2 * own.size),
        compiler_params=PARAMS,
    )(place, own, *pieces)


def pick_kernel(chips, place_ref, *refs):
    toks, refs = refs[:chips], refs[chips:]
    weights, (keep_ref, send_ref, routing_ref, left) = refs[:CORES], refs[CORES:]
    experts, depth, width = weights[0].shape
    rows = toks[0].shape[0]
    for step, tok in enumerate(toks):
        block = jnp.bitwise_xor(step, place_ref[2])
        left[rows_of(block, rows), :] = tok[:, : CORES * depth]
        routing_ref[block] = tok[:, CORES * depth :]
    slots = keep_ref.shape[2] // width
    tile = min(TILE, width)
    for start in range(0, width, tile):
        sums = []
        for which in range(experts):
            total = None
            for side, weight in enumerate(weights):
                term = jnp.dot(
                    left[:, side * depth : (side + 1) * depth],
                    weight[which, :, start : start + tile],
                    preferred_element_type=jnp.float32,
                )
                total = term if total is None else total + term
            sums.append(total)
        for step in range(chips):
            out_ref = (keep_ref, send_ref)[step % 2]
            ids = routing_ref[step].astype(jnp.float32)
            for slot in range(slots):
                chosen = ids[:, slot : slot + 1]
                picked = sums[0][step * rows : (step + 1) * rows]
                for which in range(1, experts):
                    other = sums[which][step * rows : (step + 1) * rows]
                    picked = jnp.where(chosen == which, other, picked)
                first = slot * width + start
                out_ref[step // 2, :, first : first + tile] = picked.astype(out_ref.dtype)


def picked_sums(place, toks, weights, slots):
    chips, rows = len(toks), toks[0].shape[0]
    experts, depth, width = weights[0].shape
    wide = CORES * depth
    count = chips * rows
    return pl.pallas_call(
        functools.partial(pick_kernel, chips),
        in_specs=[SMEM_SPEC] + [VMEM_SPEC] * (chips + CORES),
        out_specs=[VMEM_SPEC] * 3,
        out_shape=[bf16(chips // 2, rows, slots * width)] * 2 + [bf16(chips, rows, LANES)],
        scratch_shapes=[pltpu.VMEM((count, wide), jnp.bfloat16)],
        cost_estimate=cost(
            2 * count * wide * width * experts,
            count * wide + experts * wide * width + count * slots * width,
        ),
        compiler_params=PARAMS,
    )(place, *toks, *weights)


def hidden_kernel(terms, slots, routing_ref, *refs):
    gates, ups, out_ref = refs[:terms], refs[terms : 2 * terms], refs[2 * terms]
    scores = routing_ref[0].astype(jnp.float32)[:, slots : 2 * slots]
    combine = scores / jnp.sum(scores, axis=1, keepdims=True)
    width = out_ref.shape[1] // slots
    for slot in range(slots):
        columns = slice(slot * width, (slot + 1) * width)
        gate_sum = sum(ref[0, :, columns].astype(jnp.float32) for ref in gates)
        up_sum = sum(ref[0, :, columns].astype(jnp.float32) for ref in ups)
        value = gate_sum / (1.0 + jnp.exp(-gate_sum)) * up_sum * combine[:, slot : slot + 1]
        out_ref[:, columns] = value.astype(out_ref.dtype)


def hidden_rows(routing, gates, ups, slots):
    return pl.pallas_call(
        functools.partial(hidden_kernel, len(gates), slots),
        in_specs=[VMEM_SPEC] * (1 + 2 * len(gates)),
        out_specs=VMEM_SPEC,
        out_shape=bf16(*gates[0].shape[1:]),
        compiler_params=PARAMS,
    )(routing, *gates, *ups)


def down_kernel(slots, levels, place_ref, routing_ref, *refs):
    hids, refs = refs[:levels], refs[levels:]
    weights, (*outs, left) = refs[:CORES], refs[CORES:]
    experts, depth, width = weights[0].shape
    rows = hids[0].shape[0]
    for step, hid_ref in enumerate(hids):
        block = jnp.bitwise_xor(place_ref[2], step)
        ids = routing_ref[step].astype(jnp.float32)
        values = hid_ref[...].astype(jnp.float32)
        values = [values[:, slot * width : (slot + 1) * width] for slot in range(slots)]
        for which in range(experts):
            mine = jnp.zeros((rows, width), jnp.float32)
            for slot in range(slots):
                mine = jnp.where(ids[:, slot : slot + 1] == which, values[slot], mine)
            left[rows_of(block, rows), which * width : (which + 1) * width] = mine.astype(
                left.dtype
            )
    for side, weight in enumerate(weights):
        joined = jnp.concatenate([weight[which] for which in range(experts)], axis=1)
        total = lax.dot_general(
            left[...], joined, (((1,), (1,)), ((), ())), preferred_element_type=jnp.float32
        )
        for step, out_ref in enumerate(outs):
            part = total[step * rows : (step + 1) * rows]
            out_ref[:, side * depth : (side + 1) * depth] = part.astype(out_ref.dtype)


def down_sums(place, routing, hids, weights, slots):
    rows, levels = hids[0].shape[0], len(hids)
    experts, depth, width = weights[0].shape
    wide, count = CORES * depth, levels * rows
    return pl.pallas_call(
        functools.partial(down_kernel, slots, levels),
        in_specs=[SMEM_SPEC] + [VMEM_SPEC] * (1 + levels + CORES),
        out_specs=[VMEM_SPEC] * levels,
        out_shape=[bf16(rows, wide)] * levels,
        scratch_shapes=[pltpu.VMEM((count, experts * width), jnp.bfloat16)],
        cost_estimate=cost(
            2 * count * wide * width * experts,
            count * slots * width + experts * wide * width + count * wide,
        ),
        compiler_params=PARAMS,
    )(place, routing, *hids, *weights)


def after(values, others):
    return lax.optimization_barrier((values, others))[0]


def local(tokens, expert_ids, gate_scores, gate_weight, up_weight, down_weight):
    n_expert, n_tensor = lax.axis_size("expert"), lax.axis_size("tensor")
    chips = n_expert // CORES
    rows = tokens.shape[0]
    depth, units = gate_weight.shape[1:]
    slots = expert_ids.shape[1]
    width = units // chips
    spot, level = lax.axis_index("expert"), lax.axis_index("tensor")
    q, c = spot // CORES, spot % CORES
    place = jnp.stack([q, c, level])

    def to_chip(value, step):
        pairs = [(s, s ^ (step * CORES)) for s in range(n_expert)]
        return lax.ppermute(value, "expert", pairs)

    def to_core(value):
        return lax.ppermute(value, "expert", [(s, s ^ 1) for s in range(n_expert)])

    def to_level(value, step):
        return lax.ppermute(value, "tensor", [(s, s ^ step) for s in range(n_tensor)])

    def copies(held, send, bits):
        held = dict(held)
        for bit in bits:
            for step in sorted(held):
                held[step + bit] = send(held[step], bit)
        return [held[step] for step in range(len(held))]

    def level_sums(keep, send, behind, pieces=1):
        terms, marks, bit = [keep], [], 1
        send = after(send, behind[:1])
        while True:
            if 2 * bit == n_tensor:
                got = [to_level(part, bit) for part in jnp.split(send, pieces, axis=1)]
                terms.append(jnp.concatenate(got, axis=1) if pieces > 1 else got[0])
                return terms, marks + [got]
            terms.append(to_level(send, bit))
            bit *= 2
            send = sum(term[1::2].astype(jnp.float32) for term in terms).astype(jnp.bfloat16)
            terms = [term[::2] for term in terms]
            send = after(send, behind[len(marks) + 1 : len(marks) + 2])
            marks.append(send)

    def blocks_of(weight):
        return [
            lax.dynamic_slice_in_dim(weight, (q ^ step) * width, width, 2)
            for step in range(1, chips)
        ]

    def chip_exchange(blocks):
        return [to_chip(block, step) for step, block in enumerate(blocks, 1)]

    def core_exchange(joined):
        pair = [joined, to_core(joined)]
        return [side.reshape(side.shape[0], chips * depth, width) for side in pair]

    routing = jnp.concatenate([expert_ids, gate_scores], axis=1).astype(jnp.bfloat16)
    routing = jnp.pad(routing, ((0, 0), (0, LANES - 2 * slots)))
    gate_same = chip_exchange(blocks_of(gate_weight))
    cut = cut_tokens(place, tokens, n_tensor, depth)
    cut = [cut[0]] + [to_level(cut[step], step) for step in range(1, n_tensor)]
    groups = group_tokens(place, routing, cut)

    bits = [1 << bit for bit in range(chips.bit_length() - 1)]
    toks = []
    for half in range(HALVES):
        turn = (half + 1) % len(bits)
        toks.append(copies({0: groups[half]}, to_chip, bits[turn:] + bits[:turn]))
    near = [tok[bit] for tok in toks for bit in bits]
    gate_joined = join_blocks(place, gate_weight, after(gate_same, near))
    gate_pair = core_exchange(gate_joined)
    up_blocks = blocks_of(up_weight)
    toks = after(toks, up_blocks)
    up_same = chip_exchange(after(up_blocks, toks))

    def products(weights, chained, late):
        sums, routings, parts, behind = [], [], [], []
        for half in range(HALVES):
            left = after(toks[half], [parts, late if half else []])
            *parts, routing = picked_sums(place, left, weights, slots)
            terms, marks = level_sums(*parts, behind, 1 if chained or not half else 2)
            behind = marks if chained else [(), *marks[1:]]
            sums.append((terms, marks))
            routings.append(routing)
        return sums, routings

    gate_sums, routings = products(gate_pair, False, [])
    ready = [gate_sums[0][1], gate_sums[-1][1][0], gate_sums[-1][1][-1][0]]
    up_joined = join_blocks(place, up_weight, after(up_same, ready))
    up_pair = core_exchange(up_joined)
    down_same = chip_exchange(after(blocks_of(down_weight), up_joined))
    up_sums, _ = products(up_pair, True, gate_sums[-1][1])

    held, first = [], [up_sums[-1][1][0]]
    bits = [n_tensor >> bit for bit in range(1, n_tensor.bit_length())]
    for half in range(HALVES):
        up_terms = after(up_sums[half][0], first)
        hidden = hidden_rows(routings[half], gate_sums[half][0], up_terms, slots)
        held.append({0: hidden, bits[0]: to_level(after(hidden, first[1:]), bits[0])})
        if half == 0:
            blocks = copies(held[0], to_level, bits[1:])
            first = [first[0], blocks[1]]
    down_joined = join_blocks(place, down_weight, after(down_same, [hidden, blocks[bits[0]]]))
    down_pair = core_exchange(down_joined)
    backs, got = [], []
    for half in range(HALVES):
        if half:
            blocks = copies(after(held[half], parts), to_level, bits[1:])
        parts = down_sums(place, routings[half], blocks, down_pair, slots)
        got = [to_chip(part, step) for step, part in enumerate(after(parts, got)) if step]
        total = sum(part.astype(jnp.float32) for part in [parts[0], *got])
        total = total.astype(jnp.bfloat16).reshape(n_tensor, rows // HALVES, -1)
        for other in range(n_tensor):
            piece = lax.dynamic_index_in_dim(total, level ^ other, 0, keepdims=False)
            backs.append(to_level(piece, other) if other else piece)
    return finish(place, backs, n_tensor, depth)


def solution(mesh):
    return jax.shard_map(
        local,
        mesh=mesh,
        in_specs=(
            P(("expert", "tensor"), None),
            P("expert", None),
            P("expert", None),
            P(None, ("expert", "tensor"), None),
            P(None, ("expert", "tensor"), None),
            P(None, ("expert", "tensor"), None),
        ),
        out_specs=P(("expert", "tensor"), None),
        check_vma=False,
    )
```

```python
import functools

import jax
import jax.numpy as jnp
from jax import lax
from jax.experimental import pallas as pl
from jax.experimental.pallas import tpu as pltpu
from jax.sharding import PartitionSpec as P

VMEM_BYTES = 14 * 1024 * 1024
CORES = 2
HALVES = 2
TILE = 256
LANES = 128

SMEM_SPEC = pl.BlockSpec(memory_space=pltpu.SMEM)
VMEM_SPEC = pl.BlockSpec(memory_space=pltpu.VMEM)
ANY_SPEC = pl.BlockSpec(memory_space=pl.ANY)
PARAMS = pltpu.CompilerParams(vmem_limit_bytes=VMEM_BYTES)


def bf16(*shape):
    return jax.ShapeDtypeStruct(shape, jnp.bfloat16)


def cost(flops, elements):
    return pl.CostEstimate(flops=flops, bytes_accessed=2 * elements, transcendentals=0)


def rows_of(block, rows):
    return pl.ds(pl.multiple_of(block * rows, rows), rows)


def cut_kernel(depth, place_ref, tokens_ref, *refs):
    outs, held = refs[:-1], refs[-1]
    levels, _, wide = held.shape
    core, level = place_ref[1], place_ref[2]
    tokens = tokens_ref[...]
    for other in range(levels):
        sides = []
        for side in range(CORES):
            blocks = range(side, wide // depth, CORES)
            starts = [(block * levels + other) * depth for block in blocks]
            sides.append(jnp.concatenate([tokens[:, s : s + depth] for s in starts], axis=1))
        swapped = jnp.concatenate(sides[::-1], axis=1)
        piece = jnp.where(core == 0, jnp.concatenate(sides, axis=1), swapped)
        held[jnp.bitwise_xor(level, other)] = piece
    for step, out_ref in enumerate(outs):
        out_ref[...] = held[step]


def cut_tokens(place, tokens, levels, depth):
    rows, model = tokens.shape
    shape = (rows, model // levels)
    return pl.pallas_call(
        functools.partial(cut_kernel, depth),
        in_specs=[SMEM_SPEC, VMEM_SPEC],
        out_specs=[VMEM_SPEC] * levels,
        out_shape=[bf16(*shape)] * levels,
        scratch_shapes=[pltpu.VMEM((levels,) + shape, jnp.bfloat16)],
        compiler_params=PARAMS,
    )(place, tokens)


def group_kernel(levels, place_ref, routing_ref, *refs):
    pieces, outs = refs[:levels], refs[levels:]
    wide = pieces[0].shape[1]
    rows = pieces[0].shape[0] // HALVES
    for step, piece in enumerate(pieces):
        target = rows_of(jnp.bitwise_xor(place_ref[2], step), rows)
        for half, out_ref in enumerate(outs):
            out_ref[target, :wide] = piece[half * rows : (half + 1) * rows, :]
    for level in range(levels):
        for half, out_ref in enumerate(outs):
            first = (level * HALVES + half) * rows
            out_ref[level * rows : (level + 1) * rows, wide:] = routing_ref[first : first + rows, :]


def group_tokens(place, routing, pieces):
    rows, wide = pieces[0].shape
    levels = len(pieces)
    return pl.pallas_call(
        functools.partial(group_kernel, levels),
        in_specs=[SMEM_SPEC, VMEM_SPEC] + [VMEM_SPEC] * levels,
        out_specs=[VMEM_SPEC] * HALVES,
        out_shape=[bf16(levels * rows // HALVES, wide + LANES)] * HALVES,
        compiler_params=PARAMS,
    )(place, routing, *pieces)


def finish_kernel(depth, levels, place_ref, *refs):
    pieces, (out_ref, held) = refs[:-2], refs[-2:]
    rows, wide = pieces[0].shape
    for index, piece in enumerate(pieces):
        half, step = index // levels, index % levels
        other = jnp.bitwise_xor(place_ref[2], step)
        held[other, half * rows : (half + 1) * rows, :] = piece[...]
    chips = wide // depth // CORES
    first, second = [], []
    for chip in range(chips):
        for side in range(CORES):
            for other in range(levels):
                for parts, place in ((first, side), (second, 1 - side)):
                    start = (place * chips + chip) * depth
                    parts.append(held[other, :, start : start + depth])
    first, second = jnp.concatenate(first, axis=1), jnp.concatenate(second, axis=1)
    out_ref[...] = jnp.where(place_ref[1] == 0, first, second)


def finish(place, pieces, levels, depth):
    rows, wide = pieces[0].shape
    rows = rows * HALVES
    return pl.pallas_call(
        functools.partial(finish_kernel, depth, levels),
        in_specs=[SMEM_SPEC] + [VMEM_SPEC] * len(pieces),
        out_specs=VMEM_SPEC,
        out_shape=bf16(rows, wide * levels),
        scratch_shapes=[pltpu.VMEM((levels, rows, wide), jnp.bfloat16)],
        compiler_params=PARAMS,
    )(place, *pieces)


def join_kernel(chips, place_ref, own_ref, *refs):
    pieces, (out_ref, sems) = refs[: chips - 1], refs[chips - 1 :]
    width = out_ref.shape[3]
    chip = place_ref[0]
    columns = pl.ds(pl.multiple_of(chip * width, width), width)
    sources = [own_ref.at[:, :, columns]] + list(pieces)
    copies = [
        pltpu.make_async_copy(source, out_ref.at[:, jnp.bitwise_xor(chip, step)], sems.at[step])
        for step, source in enumerate(sources)
    ]
    for copy in copies:
        copy.start()
    for copy in copies:
        copy.wait()


def join_blocks(place, own, pieces):
    experts, depth, units = own.shape
    chips = len(pieces) + 1
    shape = (experts, chips, depth, units // chips)
    return pl.pallas_call(
        functools.partial(join_kernel, chips),
        in_specs=[SMEM_SPEC] + [ANY_SPEC] * chips,
        out_specs=VMEM_SPEC,
        out_shape=bf16(*shape),
        scratch_shapes=[pltpu.SemaphoreType.DMA((chips,))],
        cost_estimate=cost(0, 2 * own.size),
        compiler_params=PARAMS,
    )(place, own, *pieces)


def pick_kernel(chips, place_ref, *refs):
    toks, refs = refs[:chips], refs[chips:]
    weights, (keep_ref, send_ref, routing_ref, left) = refs[:CORES], refs[CORES:]
    experts, depth, width = weights[0].shape
    rows = toks[0].shape[0]
    for step, tok in enumerate(toks):
        block = jnp.bitwise_xor(step, place_ref[2])
        left[rows_of(block, rows), :] = tok[:, : CORES * depth]
        routing_ref[block] = tok[:, CORES * depth :]
    slots = keep_ref.shape[2] // width
    tile = min(TILE, width)
    for start in range(0, width, tile):
        sums = []
        for which in range(experts):
            total = None
            for side, weight in enumerate(weights):
                term = jnp.dot(
                    left[:, side * depth : (side + 1) * depth],
                    weight[which, :, start : start + tile],
                    preferred_element_type=jnp.float32,
                )
                total = term if total is None else total + term
            sums.append(total)
        for step in range(chips):
            out_ref = (keep_ref, send_ref)[step % 2]
            ids = routing_ref[step].astype(jnp.float32)
            for slot in range(slots):
                chosen = ids[:, slot : slot + 1]
                picked = sums[0][step * rows : (step + 1) * rows]
                for which in range(1, experts):
                    other = sums[which][step * rows : (step + 1) * rows]
                    picked = jnp.where(chosen == which, other, picked)
                first = slot * width + start
                out_ref[step // 2, :, first : first + tile] = picked.astype(out_ref.dtype)


def picked_sums(place, toks, weights, slots):
    chips, rows = len(toks), toks[0].shape[0]
    experts, depth, width = weights[0].shape
    wide = CORES * depth
    count = chips * rows
    return pl.pallas_call(
        functools.partial(pick_kernel, chips),
        in_specs=[SMEM_SPEC] + [VMEM_SPEC] * (chips + CORES),
        out_specs=[VMEM_SPEC] * 3,
        out_shape=[bf16(chips // 2, rows, slots * width)] * 2 + [bf16(chips, rows, LANES)],
        scratch_shapes=[pltpu.VMEM((count, wide), jnp.bfloat16)],
        cost_estimate=cost(
            2 * count * wide * width * experts,
            count * wide + experts * wide * width + count * slots * width,
        ),
        compiler_params=PARAMS,
    )(place, *toks, *weights)


def hidden_kernel(terms, slots, routing_ref, *refs):
    gates, ups, out_ref = refs[:terms], refs[terms : 2 * terms], refs[2 * terms]
    scores = routing_ref[0].astype(jnp.float32)[:, slots : 2 * slots]
    combine = scores / jnp.sum(scores, axis=1, keepdims=True)
    width = out_ref.shape[1] // slots
    for slot in range(slots):
        columns = slice(slot * width, (slot + 1) * width)
        gate_sum = sum(ref[0, :, columns].astype(jnp.float32) for ref in gates)
        up_sum = sum(ref[0, :, columns].astype(jnp.float32) for ref in ups)
        value = gate_sum / (1.0 + jnp.exp(-gate_sum)) * up_sum * combine[:, slot : slot + 1]
        out_ref[:, columns] = value.astype(out_ref.dtype)


def hidden_rows(routing, gates, ups, slots):
    return pl.pallas_call(
        functools.partial(hidden_kernel, len(gates), slots),
        in_specs=[VMEM_SPEC] * (1 + 2 * len(gates)),
        out_specs=VMEM_SPEC,
        out_shape=bf16(*gates[0].shape[1:]),
        compiler_params=PARAMS,
    )(routing, *gates, *ups)


def down_kernel(slots, levels, place_ref, routing_ref, *refs):
    hids, refs = refs[:levels], refs[levels:]
    weights, (*outs, left) = refs[:CORES], refs[CORES:]
    experts, depth, width = weights[0].shape
    rows = hids[0].shape[0]
    for step, hid_ref in enumerate(hids):
        block = jnp.bitwise_xor(place_ref[2], step)
        ids = routing_ref[step].astype(jnp.float32)
        values = hid_ref[...].astype(jnp.float32)
        values = [values[:, slot * width : (slot + 1) * width] for slot in range(slots)]
        for which in range(experts):
            mine = jnp.zeros((rows, width), jnp.float32)
            for slot in range(slots):
                mine = jnp.where(ids[:, slot : slot + 1] == which, values[slot], mine)
            left[rows_of(block, rows), which * width : (which + 1) * width] = mine.astype(
                left.dtype
            )
    for side, weight in enumerate(weights):
        joined = jnp.concatenate([weight[which] for which in range(experts)], axis=1)
        total = lax.dot_general(
            left[...], joined, (((1,), (1,)), ((), ())), preferred_element_type=jnp.float32
        )
        for step, out_ref in enumerate(outs):
            part = total[step * rows : (step + 1) * rows]
            out_ref[:, side * depth : (side + 1) * depth] = part.astype(out_ref.dtype)


def down_sums(place, routing, hids, weights, slots):
    rows, levels = hids[0].shape[0], len(hids)
    experts, depth, width = weights[0].shape
    wide, count = CORES * depth, levels * rows
    return pl.pallas_call(
        functools.partial(down_kernel, slots, levels),
        in_specs=[SMEM_SPEC] + [VMEM_SPEC] * (1 + levels + CORES),
        out_specs=[VMEM_SPEC] * levels,
        out_shape=[bf16(rows, wide)] * levels,
        scratch_shapes=[pltpu.VMEM((count, experts * width), jnp.bfloat16)],
        cost_estimate=cost(
            2 * count * wide * width * experts,
            count * slots * width + experts * wide * width + count * wide,
        ),
        compiler_params=PARAMS,
    )(place, routing, *hids, *weights)


def after(values, others):
    return lax.optimization_barrier((values, others))[0]


def local(tokens, expert_ids, gate_scores, gate_weight, up_weight, down_weight):
    n_expert, n_tensor = lax.axis_size("expert"), lax.axis_size("tensor")
    chips = n_expert // CORES
    rows = tokens.shape[0]
    depth, units = gate_weight.shape[1:]
    slots = expert_ids.shape[1]
    width = units // chips
    spot, level = lax.axis_index("expert"), lax.axis_index("tensor")
    q, c = spot // CORES, spot % CORES
    place = jnp.stack([q, c, level])

    def to_chip(value, step):
        pairs = [(s, s ^ (step * CORES)) for s in range(n_expert)]
        return lax.ppermute(value, "expert", pairs)

    def to_core(value):
        return lax.ppermute(value, "expert", [(s, s ^ 1) for s in range(n_expert)])

    def to_level(value, step):
        return lax.ppermute(value, "tensor", [(s, s ^ step) for s in range(n_tensor)])

    def copies(held, send, bits):
        held = dict(held)
        for bit in bits:
            for step in sorted(held):
                held[step + bit] = send(held[step], bit)
        return [held[step] for step in range(len(held))]

    def level_sums(keep, send, behind, pieces=1):
        terms, marks, bit = [keep], [], 1
        send = after(send, behind[:1])
        while True:
            if 2 * bit == n_tensor:
                got = [to_level(part, bit) for part in jnp.split(send, pieces, axis=1)]
                terms.append(jnp.concatenate(got, axis=1) if pieces > 1 else got[0])
                return terms, marks + [got]
            terms.append(to_level(send, bit))
            bit *= 2
            send = sum(term[1::2].astype(jnp.float32) for term in terms).astype(jnp.bfloat16)
            terms = [term[::2] for term in terms]
            send = after(send, behind[len(marks) + 1 : len(marks) + 2])
            marks.append(send)

    def blocks_of(weight):
        return [
            lax.dynamic_slice_in_dim(weight, (q ^ step) * width, width, 2)
            for step in range(1, chips)
        ]

    def chip_exchange(blocks):
        return [to_chip(block, step) for step, block in enumerate(blocks, 1)]

    def core_exchange(joined):
        pair = [joined, to_core(joined)]
        return [side.reshape(side.shape[0], chips * depth, width) for side in pair]

    routing = jnp.concatenate([expert_ids, gate_scores], axis=1).astype(jnp.bfloat16)
    routing = jnp.pad(routing, ((0, 0), (0, LANES - 2 * slots)))
    gate_same = chip_exchange(blocks_of(gate_weight))
    cut = cut_tokens(place, tokens, n_tensor, depth)
    cut = [cut[0]] + [to_level(cut[step], step) for step in range(1, n_tensor)]
    groups = group_tokens(place, routing, cut)

    bits = [1 << bit for bit in range(chips.bit_length() - 1)]
    toks = []
    for half in range(HALVES):
        turn = (half + 1) % len(bits)
        toks.append(copies({0: groups[half]}, to_chip, bits[turn:] + bits[:turn]))
    near = [tok[bit] for tok in toks for bit in bits]
    gate_joined = join_blocks(place, gate_weight, after(gate_same, near))
    gate_pair = core_exchange(gate_joined)
    up_blocks = blocks_of(up_weight)
    toks = after(toks, up_blocks)
    up_same = chip_exchange(after(up_blocks, toks))

    def products(weights, chained, late):
        sums, routings, parts, behind = [], [], [], []
        for half in range(HALVES):
            left = after(toks[half], parts or late)
            *parts, routing = picked_sums(place, left, weights, slots)
            terms, marks = level_sums(*parts, behind, 1 if chained or not half else 2)
            behind = marks if chained else [(), *marks[1:]]
            sums.append((terms, marks))
            routings.append(routing)
        return sums, routings

    gate_sums, routings = products(gate_pair, False, [])
    ready = [gate_sums[0][1], gate_sums[-1][1][0], gate_sums[-1][1][-1][0]]
    up_joined = join_blocks(place, up_weight, after(up_same, ready))
    up_pair = core_exchange(up_joined)
    down_same = chip_exchange(after(blocks_of(down_weight), up_joined))
    up_sums, _ = products(up_pair, True, gate_sums[-1][1])

    held, first = [], [up_sums[-1][1][0]]
    bits = [n_tensor >> bit for bit in range(1, n_tensor.bit_length())]
    for half in range(HALVES):
        up_terms = after(up_sums[half][0], first)
        hidden = hidden_rows(routings[half], gate_sums[half][0], up_terms, slots)
        held.append({0: hidden, bits[0]: to_level(after(hidden, first[1:]), bits[0])})
        if half == 0:
            blocks = copies(held[0], to_level, bits[1:])
            first = [first[0], blocks[1]]
    down_joined = join_blocks(place, down_weight, after(down_same, [hidden, blocks[bits[0]]]))
    down_pair = core_exchange(down_joined)
    backs, got = [], []
    for half in range(HALVES):
        if half:
            blocks = copies(after(held[half], parts), to_level, bits[1:])
        parts = down_sums(place, routings[half], blocks, down_pair, slots)
        got = [to_chip(part, step) for step, part in enumerate(after(parts, got)) if step]
        total = sum(part.astype(jnp.float32) for part in [parts[0], *got])
        total = total.astype(jnp.bfloat16).reshape(n_tensor, rows // HALVES, -1)
        for other in range(n_tensor):
            piece = lax.dynamic_index_in_dim(total, level ^ other, 0, keepdims=False)
            backs.append(to_level(piece, other) if other else piece)
    return finish(place, backs, n_tensor, depth)


def solution(mesh):
    return jax.shard_map(
        local,
        mesh=mesh,
        in_specs=(
            P(("expert", "tensor"), None),
            P("expert", None),
            P("expert", None),
            P(None, ("expert", "tensor"), None),
            P(None, ("expert", "tensor"), None),
            P(None, ("expert", "tensor"), None),
        ),
        out_specs=P(("expert", "tensor"), None),
        check_vma=False,
    )
```
